32 devices in a mesh: ens: 2 (over x), cell: 16 (over z, y, core).
Axes of the slice: x: 2, y: 2, z: 4, core: 2. Of those that a mesh axis runs over, the one named last changes fastest.
Arguments:
- prior_members: float32 [8, 128, 4096], P(None, 'ens', 'cell'), parts along dimension 1, may hold values from -4 to 4
- blocks: bfloat16 [1024, 128, 128], P('cell'), may hold values from -0.3125 to 0.3125
- block_ray: int32 [1024], P('cell'), may hold values from 0 to 15
- block_cell: int32 [1024], P('cell'), may hold values from 0 to 1
- block_count: int32 [16], P('cell'), may hold values from 8 to 64, as said below
- ray_survey: int32 [16], replicated, may hold values from 0 to 7
- observed: float32 [16, 128, 128], P('cell', 'ens'), parts along dimension 1, may hold values from -6 to 6
- noise_scale: float32 [16, 128], P('cell'), may hold values from 0.8 to 1.6
Outputs:
- updated_members: float32 [8, 128, 4096], P(None, 'ens', 'cell'), parts along dimension 1
- last_gradient: bfloat16 [8, 128, 4096], P(None, 'ens', 'cell'), parts along dimension 1
The draws below stay inside these ranges and needn't reach their ends.
There are 2 independent parts, one for each index of `ens`. The reference program is written for one: setup_inputs(seed, part) draws one part's arguments, and reference() takes and returns one part's arrays. A program takes and returns all parts, laid end to end along the dimension named above; an argument that names none is the same for every part. Nothing has to cross between parts.
Inputs may be any that keep to these rules, and one draw needn't show every extreme that they name: `block_count`: slots a slab uses; slots from this count on hold blocks that are not part of the operator. Some slab uses all 64 slots in every draw.
All inputs are finite; a program needn't handle non-finite values.
Results may differ from the reference program's by a relative error of at most 0.0073.
Values may be sent and summed in bfloat16 or wider, within the bound.
No kernel may reach another device: no remote copies, remote signals or barrier semaphores. Data moves between devices by JAX's collectives and lax.ppermute only.
A program may use at most 64 MiB of HBM per device.

```python
import math
import jax
import jax.numpy as jnp
from jax import lax

S = 8
E = 64
RB = 128
CB = 128
PLANE = 256
ITERS = 3
CBD = 2
CAP = 64
NRB = 16
CELLS = 4096
N_CELL = 16


def draw_block_count(key, part):
    key = jax.random.fold_in(key, 11)
    first_key, second_key = jax.random.split(key)
    levels = jax.random.randint(first_key, (N_CELL,), 0, 65)
    floor_count = CAP // 8
    counts = floor_count + (CAP - floor_count) * levels * levels // 4096
    busiest = jax.random.randint(second_key, (), 0, N_CELL)
    return jnp.where(jnp.arange(N_CELL) == busiest, CAP, counts).astype(jnp.int32)


def with_ends(result, own_key, smallest, high):
    longest = result.shape.index(max(result.shape))
    spots = []
    for shift in (0, 1):
        where = [jax.random.randint(jax.random.fold_in(own_key, axis), (), 0, length) for axis, length in enumerate(result.shape)]
        where[longest] = (where[longest] + shift) % result.shape[longest]
        spots.append(tuple(where))
    return result.at[spots[0]].set(smallest).at[spots[1]].set(high)


def steps_of(key, shape, cuts, low, top_value):
    gain = 1.0
    for position, shards_of in cuts:
        steps = jax.random.uniform(jax.random.fold_in(jax.random.fold_in(key, 6), position), (shards_of,), jnp.float32, low / len(cuts), top_value / len(cuts))
        gain = gain * jnp.repeat(jnp.exp(steps), shape[position] // shards_of).reshape((-1,) + (1,) * (len(shape) - 1 - position))
    return gain


def scatter_about(rng, dims, width, most, cuts=(), kind=jnp.bfloat16):
    array = jax.random.normal(rng, dims, jnp.float32) * width
    if len(cuts) > 0:
        array = steps_of(rng, dims, cuts, -0.22, 0.18) * array
    return jnp.clip(array, min=-most, max=most).astype(kind)


def setup_inputs(seed: int = 0, part: int = 0) -> dict:
    streams_of = jax.random.split(jax.random.key(seed), 9)
    part_keys = jax.random.split(jax.random.fold_in(streams_of[8], part), 9)
    prior_members = scatter_about(part_keys[0], (S, E, CELLS), 0.3, 4.0, ((2, 16),), jnp.float32)
    blocks = scatter_about(streams_of[1], (N_CELL * CAP, RB, CB), (CAP * CB // 24) ** -0.5, 0.3125, ((0, 16),))
    block_ray = with_ends(jax.random.randint(streams_of[2], (N_CELL * CAP,), 0, NRB), jax.random.fold_in(streams_of[2], 1), 0, NRB - 1).astype(jnp.int32)
    block_cell = with_ends(jax.random.randint(streams_of[3], (N_CELL * CAP,), 0, CBD), jax.random.fold_in(streams_of[3], 1), 0, CBD - 1).astype(jnp.int32)
    block_count = draw_block_count(jax.random.fold_in(streams_of[8], 71), part)
    ray_survey = with_ends(jax.random.randint(streams_of[5], (NRB,), 0, S), jax.random.fold_in(streams_of[5], 1), 0, S - 1).astype(jnp.int32)
    observed = scatter_about(part_keys[6], (NRB, E, RB), 0.5, 6.0, ((0, 16),), jnp.float32)
    noise_scale = jnp.clip(jnp.exp(math.log(1.6) - 0.6931472 * jax.random.uniform(streams_of[7], (NRB, RB), jnp.float32) ** steps_of(streams_of[7], (NRB, RB), ((0, 16),), -0.2, 0.2)), 0.8, 1.6)
    return dict(prior_members=prior_members, blocks=blocks, block_ray=block_ray, block_cell=block_cell, block_count=block_count, ray_survey=ray_survey, observed=observed, noise_scale=noise_scale)


ALPHA_PRIOR = 0.5
BETA_TIME = 0.25
GAMMA_DEPTH = 0.25
STEP_SIZE = 0.05
DATA_GAIN = 1.0
HIGHEST = lax.Precision.HIGHEST


def temporal(members):
    before = jnp.concatenate([members[:1], members[:-1]], axis=0)
    following = jnp.concatenate([members[1:], members[-1:]], axis=0)
    return (members - before) + (members - following)


def reference(prior_members, blocks, block_ray, block_cell, block_count, ray_survey, observed, noise_scale):
    slot_blocks = blocks.reshape(N_CELL, CAP, RB, CB)
    slot_rays = block_ray.reshape(N_CELL, CAP)
    slot_cells = block_cell.reshape(N_CELL, CAP)
    slab_index = jnp.arange(N_CELL, dtype=jnp.int32)
    slot_index = jnp.arange(CAP, dtype=jnp.int32)
    spread = noise_scale[:, None, :]
    members = prior_members
    gradient = jnp.zeros_like(prior_members)
    for iteration in range(ITERS):
        member_grid = members.astype(jnp.bfloat16).reshape(S, E, N_CELL * CBD, CB)

        def forward(travel, slab):
            these_blocks, these_rays, these_cells, slab_count, slab_id = slab
            model_tiles = member_grid[ray_survey[these_rays], :, slab_id * CBD + these_cells, :].astype(jnp.float32)
            in_use = (slot_index < slab_count).astype(jnp.float32)
            slab_travel = jnp.einsum("kec,krc->ker", model_tiles, these_blocks.astype(jnp.float32), precision=HIGHEST)
            return travel.at[these_rays].add(slab_travel * in_use[:, None, None]), None

        travel, _ = lax.scan(forward, jnp.zeros((NRB, E, RB), jnp.float32),
                             (slot_blocks, slot_rays, slot_cells, block_count, slab_index))
        scaled = (travel - observed) / spread
        residual = (DATA_GAIN * scaled / (spread * (1.0 + scaled * scaled))).astype(jnp.bfloat16)

        def backward(carry, slab):
            these_blocks, these_rays, these_cells, slab_count = slab
            ray_rows = residual[these_rays].astype(jnp.float32)
            in_use = (slot_index < slab_count).astype(jnp.float32)
            slab_grad = jnp.einsum("ker,krc->kec", ray_rows, these_blocks.astype(jnp.float32), precision=HIGHEST)
            targets = ray_survey[these_rays] * CBD + these_cells
            summed = jnp.zeros((S * CBD, E, CB), jnp.float32).at[targets].add(slab_grad * in_use[:, None, None])
            return carry, summed

        _, pieces = lax.scan(backward, jnp.zeros((), jnp.float32),
                             (slot_blocks, slot_rays, slot_cells, block_count))
        data_grad = pieces.reshape(N_CELL, S, CBD, E, CB).transpose(1, 3, 0, 2, 4).reshape(S, E, CELLS)
        outside = jnp.zeros((S, E, PLANE), jnp.float32)
        padded = jnp.concatenate([outside, members, outside], axis=2)
        vertical = 2.0 * members - padded[:, :, :CELLS] - padded[:, :, 2 * PLANE:]
        gradient = data_grad + ALPHA_PRIOR * (members - prior_members) + BETA_TIME * temporal(members) + GAMMA_DEPTH * vertical
        members = members - STEP_SIZE * gradient
    return members, gradient.astype(jnp.bfloat16)
```

```python
import functools

import jax
import jax.numpy as jnp
from jax import lax
from jax.experimental import pallas as pl
from jax.experimental.pallas import tpu as pltpu
from jax.sharding import PartitionSpec as P

ITERS = 3

ALPHA_PRIOR = 0.5
BETA_TIME = 0.25
GAMMA_DEPTH = 0.25
STEP_SIZE = 0.05
DATA_GAIN = 1.0

CHUNK = 8
VMEM_BYTES = 48 * 1024 * 1024

SMEM = pl.BlockSpec(memory_space=pltpu.SMEM)
VMEM = pl.BlockSpec(memory_space=pltpu.VMEM)
ANY = pl.BlockSpec(memory_space=pl.ANY)


def forward(survey_ref, half_ref, dense_ref, travel_ref):
    for q in range(dense_ref.shape[0]):
        travel_ref[q] = lax.dot_general(
            half_ref[survey_ref[q]],
            dense_ref[q],
            (((1,), (1,)), ((), ())),
            preferred_element_type=jnp.float32,
        ).astype(travel_ref.dtype)


def setup_kernel(
    ray_ref, cell_ref, count_ref, survey_ref, members_ref, blocks_ref,
    dense_ref, half_ref, travel_ref,
    total, staged, sems,
):
    slots, rays, width = blocks_ref.shape
    count = count_ref[0]
    chunks = slots // CHUNK

    def chunk_copy(i):
        part = pl.ds(i * CHUNK, CHUNK)
        return pltpu.make_async_copy(blocks_ref.at[part], staged.at[part], sems.at[i])

    for i in range(chunks):
        chunk_copy(i).start()
    total[...] = jnp.zeros_like(total)
    half_ref[...] = members_ref[...].astype(half_ref.dtype)
    for i in range(chunks):
        chunk_copy(i).wait()

        def add(k, carry):
            b, q = cell_ref[k], ray_ref[k]
            total[b, q] = total[b, q] + staged[k].astype(jnp.float32)
            return carry

        lax.fori_loop(i * CHUNK, jnp.minimum((i + 1) * CHUNK, count), add, 0)
    for b in range(total.shape[0]):
        dense_ref[:, :, b * width : (b + 1) * width] = total[b].astype(dense_ref.dtype)
    forward(survey_ref, half_ref, dense_ref, travel_ref)


def misfit_kernel(parts_ref, observed_ref, noise_ref, out_ref):
    travel = jnp.sum(parts_ref[...].astype(jnp.float32), axis=0)
    spread = noise_ref[...][:, None, :]
    scaled = (travel - observed_ref[...]) / spread
    residual = DATA_GAIN * scaled / (spread * (1.0 + scaled * scaled))
    out_ref[...] = jnp.broadcast_to(residual.astype(out_ref.dtype)[None], out_ref.shape)


def gradient_sum(survey_ref, residual_ref, dense_ref, members_ref, prior_ref, above_ref, below_ref, grad):
    surveys = members_ref.shape[0]
    for s in range(surveys):
        m = members_ref[s]
        value = ALPHA_PRIOR * (m - prior_ref[s])
        if s > 0:
            value = value + BETA_TIME * (m - members_ref[s - 1])
        if s < surveys - 1:
            value = value + BETA_TIME * (m - members_ref[s + 1])
        vertical = 2.0 * m - above_ref[s].astype(jnp.float32) - below_ref[s].astype(jnp.float32)
        grad[s] = value + GAMMA_DEPTH * vertical
    for q in range(dense_ref.shape[0]):
        s = survey_ref[q]
        grad[s] = grad[s] + jnp.dot(residual_ref[q], dense_ref[q], preferred_element_type=jnp.float32)


def step_kernel(
    survey_ref, residual_ref, dense_ref, members_ref, prior_ref, above_ref, below_ref,
    out_ref, half_ref, travel_ref,
    grad,
):
    gradient_sum(survey_ref, residual_ref, dense_ref, members_ref, prior_ref, above_ref, below_ref, grad)
    updated = members_ref[...] - STEP_SIZE * grad[...]
    out_ref[...] = updated
    half_ref[...] = updated.astype(half_ref.dtype)
    forward(survey_ref, half_ref, dense_ref, travel_ref)


def last_kernel(
    survey_ref, residual_ref, dense_ref, members_ref, prior_ref, above_ref, below_ref,
    out_ref, gradient_ref,
    grad,
):
    gradient_sum(survey_ref, residual_ref, dense_ref, members_ref, prior_ref, above_ref, below_ref, grad)
    out_ref[...] = members_ref[...] - STEP_SIZE * grad[...]
    gradient_ref[...] = grad[...].astype(gradient_ref.dtype)


def shards(
    prior_members, blocks, block_ray, block_cell, block_count, ray_survey, observed, noise_scale
):
    surveys, ensemble, cells_dev = prior_members.shape
    slots, rays, width = blocks.shape
    ray_blocks = ray_survey.shape[0]
    count = lax.axis_size("cell")
    owned = ray_blocks // count
    params = pltpu.CompilerParams(vmem_limit_bytes=VMEM_BYTES)

    members_f32 = jax.ShapeDtypeStruct(prior_members.shape, jnp.float32)
    members_bf16 = jax.ShapeDtypeStruct(prior_members.shape, jnp.bfloat16)
    travel_bf16 = jax.ShapeDtypeStruct((ray_blocks, ensemble, rays), jnp.bfloat16)
    grad_scratch = [pltpu.VMEM(prior_members.shape, jnp.float32)]

    dense, half, travel = pl.pallas_call(
        setup_kernel,
        out_shape=(
            jax.ShapeDtypeStruct((ray_blocks, rays, cells_dev), jnp.bfloat16),
            members_bf16,
            travel_bf16,
        ),
        in_specs=[SMEM] * 4 + [VMEM, ANY],
        out_specs=(VMEM, VMEM, VMEM),
        scratch_shapes=[
            pltpu.VMEM((cells_dev // width, ray_blocks, rays, width), jnp.float32),
            pltpu.VMEM(blocks.shape, blocks.dtype),
            pltpu.SemaphoreType.DMA((slots // CHUNK,)),
        ],
        compiler_params=params,
    )(block_ray, block_cell, block_count, ray_survey, prior_members, blocks)

    up = [(i, i + 1) for i in range(count - 1)]
    down = [(i + 1, i) for i in range(count - 1)]
    members = prior_members
    for iteration in range(ITERS):
        above = lax.ppermute(half, "cell", up)
        below = lax.ppermute(half, "cell", down)
        parts = lax.all_to_all(travel, "cell", split_axis=0, concat_axis=0, tiled=True)
        spread = pl.pallas_call(
            misfit_kernel,
            out_shape=jax.ShapeDtypeStruct((count, owned, ensemble, rays), jnp.bfloat16),
            in_specs=[VMEM] * 3,
            out_specs=VMEM,
            compiler_params=params,
        )(parts.reshape(count, owned, ensemble, rays), observed, noise_scale)
        residual = lax.all_to_all(
            spread.reshape(travel.shape), "cell", split_axis=0, concat_axis=0, tiled=True
        )
        operands = (ray_survey, residual, dense, members, prior_members, above, below)
        last = iteration == ITERS - 1
        results = pl.pallas_call(
            last_kernel if last else step_kernel,
            out_shape=(members_f32, members_bf16) + (() if last else (travel_bf16,)),
            in_specs=[SMEM] + [VMEM] * 6,
            out_specs=(VMEM, VMEM) + (() if last else (VMEM,)),
            scratch_shapes=grad_scratch,
            compiler_params=params,
        )(*operands)
        if last:
            return results
        members, half, travel = results


def solution(mesh):
    placed = (
        P(None, "ens", "cell"),
        P("cell", None, None),
        P("cell"),
        P("cell"),
        P("cell"),
        P(),
        P("cell", "ens", None),
        P("cell", None),
    )
    return jax.shard_map(
        shards,
        mesh=mesh,
        in_specs=placed,
        out_specs=(P(None, "ens", "cell"), P(None, "ens", "cell")),
        check_vma=False,
    )
```

```python
import functools

import jax
import jax.numpy as jnp
from jax import lax
from jax.experimental import pallas as pl
from jax.experimental.pallas import tpu as pltpu
from jax.sharding import PartitionSpec as P

ITERS = 3

ALPHA_PRIOR = 0.5
BETA_TIME = 0.25
GAMMA_DEPTH = 0.25
STEP_SIZE = 0.05
DATA_GAIN = 1.0

CHUNK = 8
VMEM_BYTES = 24 * 1024 * 1024
SETUP_VMEM_BYTES = 60 * 1024 * 1024

SMEM = pl.BlockSpec(memory_space=pltpu.SMEM)
VMEM = pl.BlockSpec(memory_space=pltpu.VMEM)
ANY = pl.BlockSpec(memory_space=pl.ANY)
HBM = pl.BlockSpec(memory_space=pltpu.HBM)


def forward(survey_ref, half_ref, dense_ref, own_ref, away_ref):
    half = own_ref.shape[0]
    for i in range(2 * half):
        travel = lax.dot_general(
            half_ref[survey_ref[i]],
            dense_ref[i],
            (((1,), (1,)), ((), ())),
            preferred_element_type=jnp.float32,
        )
        if i < half:
            own_ref[i] = travel
        else:
            away_ref[i - half] = travel.astype(away_ref.dtype)


def store_half(half, half_ref, first_ref, second_ref):
    split = first_ref.shape[0]
    half_ref[...] = half
    first_ref[...] = half[:split]
    second_ref[...] = half[split:]


def setup_kernel(
    owned, ray_hbm, cell_hbm, count_hbm, survey_hbm, members_hbm, blocks_hbm,
    dense_ref, order_ref, half_ref, first_ref, second_ref, own_ref, away_ref,
    ray_ref, cell_ref, count_ref, survey_ref, members_ref, staged, total, small_sems, sems,
):
    slots, rays, width = blocks_hbm.shape
    ray_blocks = dense_ref.shape[0]
    half = ray_blocks // 2
    chunks = slots // CHUNK
    parity = lax.rem(lax.axis_index("cell"), 2)
    small = [
        pltpu.make_async_copy(source, target, small_sems.at[i])
        for i, (source, target) in enumerate(
            (
                (ray_hbm, ray_ref),
                (cell_hbm, cell_ref),
                (count_hbm, count_ref),
                (survey_hbm, survey_ref),
                (members_hbm, members_ref),
            )
        )
    ]
    large = []
    for i in range(chunks):
        part = pl.ds(i * CHUNK, CHUNK)
        large.append(pltpu.make_async_copy(blocks_hbm.at[part], staged.at[part], sems.at[i]))
    for copy in small + large:
        copy.start()
    total[...] = jnp.zeros_like(total)
    for copy in small:
        copy.wait()
    store_half(members_ref[...].astype(half_ref.dtype), half_ref, first_ref, second_ref)
    for i in range(ray_blocks):
        side, rest = divmod(i, half)
        pair, offset = divmod(rest, owned)
        owner = 2 * pair + (parity if side == 0 else 1 - parity)
        order_ref[i] = survey_ref[owner * owned + offset]
    count = count_ref[0]
    for i in range(chunks):
        large[i].wait()

        def add(k, carry):
            b, q = cell_ref[k], ray_ref[k]
            owner = lax.div(q, owned)
            side = lax.rem(owner + parity, 2)
            place = side * half + lax.div(owner, 2) * owned + lax.rem(q, owned)
            total[b, place] = total[b, place] + staged[k].astype(jnp.float32)
            return carry

        lax.fori_loop(i * CHUNK, jnp.minimum((i + 1) * CHUNK, count), add, 0)
    for b in range(total.shape[0]):
        dense_ref[:, :, b * width : (b + 1) * width] = total[b].astype(dense_ref.dtype)
    forward(order_ref, half_ref, dense_ref, own_ref, away_ref)


def add_kernel(own_ref, received_ref, out_ref):
    out_ref[...] = (own_ref[...] + received_ref[...].astype(jnp.float32)).astype(out_ref.dtype)


def misfit_kernel(parts_ref, observed_ref, noise_ref, halo_ref, out_ref):
    del halo_ref
    travel = jnp.sum(parts_ref[...].astype(jnp.float32), axis=0)
    spread = noise_ref[...][:, None, :]
    scaled = (travel - observed_ref[...]) / spread
    residual = DATA_GAIN * scaled / (spread * (1.0 + scaled * scaled))
    out_ref[...] = jnp.broadcast_to(residual.astype(out_ref.dtype)[None], out_ref.shape)


def gradient_kernel(order_ref, residual_ref, dense_ref, members_ref, prior_ref, grad_ref):
    surveys = members_ref.shape[0]
    for s in range(surveys):
        m = members_ref[s]
        value = ALPHA_PRIOR * (m - prior_ref[s])
        if s > 0:
            value = value + BETA_TIME * (m - members_ref[s - 1])
        if s < surveys - 1:
            value = value + BETA_TIME * (m - members_ref[s + 1])
        grad_ref[s] = value
    for i in range(residual_ref.shape[0]):
        s = order_ref[i]
        grad_ref[s] = grad_ref[s] + jnp.dot(
            residual_ref[i], dense_ref[i], preferred_element_type=jnp.float32
        )


def finish_gradient(
    order_ref, residual_ref, dense_ref, partial_ref, members_ref, chip_ref, first_halo_ref, second_halo_ref, grad
):
    surveys = members_ref.shape[0]
    split = first_halo_ref.shape[0]
    half = residual_ref.shape[0]
    for s in range(surveys):
        link = first_halo_ref[s] if s < split else second_halo_ref[s - split]
        vertical = 2.0 * members_ref[s] - chip_ref[s].astype(jnp.float32) - link.astype(jnp.float32)
        grad[s] = partial_ref[s] + GAMMA_DEPTH * vertical
    for i in range(half):
        s = order_ref[half + i]
        grad[s] = grad[s] + jnp.dot(
            residual_ref[i], dense_ref[half + i], preferred_element_type=jnp.float32
        )


def step_kernel(
    order_ref, residual_ref, dense_ref, partial_ref, members_ref, chip_ref, first_halo_ref, second_halo_ref,
    out_ref, half_ref, first_ref, second_ref, own_ref, away_ref,
    grad,
):
    finish_gradient(
        order_ref, residual_ref, dense_ref, partial_ref, members_ref, chip_ref, first_halo_ref, second_halo_ref, grad
    )
    updated = members_ref[...] - STEP_SIZE * grad[...]
    out_ref[...] = updated
    store_half(updated.astype(half_ref.dtype), half_ref, first_ref, second_ref)
    forward(order_ref, half_ref, dense_ref, own_ref, away_ref)


def last_kernel(
    order_ref, residual_ref, dense_ref, partial_ref, members_ref, chip_ref, first_halo_ref, second_halo_ref,
    out_ref, gradient_ref,
    grad,
):
    finish_gradient(
        order_ref, residual_ref, dense_ref, partial_ref, members_ref, chip_ref, first_halo_ref, second_halo_ref, grad
    )
    out_ref[...] = members_ref[...] - STEP_SIZE * grad[...]
    gradient_ref[...] = grad[...].astype(gradient_ref.dtype)


def shards(
    prior_members, blocks, block_ray, block_cell, block_count, ray_survey, observed, noise_scale
):
    surveys, ensemble, cells_dev = prior_members.shape
    slots, rays, width = blocks.shape
    ray_blocks = ray_survey.shape[0]
    count = lax.axis_size("cell")
    owned = ray_blocks // count
    chips = count // 2
    half_blocks = ray_blocks // 2
    split = surveys // 2
    params = pltpu.CompilerParams(vmem_limit_bytes=VMEM_BYTES)

    def bf16(*shape):
        return jax.ShapeDtypeStruct(shape, jnp.bfloat16)

    def f32(*shape):
        return jax.ShapeDtypeStruct(shape, jnp.float32)

    members_f32 = f32(surveys, ensemble, cells_dev)
    halves = (
        bf16(surveys, ensemble, cells_dev),
        bf16(split, ensemble, cells_dev),
        bf16(surveys - split, ensemble, cells_dev),
    )
    travels = (f32(half_blocks, ensemble, rays), bf16(half_blocks, ensemble, rays))

    dense, order, half, first, second, own, away = pl.pallas_call(
        functools.partial(setup_kernel, owned),
        out_shape=(
            bf16(ray_blocks, rays, cells_dev),
            jax.ShapeDtypeStruct((ray_blocks,), jnp.int32),
        )
        + halves
        + travels,
        in_specs=[HBM] * 6,
        out_specs=(VMEM, SMEM) + (VMEM,) * 5,
        scratch_shapes=[
            pltpu.SMEM(block_ray.shape, jnp.int32),
            pltpu.SMEM(block_cell.shape, jnp.int32),
            pltpu.SMEM(block_count.shape, jnp.int32),
            pltpu.SMEM(ray_survey.shape, jnp.int32),
            pltpu.VMEM(prior_members.shape, jnp.float32),
            pltpu.VMEM(blocks.shape, blocks.dtype),
            pltpu.VMEM((cells_dev // width, ray_blocks, rays, width), jnp.float32),
            pltpu.SemaphoreType.DMA((5,)),
            pltpu.SemaphoreType.DMA((slots // CHUNK,)),
        ],
        compiler_params=pltpu.CompilerParams(vmem_limit_bytes=SETUP_VMEM_BYTES),
    )(block_ray, block_cell, block_count, ray_survey, prior_members, blocks)

    chip_pairs = [(i, i ^ 1) for i in range(count)]
    link_pairs = [pair for i in range(1, count - 1, 2) for pair in ((i, i + 1), (i + 1, i))]
    same_core = [list(range(core, count, 2)) for core in range(2)]

    def exchange(array):
        return lax.all_to_all(
            array, "cell", split_axis=0, concat_axis=0, axis_index_groups=same_core, tiled=True
        )

    members = prior_members
    for iteration in range(ITERS):
        received = lax.ppermute(away, "cell", chip_pairs)
        chip_travel = pl.pallas_call(
            add_kernel,
            out_shape=bf16(half_blocks, ensemble, rays),
            in_specs=[VMEM] * 2,
            out_specs=VMEM,
            compiler_params=params,
        )(own, received)
        first_halo = lax.ppermute(first, "cell", link_pairs)
        second_halo = lax.ppermute(second, "cell", link_pairs)
        chip_halo = lax.ppermute(half, "cell", chip_pairs)
        parts = exchange(chip_travel)
        copies = pl.pallas_call(
            misfit_kernel,
            out_shape=bf16(chips, owned, ensemble, rays),
            in_specs=[VMEM] * 3 + [ANY],
            out_specs=VMEM,
            compiler_params=params,
        )(parts.reshape(chips, owned, ensemble, rays), observed, noise_scale, first_halo)
        residual = exchange(copies.reshape(half_blocks, ensemble, rays))
        other_residual = lax.ppermute(residual, "cell", chip_pairs)
        partial = pl.pallas_call(
            gradient_kernel,
            out_shape=members_f32,
            in_specs=[SMEM] + [VMEM] * 4,
            out_specs=VMEM,
            compiler_params=params,
        )(order, residual, dense, members, prior_members)
        last = iteration == ITERS - 1
        outputs = (members_f32, halves[0]) if last else (members_f32,) + halves + travels
        results = pl.pallas_call(
            last_kernel if last else step_kernel,
            out_shape=outputs,
            in_specs=[SMEM] + [VMEM] * 7,
            out_specs=(VMEM,) * len(outputs),
            scratch_shapes=[pltpu.VMEM(prior_members.shape, jnp.float32)],
            compiler_params=params,
        )(order, other_residual, dense, partial, members, chip_halo, first_halo, second_halo)
        if last:
            return results
        members, half, first, second, own, away = results


def solution(mesh):
    placed = (
        P(None, "ens", "cell"),
        P("cell", None, None),
        P("cell"),
        P("cell"),
        P("cell"),
        P(),
        P("cell", "ens", None),
        P("cell", None),
    )
    return jax.shard_map(
        shards,
        mesh=mesh,
        in_specs=placed,
        out_specs=(P(None, "ens", "cell"), P(None, "ens", "cell")),
        check_vma=False,
    )
```

```python
import functools

import jax
import jax.numpy as jnp
from jax import lax
from jax.experimental import pallas as pl
from jax.experimental.pallas import tpu as pltpu
from jax.sharding import PartitionSpec as P

ITERS = 3

ALPHA_PRIOR = 0.5
BETA_TIME = 0.25
GAMMA_DEPTH = 0.25
STEP_SIZE = 0.05
DATA_GAIN = 1.0

CHUNK = 8
VMEM_BYTES = 24 * 1024 * 1024
SETUP_VMEM_BYTES = 60 * 1024 * 1024

SMEM = pl.BlockSpec(memory_space=pltpu.SMEM)
VMEM = pl.BlockSpec(memory_space=pltpu.VMEM)
ANY = pl.BlockSpec(memory_space=pl.ANY)
HBM = pl.BlockSpec(memory_space=pltpu.HBM)


def survey_of(survey_ref, owned, i):
    half = survey_ref.shape[0] // 2
    parity = lax.rem(lax.axis_index("cell"), 2)
    side, rest = divmod(i, half)
    pair, offset = divmod(rest, owned)
    owner = 2 * pair + (parity if side == 0 else 1 - parity)
    return survey_ref[owner * owned + offset]


def forward(owned, survey_ref, half_ref, dense_ref, own_ref, away_ref):
    half = own_ref.shape[0]
    for i in range(2 * half):
        travel = lax.dot_general(
            half_ref[survey_of(survey_ref, owned, i)],
            dense_ref[i],
            (((1,), (1,)), ((), ())),
            preferred_element_type=jnp.float32,
        )
        if i < half:
            own_ref[i] = travel
        else:
            away_ref[i - half] = travel.astype(away_ref.dtype)


def store_half(half, half_ref, first_ref, second_ref):
    split = first_ref.shape[0]
    half_ref[...] = half
    first_ref[...] = half[:split]
    second_ref[...] = half[split:]


def setup_kernel(
    owned, count_ref, ray_hbm, cell_hbm, survey_hbm, members_hbm, blocks_hbm,
    dense_ref, half_ref, first_ref, second_ref, own_ref, away_ref,
    ray_ref, cell_ref, survey_ref, members_ref, staged, total, small_sems, sems,
):
    slots, rays, width = blocks_hbm.shape
    ray_blocks = dense_ref.shape[0]
    half = ray_blocks // 2
    chunks = slots // CHUNK
    parity = lax.rem(lax.axis_index("cell"), 2)
    small = [
        pltpu.make_async_copy(source, target, small_sems.at[i])
        for i, (source, target) in enumerate(
            (
                (ray_hbm, ray_ref),
                (cell_hbm, cell_ref),
                (survey_hbm, survey_ref),
                (members_hbm, members_ref),
            )
        )
    ]
    large = []
    for i in range(chunks):
        part = pl.ds(i * CHUNK, CHUNK)
        large.append(pltpu.make_async_copy(blocks_hbm.at[part], staged.at[part], sems.at[i]))
    for copy in small + large:
        copy.start()
    total[...] = jnp.zeros_like(total)
    for copy in small:
        copy.wait()
    store_half(members_ref[...].astype(half_ref.dtype), half_ref, first_ref, second_ref)
    count = count_ref[0]
    for i in range(chunks):
        large[i].wait()

        def add(k, carry):
            b, q = cell_ref[k], ray_ref[k]
            owner = lax.div(q, owned)
            side = lax.rem(owner + parity, 2)
            place = side * half + lax.div(owner, 2) * owned + lax.rem(q, owned)
            total[b, place] = total[b, place] + staged[k].astype(jnp.float32)
            return carry

        lax.fori_loop(i * CHUNK, jnp.minimum((i + 1) * CHUNK, count), add, 0)
    for b in range(total.shape[0]):
        dense_ref[:, :, b * width : (b + 1) * width] = total[b].astype(dense_ref.dtype)
    forward(owned, survey_ref, half_ref, dense_ref, own_ref, away_ref)


def add_kernel(own_ref, received_ref, out_ref):
    out_ref[...] = (own_ref[...] + received_ref[...].astype(jnp.float32)).astype(out_ref.dtype)


def misfit_kernel(parts_ref, observed_ref, noise_ref, out_ref):
    travel = jnp.sum(parts_ref[...].astype(jnp.float32), axis=0)
    spread = noise_ref[...][:, None, :]
    scaled = (travel - observed_ref[...]) / spread
    residual = DATA_GAIN * scaled / (spread * (1.0 + scaled * scaled))
    out_ref[...] = jnp.broadcast_to(residual.astype(out_ref.dtype)[None], out_ref.shape)


def gradient_kernel(owned, survey_ref, residual_ref, dense_ref, members_ref, prior_ref, grad_ref):
    surveys = members_ref.shape[0]
    for s in range(surveys):
        m = members_ref[s]
        value = ALPHA_PRIOR * (m - prior_ref[s])
        if s > 0:
            value = value + BETA_TIME * (m - members_ref[s - 1])
        if s < surveys - 1:
            value = value + BETA_TIME * (m - members_ref[s + 1])
        grad_ref[s] = value
    for i in range(residual_ref.shape[0]):
        s = survey_of(survey_ref, owned, i)
        grad_ref[s] = grad_ref[s] + jnp.dot(
            residual_ref[i], dense_ref[i], preferred_element_type=jnp.float32
        )


def finish_gradient(
    owned, survey_ref, residual_ref, dense_ref, partial_ref, members_ref, chip_ref, first_halo_ref, second_halo_ref, grad
):
    surveys = members_ref.shape[0]
    split = first_halo_ref.shape[0]
    half = residual_ref.shape[0]
    for s in range(surveys):
        link = first_halo_ref[s] if s < split else second_halo_ref[s - split]
        vertical = 2.0 * members_ref[s] - chip_ref[s].astype(jnp.float32) - link.astype(jnp.float32)
        grad[s] = partial_ref[s] + GAMMA_DEPTH * vertical
    for i in range(half):
        s = survey_of(survey_ref, owned, half + i)
        grad[s] = grad[s] + jnp.dot(
            residual_ref[i], dense_ref[half + i], preferred_element_type=jnp.float32
        )


def step_kernel(
    owned, survey_ref, residual_ref, dense_ref, partial_ref, members_ref, chip_ref, first_halo_ref, second_halo_ref,
    out_ref, half_ref, first_ref, second_ref, own_ref, away_ref,
    grad,
):
    finish_gradient(
        owned, survey_ref, residual_ref, dense_ref, partial_ref, members_ref, chip_ref, first_halo_ref, second_halo_ref, grad
    )
    updated = members_ref[...] - STEP_SIZE * grad[...]
    out_ref[...] = updated
    store_half(updated.astype(half_ref.dtype), half_ref, first_ref, second_ref)
    forward(owned, survey_ref, half_ref, dense_ref, own_ref, away_ref)


def last_kernel(
    owned, survey_ref, residual_ref, dense_ref, partial_ref, members_ref, chip_ref, first_halo_ref, second_halo_ref,
    out_ref, gradient_ref,
    grad,
):
    finish_gradient(
        owned, survey_ref, residual_ref, dense_ref, partial_ref, members_ref, chip_ref, first_halo_ref, second_halo_ref, grad
    )
    out_ref[...] = members_ref[...] - STEP_SIZE * grad[...]
    gradient_ref[...] = grad[...].astype(gradient_ref.dtype)


def shards(
    prior_members, blocks, block_ray, block_cell, block_count, ray_survey, observed, noise_scale
):
    surveys, ensemble, cells_dev = prior_members.shape
    slots, rays, width = blocks.shape
    ray_blocks = ray_survey.shape[0]
    count = lax.axis_size("cell")
    owned = ray_blocks // count
    chips = count // 2
    half_blocks = ray_blocks // 2
    split = surveys // 2
    params = pltpu.CompilerParams(vmem_limit_bytes=VMEM_BYTES)

    def bf16(*shape):
        return jax.ShapeDtypeStruct(shape, jnp.bfloat16)

    def f32(*shape):
        return jax.ShapeDtypeStruct(shape, jnp.float32)

    members_f32 = f32(surveys, ensemble, cells_dev)
    halves = (
        bf16(surveys, ensemble, cells_dev),
        bf16(split, ensemble, cells_dev),
        bf16(surveys - split, ensemble, cells_dev),
    )
    travels = (f32(half_blocks, ensemble, rays), bf16(half_blocks, ensemble, rays))

    dense, half, first, second, own, away = pl.pallas_call(
        functools.partial(setup_kernel, owned),
        out_shape=(bf16(ray_blocks, rays, cells_dev),) + halves + travels,
        in_specs=[SMEM] + [HBM] * 5,
        out_specs=(VMEM,) * 6,
        scratch_shapes=[
            pltpu.SMEM(block_ray.shape, jnp.int32),
            pltpu.SMEM(block_cell.shape, jnp.int32),
            pltpu.SMEM(ray_survey.shape, jnp.int32),
            pltpu.VMEM(prior_members.shape, jnp.float32),
            pltpu.VMEM(blocks.shape, blocks.dtype),
            pltpu.VMEM((cells_dev // width, ray_blocks, rays, width), jnp.float32),
            pltpu.SemaphoreType.DMA((4,)),
            pltpu.SemaphoreType.DMA((slots // CHUNK,)),
        ],
        compiler_params=pltpu.CompilerParams(vmem_limit_bytes=SETUP_VMEM_BYTES),
    )(block_count, block_ray, block_cell, ray_survey, prior_members, blocks)

    chip_pairs = [(i, i ^ 1) for i in range(count)]
    link_pairs = [pair for i in range(1, count - 1, 2) for pair in ((i, i + 1), (i + 1, i))]
    same_core = [list(range(core, count, 2)) for core in range(2)]

    def exchange(array):
        return lax.all_to_all(
            array, "cell", split_axis=0, concat_axis=0, axis_index_groups=same_core, tiled=True
        )

    members = prior_members
    for iteration in range(ITERS):
        received = lax.ppermute(away, "cell", chip_pairs)
        chip_travel = pl.pallas_call(
            add_kernel,
            out_shape=bf16(half_blocks, ensemble, rays),
            in_specs=[VMEM] * 2,
            out_specs=VMEM,
            compiler_params=params,
        )(own, received)
        first_halo = lax.ppermute(first, "cell", link_pairs)
        chip_travel, first_halo = lax.optimization_barrier((chip_travel, first_halo))
        chip_halo = lax.ppermute(half, "cell", chip_pairs)
        parts = exchange(chip_travel)
        copies = pl.pallas_call(
            misfit_kernel,
            out_shape=bf16(chips, owned, ensemble, rays),
            in_specs=[VMEM] * 3,
            out_specs=VMEM,
            compiler_params=params,
        )(parts.reshape(chips, owned, ensemble, rays), observed, noise_scale)
        residual = exchange(copies.reshape(half_blocks, ensemble, rays))
        residual, second = lax.optimization_barrier((residual, second))
        second_halo = lax.ppermute(second, "cell", link_pairs)
        other_residual = lax.ppermute(residual, "cell", chip_pairs)
        partial = pl.pallas_call(
            functools.partial(gradient_kernel, owned),
            out_shape=members_f32,
            in_specs=[SMEM] + [VMEM] * 4,
            out_specs=VMEM,
            compiler_params=params,
        )(ray_survey, residual, dense, members, prior_members)
        last = iteration == ITERS - 1
        outputs = (members_f32, halves[0]) if last else (members_f32,) + halves + travels
        results = pl.pallas_call(
            functools.partial(last_kernel if last else step_kernel, owned),
            out_shape=outputs,
            in_specs=[SMEM] + [VMEM] * 7,
            out_specs=(VMEM,) * len(outputs),
            scratch_shapes=[pltpu.VMEM(prior_members.shape, jnp.float32)],
            compiler_params=params,
        )(ray_survey, other_residual, dense, partial, members, chip_halo, first_halo, second_halo)
        if last:
            return results
        members, half, first, second, own, away = results


def solution(mesh):
    placed = (
        P(None, "ens", "cell"),
        P("cell", None, None),
        P("cell"),
        P("cell"),
        P("cell"),
        P(),
        P("cell", "ens", None),
        P("cell", None),
    )
    return jax.shard_map(
        shards,
        mesh=mesh,
        in_specs=placed,
        out_specs=(P(None, "ens", "cell"), P(None, "ens", "cell")),
        check_vma=False,
    )
```

```python
import functools

import jax
import jax.numpy as jnp
from jax import lax
from jax.experimental import pallas as pl
from jax.experimental.pallas import tpu as pltpu
from jax.sharding import PartitionSpec as P

ITERS = 3

ALPHA_PRIOR = 0.5
BETA_TIME = 0.25
GAMMA_DEPTH = 0.25
STEP_SIZE = 0.05
DATA_GAIN = 1.0

CHUNK = 8
VMEM_BYTES = 24 * 1024 * 1024
SETUP_VMEM_BYTES = 60 * 1024 * 1024

SMEM = pl.BlockSpec(memory_space=pltpu.SMEM)
VMEM = pl.BlockSpec(memory_space=pltpu.VMEM)
ANY = pl.BlockSpec(memory_space=pl.ANY)
HBM = pl.BlockSpec(memory_space=pltpu.HBM)


class Order:
    def __init__(self, count, ray_blocks):
        self.half_count = count // 2
        self.owned = ray_blocks // count
        self.half_blocks = ray_blocks // 2
        self.shared = 2 * self.owned

    def here(self):
        index = lax.axis_index("cell")
        return lax.rem(index, 2), lax.div(index, self.half_count)

    def place(self, here, q):
        core, half = here
        owner = lax.div(q, self.owned)
        other_core = lax.rem(owner + core, 2)
        other_half = lax.rem(lax.div(owner, self.half_count) + half, 2)
        chip = lax.div(lax.rem(owner, self.half_count), 2)
        first = other_core * self.half_blocks + chip * self.shared + other_half * self.owned
        return first + lax.rem(q, self.owned)

    def survey(self, here, survey_ref, i):
        core, half = here
        other_core, rest = divmod(i, self.half_blocks)
        chip, rest = divmod(rest, self.shared)
        other_half, offset = divmod(rest, self.owned)
        owner_half = 1 - half if other_half else half
        owner = owner_half * self.half_count + 2 * chip + (1 - core if other_core else core)
        return survey_ref[owner * self.owned + offset]


def forward(order, survey_ref, half_ref, dense_ref, own_ref, away_ref):
    here = order.here()
    half = own_ref.shape[0]
    for i in range(2 * half):
        travel = lax.dot_general(
            half_ref[order.survey(here, survey_ref, i)],
            dense_ref[i],
            (((1,), (1,)), ((), ())),
            preferred_element_type=jnp.float32,
        )
        if i < half:
            own_ref[i] = travel
        else:
            away_ref[i - half] = travel.astype(away_ref.dtype)


def store_half(half, half_ref, first_ref, second_ref):
    split = first_ref.shape[0]
    half_ref[...] = half
    first_ref[...] = half[:split]
    second_ref[...] = half[split:]


def setup_kernel(
    order, count_ref, ray_hbm, cell_hbm, survey_hbm, members_hbm, blocks_hbm,
    dense_ref, half_ref, first_ref, second_ref, own_ref, away_ref,
    ray_ref, cell_ref, survey_ref, members_ref, staged, total, small_sems, sems,
):
    slots, rays, width = blocks_hbm.shape
    chunks = slots // CHUNK
    here = order.here()
    small = [
        pltpu.make_async_copy(source, target, small_sems.at[i])
        for i, (source, target) in enumerate(
            (
                (ray_hbm, ray_ref),
                (cell_hbm, cell_ref),
                (survey_hbm, survey_ref),
                (members_hbm, members_ref),
            )
        )
    ]
    large = []
    for i in range(chunks):
        part = pl.ds(i * CHUNK, CHUNK)
        large.append(pltpu.make_async_copy(blocks_hbm.at[part], staged.at[part], sems.at[i]))
    for copy in small + large:
        copy.start()
    total[...] = jnp.zeros_like(total)
    for copy in small:
        copy.wait()
    store_half(members_ref[...].astype(half_ref.dtype), half_ref, first_ref, second_ref)
    count = count_ref[0]
    for i in range(chunks):
        large[i].wait()

        def add(k, carry):
            b, place = cell_ref[k], order.place(here, ray_ref[k])
            total[b, place] = total[b, place] + staged[k].astype(jnp.float32)
            return carry

        lax.fori_loop(i * CHUNK, jnp.minimum((i + 1) * CHUNK, count), add, 0)
    for b in range(total.shape[0]):
        dense_ref[:, :, b * width : (b + 1) * width] = total[b].astype(dense_ref.dtype)
    forward(order, survey_ref, half_ref, dense_ref, own_ref, away_ref)


def add_kernel(own_ref, received_ref, out_ref):
    out_ref[...] = (own_ref[...] + received_ref[...].astype(jnp.float32)).astype(out_ref.dtype)


def sum_kernel(parts_ref, out_ref, sent_ref):
    total = jnp.sum(parts_ref[...].astype(jnp.float32), axis=0)
    out_ref[...] = total
    sent_ref[...] = total.astype(sent_ref.dtype)


def misfit_kernel(total_ref, received_ref, own_ref, other_ref, halo_ref, out_ref):
    del halo_ref
    owned = own_ref.shape[0]
    ensemble = total_ref.shape[1]
    for side, data_ref in enumerate((own_ref, other_ref)):
        for i in range(owned):
            travel = total_ref[side * owned + i] + received_ref[(1 - side) * owned + i].astype(jnp.float32)
            spread = data_ref[i, ensemble : ensemble + 1, :]
            scaled = (travel - data_ref[i, :ensemble, :]) / spread
            residual = DATA_GAIN * scaled / (spread * (1.0 + scaled * scaled))
            residual = residual.astype(out_ref.dtype)
            for chip in range(out_ref.shape[0]):
                out_ref[chip, side * owned + i] = residual


def gradient_kernel(order, survey_ref, residual_ref, dense_ref, members_ref, prior_ref, grad_ref):
    here = order.here()
    surveys = members_ref.shape[0]
    for s in range(surveys):
        m = members_ref[s]
        value = ALPHA_PRIOR * (m - prior_ref[s])
        if s > 0:
            value = value + BETA_TIME * (m - members_ref[s - 1])
        if s < surveys - 1:
            value = value + BETA_TIME * (m - members_ref[s + 1])
        grad_ref[s] = value
    for i in range(residual_ref.shape[0]):
        s = order.survey(here, survey_ref, i)
        grad_ref[s] = grad_ref[s] + jnp.dot(
            residual_ref[i], dense_ref[i], preferred_element_type=jnp.float32
        )


def finish_gradient(
    order, survey_ref, residual_ref, dense_ref, partial_ref, members_ref, chip_ref, first_halo_ref, second_halo_ref, grad
):
    here = order.here()
    surveys = members_ref.shape[0]
    split = first_halo_ref.shape[0]
    half = residual_ref.shape[0]
    for s in range(surveys):
        link = first_halo_ref[s] if s < split else second_halo_ref[s - split]
        vertical = 2.0 * members_ref[s] - chip_ref[s].astype(jnp.float32) - link.astype(jnp.float32)
        grad[s] = partial_ref[s] + GAMMA_DEPTH * vertical
    for i in range(half):
        s = order.survey(here, survey_ref, half + i)
        grad[s] = grad[s] + jnp.dot(
            residual_ref[i], dense_ref[half + i], preferred_element_type=jnp.float32
        )


def step_kernel(
    order, survey_ref, residual_ref, dense_ref, partial_ref, members_ref, chip_ref, first_halo_ref, second_halo_ref,
    out_ref, half_ref, first_ref, second_ref, own_ref, away_ref,
    grad,
):
    finish_gradient(
        order, survey_ref, residual_ref, dense_ref, partial_ref, members_ref, chip_ref, first_halo_ref, second_halo_ref, grad
    )
    updated = members_ref[...] - STEP_SIZE * grad[...]
    out_ref[...] = updated
    store_half(updated.astype(half_ref.dtype), half_ref, first_ref, second_ref)
    forward(order, survey_ref, half_ref, dense_ref, own_ref, away_ref)


def last_kernel(
    order, survey_ref, residual_ref, dense_ref, partial_ref, members_ref, chip_ref, first_halo_ref, second_halo_ref,
    out_ref, gradient_ref,
    grad,
):
    finish_gradient(
        order, survey_ref, residual_ref, dense_ref, partial_ref, members_ref, chip_ref, first_halo_ref, second_halo_ref, grad
    )
    out_ref[...] = members_ref[...] - STEP_SIZE * grad[...]
    gradient_ref[...] = grad[...].astype(gradient_ref.dtype)


def shards(
    prior_members, blocks, block_ray, block_cell, block_count, ray_survey, observed, noise_scale
):
    surveys, ensemble, cells_dev = prior_members.shape
    slots, rays, width = blocks.shape
    ray_blocks = ray_survey.shape[0]
    count = lax.axis_size("cell")
    order = Order(count, ray_blocks)
    half_count, owned, half_blocks, shared = order.half_count, order.owned, order.half_blocks, order.shared
    chips = half_count // 2
    split = surveys // 2
    params = pltpu.CompilerParams(vmem_limit_bytes=VMEM_BYTES)

    def bf16(*shape):
        return jax.ShapeDtypeStruct(shape, jnp.bfloat16)

    def f32(*shape):
        return jax.ShapeDtypeStruct(shape, jnp.float32)

    members_f32 = f32(surveys, ensemble, cells_dev)
    halves = (
        bf16(surveys, ensemble, cells_dev),
        bf16(split, ensemble, cells_dev),
        bf16(surveys - split, ensemble, cells_dev),
    )
    travels = (f32(half_blocks, ensemble, rays), bf16(half_blocks, ensemble, rays))

    dense, half, first, second, own, away = pl.pallas_call(
        functools.partial(setup_kernel, order),
        out_shape=(bf16(ray_blocks, rays, cells_dev),) + halves + travels,
        in_specs=[SMEM] + [HBM] * 5,
        out_specs=(VMEM,) * 6,
        scratch_shapes=[
            pltpu.SMEM(block_ray.shape, jnp.int32),
            pltpu.SMEM(block_cell.shape, jnp.int32),
            pltpu.SMEM(ray_survey.shape, jnp.int32),
            pltpu.VMEM(prior_members.shape, jnp.float32),
            pltpu.VMEM(blocks.shape, blocks.dtype),
            pltpu.VMEM((cells_dev // width, ray_blocks, rays, width), jnp.float32),
            pltpu.SemaphoreType.DMA((4,)),
            pltpu.SemaphoreType.DMA((slots // CHUNK,)),
        ],
        compiler_params=pltpu.CompilerParams(vmem_limit_bytes=SETUP_VMEM_BYTES),
    )(block_count, block_ray, block_cell, ray_survey, prior_members, blocks)

    chip_pairs = [(i, i ^ 1) for i in range(count)]
    link_pairs = [pair for i in range(1, count - 1, 2) for pair in ((i, i + 1), (i + 1, i))]
    half_pairs = [(i, (i + half_count) % count) for i in range(count)]
    groups = [
        list(range(first + core, first + half_count, 2)) for first in (0, half_count) for core in range(2)
    ]

    own_data = jnp.concatenate(
        [observed, jnp.broadcast_to(noise_scale[:, None, :], (owned, 8, rays))], axis=1
    )
    other_data = lax.ppermute(own_data, "cell", half_pairs)

    def exchange(array):
        return lax.all_to_all(
            array, "cell", split_axis=0, concat_axis=0, axis_index_groups=groups, tiled=True
        )

    members = prior_members
    for iteration in range(ITERS):
        received = lax.ppermute(away, "cell", chip_pairs)
        chip_travel = pl.pallas_call(
            add_kernel,
            out_shape=bf16(half_blocks, ensemble, rays),
            in_specs=[VMEM] * 2,
            out_specs=VMEM,
            compiler_params=params,
        )(own, received)
        first_halo = lax.ppermute(first, "cell", link_pairs)
        second_halo = lax.ppermute(second, "cell", link_pairs)
        chip_halo = lax.ppermute(half, "cell", chip_pairs)
        parts = exchange(chip_travel)
        total, sent = pl.pallas_call(
            sum_kernel,
            out_shape=(f32(shared, ensemble, rays), bf16(shared, ensemble, rays)),
            in_specs=[VMEM],
            out_specs=(VMEM, VMEM),
            compiler_params=params,
        )(parts.reshape(chips, shared, ensemble, rays))
        from_half = lax.ppermute(sent, "cell", half_pairs)
        copies = pl.pallas_call(
            misfit_kernel,
            out_shape=bf16(chips, shared, ensemble, rays),
            in_specs=[VMEM] * 4 + [ANY],
            out_specs=VMEM,
            compiler_params=params,
        )(total, from_half, own_data, other_data, first_halo)
        residual = exchange(copies.reshape(half_blocks, ensemble, rays))
        other_residual = lax.ppermute(residual, "cell", chip_pairs)
        partial = pl.pallas_call(
            functools.partial(gradient_kernel, order),
            out_shape=members_f32,
            in_specs=[SMEM] + [VMEM] * 4,
            out_specs=VMEM,
            compiler_params=params,
        )(ray_survey, residual, dense, members, prior_members)
        last = iteration == ITERS - 1
        outputs = (members_f32, halves[0]) if last else (members_f32,) + halves + travels
        results = pl.pallas_call(
            functools.partial(last_kernel if last else step_kernel, order),
            out_shape=outputs,
            in_specs=[SMEM] + [VMEM] * 7,
            out_specs=(VMEM,) * len(outputs),
            scratch_shapes=[pltpu.VMEM(prior_members.shape, jnp.float32)],
            compiler_params=params,
        )(ray_survey, other_residual, dense, partial, members, chip_halo, first_halo, second_halo)
        if last:
            return results
        members, half, first, second, own, away = results


def solution(mesh):
    placed = (
        P(None, "ens", "cell"),
        P("cell", None, None),
        P("cell"),
        P("cell"),
        P("cell"),
        P(),
        P("cell", "ens", None),
        P("cell", None),
    )
    return jax.shard_map(
        shards,
        mesh=mesh,
        in_specs=placed,
        out_specs=(P(None, "ens", "cell"), P(None, "ens", "cell")),
        check_vma=False,
    )
```

```python
import functools

import jax
import jax.numpy as jnp
from jax import lax
from jax.experimental import pallas as pl
from jax.experimental.pallas import tpu as pltpu
from jax.sharding import PartitionSpec as P

ITERS = 3

ALPHA_PRIOR = 0.5
BETA_TIME = 0.25
GAMMA_DEPTH = 0.25
STEP_SIZE = 0.05
DATA_GAIN = 1.0

CHUNK = 8
VMEM_BYTES = 24 * 1024 * 1024
SETUP_VMEM_BYTES = 60 * 1024 * 1024

SMEM = pl.BlockSpec(memory_space=pltpu.SMEM)
VMEM = pl.BlockSpec(memory_space=pltpu.VMEM)
ANY = pl.BlockSpec(memory_space=pl.ANY)
HBM = pl.BlockSpec(memory_space=pltpu.HBM)


class Order:
    def __init__(self, count, ray_blocks):
        self.half_count = count // 2
        self.owned = ray_blocks // count
        self.half_blocks = ray_blocks // 2
        self.shared = 2 * self.owned

    def here(self):
        index = lax.axis_index("cell")
        return lax.rem(index, 2), lax.div(index, self.half_count)

    def place(self, here, q):
        core, half = here
        owner = lax.div(q, self.owned)
        other_core = lax.rem(owner + core, 2)
        other_half = lax.rem(lax.div(owner, self.half_count) + half, 2)
        chip = lax.div(lax.rem(owner, self.half_count), 2)
        first = other_core * self.half_blocks + chip * self.shared + other_half * self.owned
        return first + lax.rem(q, self.owned)

    def survey(self, here, survey_ref, i):
        core, half = here
        other_core, rest = divmod(i, self.half_blocks)
        chip, rest = divmod(rest, self.shared)
        other_half, offset = divmod(rest, self.owned)
        owner_half = 1 - half if other_half else half
        owner = owner_half * self.half_count + 2 * chip + (1 - core if other_core else core)
        return survey_ref[owner * self.owned + offset]


def forward(order, survey_ref, half_ref, dense_ref, own_ref, away_ref):
    here = order.here()
    half = own_ref.shape[0]
    for i in range(2 * half):
        travel = lax.dot_general(
            half_ref[order.survey(here, survey_ref, i)],
            dense_ref[i],
            (((1,), (1,)), ((), ())),
            preferred_element_type=jnp.float32,
        )
        if i < half:
            own_ref[i] = travel
        else:
            away_ref[i - half] = travel.astype(away_ref.dtype)


def setup_kernel(
    order, count_ref, ray_hbm, cell_hbm, survey_hbm, members_hbm, blocks_hbm,
    dense_ref, half_ref, own_ref, away_ref,
    ray_ref, cell_ref, survey_ref, members_ref, staged, total, small_sems, sems,
):
    slots, rays, width = blocks_hbm.shape
    chunks = slots // CHUNK
    here = order.here()
    small = [
        pltpu.make_async_copy(source, target, small_sems.at[i])
        for i, (source, target) in enumerate(
            (
                (ray_hbm, ray_ref),
                (cell_hbm, cell_ref),
                (survey_hbm, survey_ref),
                (members_hbm, members_ref),
            )
        )
    ]
    large = []
    for i in range(chunks):
        part = pl.ds(i * CHUNK, CHUNK)
        large.append(pltpu.make_async_copy(blocks_hbm.at[part], staged.at[part], sems.at[i]))
    for copy in small + large:
        copy.start()
    total[...] = jnp.zeros_like(total)
    for copy in small:
        copy.wait()
    half_ref[...] = members_ref[...].astype(half_ref.dtype)
    count = count_ref[0]
    for i in range(chunks):
        large[i].wait()

        def add(k, carry):
            b, place = cell_ref[k], order.place(here, ray_ref[k])
            total[b, place] = total[b, place] + staged[k].astype(jnp.float32)
            return carry

        lax.fori_loop(i * CHUNK, jnp.minimum((i + 1) * CHUNK, count), add, 0)
    for b in range(total.shape[0]):
        dense_ref[:, :, b * width : (b + 1) * width] = total[b].astype(dense_ref.dtype)
    forward(order, survey_ref, half_ref, dense_ref, own_ref, away_ref)


def add_kernel(own_ref, received_ref, halo_ref, out_ref):
    del halo_ref
    out_ref[...] = (own_ref[...] + received_ref[...].astype(jnp.float32)).astype(out_ref.dtype)


def sum_kernel(parts_ref, out_ref, sent_ref):
    total = jnp.sum(parts_ref[...].astype(jnp.float32), axis=0)
    out_ref[...] = total
    sent_ref[...] = total.astype(sent_ref.dtype)


def misfit_kernel(total_ref, received_ref, own_ref, other_ref, out_ref):
    owned = own_ref.shape[0]
    ensemble = total_ref.shape[1]
    for side, data_ref in enumerate((own_ref, other_ref)):
        for i in range(owned):
            travel = total_ref[side * owned + i] + received_ref[(1 - side) * owned + i].astype(jnp.float32)
            spread = data_ref[i, ensemble : ensemble + 1, :]
            scaled = (travel - data_ref[i, :ensemble, :]) / spread
            residual = DATA_GAIN * scaled / (spread * (1.0 + scaled * scaled))
            out_ref[side * owned + i] = residual.astype(out_ref.dtype)


def gradient_kernel(order, survey_ref, residual_ref, dense_ref, members_ref, prior_ref, grad_ref):
    here = order.here()
    surveys = members_ref.shape[0]
    for s in range(surveys):
        m = members_ref[s]
        value = ALPHA_PRIOR * (m - prior_ref[s])
        if s > 0:
            value = value + BETA_TIME * (m - members_ref[s - 1])
        if s < surveys - 1:
            value = value + BETA_TIME * (m - members_ref[s + 1])
        grad_ref[s] = value
    for i in range(residual_ref.shape[0]):
        s = order.survey(here, survey_ref, i)
        grad_ref[s] = grad_ref[s] + jnp.dot(
            residual_ref[i], dense_ref[i], preferred_element_type=jnp.float32
        )


def finish_gradient(
    order, survey_ref, residual_ref, dense_ref, partial_ref, members_ref, chip_ref, link_ref, grad
):
    here = order.here()
    surveys = members_ref.shape[0]
    half = residual_ref.shape[0]
    for s in range(surveys):
        neighbours = chip_ref[s].astype(jnp.float32) + link_ref[s].astype(jnp.float32)
        vertical = 2.0 * members_ref[s] - neighbours
        grad[s] = partial_ref[s] + GAMMA_DEPTH * vertical
    for i in range(half):
        s = order.survey(here, survey_ref, half + i)
        grad[s] = grad[s] + jnp.dot(
            residual_ref[i], dense_ref[half + i], preferred_element_type=jnp.float32
        )


def step_kernel(
    order, survey_ref, residual_ref, dense_ref, partial_ref, members_ref, chip_ref, link_ref,
    out_ref, half_ref, own_ref, away_ref,
    grad,
):
    finish_gradient(
        order, survey_ref, residual_ref, dense_ref, partial_ref, members_ref, chip_ref, link_ref, grad
    )
    updated = members_ref[...] - STEP_SIZE * grad[...]
    out_ref[...] = updated
    half_ref[...] = updated.astype(half_ref.dtype)
    forward(order, survey_ref, half_ref, dense_ref, own_ref, away_ref)


def last_kernel(
    order, survey_ref, residual_ref, dense_ref, partial_ref, members_ref, chip_ref, link_ref,
    out_ref, gradient_ref,
    grad,
):
    finish_gradient(
        order, survey_ref, residual_ref, dense_ref, partial_ref, members_ref, chip_ref, link_ref, grad
    )
    out_ref[...] = members_ref[...] - STEP_SIZE * grad[...]
    gradient_ref[...] = grad[...].astype(gradient_ref.dtype)


def shards(
    prior_members, blocks, block_ray, block_cell, block_count, ray_survey, observed, noise_scale
):
    surveys, ensemble, cells_dev = prior_members.shape
    slots, rays, width = blocks.shape
    ray_blocks = ray_survey.shape[0]
    count = lax.axis_size("cell")
    order = Order(count, ray_blocks)
    half_count, owned, half_blocks, shared = order.half_count, order.owned, order.half_blocks, order.shared
    chips = half_count // 2
    params = pltpu.CompilerParams(vmem_limit_bytes=VMEM_BYTES)

    def bf16(*shape):
        return jax.ShapeDtypeStruct(shape, jnp.bfloat16)

    def f32(*shape):
        return jax.ShapeDtypeStruct(shape, jnp.float32)

    members_f32 = f32(surveys, ensemble, cells_dev)
    members_bf16 = bf16(surveys, ensemble, cells_dev)
    travels = (f32(half_blocks, ensemble, rays), bf16(half_blocks, ensemble, rays))

    dense, half, own, away = pl.pallas_call(
        functools.partial(setup_kernel, order),
        out_shape=(bf16(ray_blocks, rays, cells_dev), members_bf16) + travels,
        in_specs=[SMEM] + [HBM] * 5,
        out_specs=(VMEM,) * 4,
        scratch_shapes=[
            pltpu.SMEM(block_ray.shape, jnp.int32),
            pltpu.SMEM(block_cell.shape, jnp.int32),
            pltpu.SMEM(ray_survey.shape, jnp.int32),
            pltpu.VMEM(prior_members.shape, jnp.float32),
            pltpu.VMEM(blocks.shape, blocks.dtype),
            pltpu.VMEM((cells_dev // width, ray_blocks, rays, width), jnp.float32),
            pltpu.SemaphoreType.DMA((4,)),
            pltpu.SemaphoreType.DMA((slots // CHUNK,)),
        ],
        compiler_params=pltpu.CompilerParams(vmem_limit_bytes=SETUP_VMEM_BYTES),
    )(block_count, block_ray, block_cell, ray_survey, prior_members, blocks)

    chip_pairs = [(i, i ^ 1) for i in range(count)]
    link_pairs = [pair for i in range(1, count - 1, 2) for pair in ((i, i + 1), (i + 1, i))]
    half_pairs = [(i, (i + half_count) % count) for i in range(count)]
    groups = [
        list(range(first + core, first + half_count, 2)) for first in (0, half_count) for core in range(2)
    ]

    own_data = jnp.concatenate(
        [observed, jnp.broadcast_to(noise_scale[:, None, :], (owned, 8, rays))], axis=1
    )
    other_data = lax.ppermute(own_data, "cell", half_pairs)

    def exchange(array):
        return lax.all_to_all(
            array, "cell", split_axis=0, concat_axis=0, axis_index_groups=groups, tiled=True
        )

    members = prior_members
    for iteration in range(ITERS):
        received = lax.ppermute(away, "cell", chip_pairs)
        chip_halo = lax.ppermute(half, "cell", chip_pairs)
        chip_travel = pl.pallas_call(
            add_kernel,
            out_shape=bf16(half_blocks, ensemble, rays),
            in_specs=[VMEM, VMEM, ANY],
            out_specs=VMEM,
            compiler_params=params,
        )(own, received, chip_halo)
        link_halo = lax.ppermute(half, "cell", link_pairs)
        parts = exchange(chip_travel)
        total, sent = pl.pallas_call(
            sum_kernel,
            out_shape=(f32(shared, ensemble, rays), bf16(shared, ensemble, rays)),
            in_specs=[VMEM],
            out_specs=(VMEM, VMEM),
            compiler_params=params,
        )(parts.reshape(chips, shared, ensemble, rays))
        from_half = lax.ppermute(sent, "cell", half_pairs)
        shared_residual = pl.pallas_call(
            misfit_kernel,
            out_shape=bf16(shared, ensemble, rays),
            in_specs=[VMEM] * 4,
            out_specs=VMEM,
            compiler_params=params,
        )(total, from_half, own_data, other_data)
        residual = lax.all_gather(
            shared_residual, "cell", axis=0, axis_index_groups=groups, tiled=True
        )
        other_residual = lax.ppermute(residual, "cell", chip_pairs)
        partial = pl.pallas_call(
            functools.partial(gradient_kernel, order),
            out_shape=members_f32,
            in_specs=[SMEM] + [VMEM] * 4,
            out_specs=VMEM,
            compiler_params=params,
        )(ray_survey, residual, dense, members, prior_members)
        last = iteration == ITERS - 1
        outputs = (members_f32, members_bf16) + (() if last else travels)
        results = pl.pallas_call(
            functools.partial(last_kernel if last else step_kernel, order),
            out_shape=outputs,
            in_specs=[SMEM] + [VMEM] * 6,
            out_specs=(VMEM,) * len(outputs),
            scratch_shapes=[pltpu.VMEM(prior_members.shape, jnp.float32)],
            compiler_params=params,
        )(ray_survey, other_residual, dense, partial, members, chip_halo, link_halo)
        if last:
            return results
        members, half, own, away = results


def solution(mesh):
    placed = (
        P(None, "ens", "cell"),
        P("cell", None, None),
        P("cell"),
        P("cell"),
        P("cell"),
        P(),
        P("cell", "ens", None),
        P("cell", None),
    )
    return jax.shard_map(
        shards,
        mesh=mesh,
        in_specs=placed,
        out_specs=(P(None, "ens", "cell"), P(None, "ens", "cell")),
        check_vma=False,
    )
```

```python
import functools

import jax
import jax.numpy as jnp
from jax import lax
from jax.experimental import pallas as pl
from jax.experimental.pallas import tpu as pltpu
from jax.sharding import PartitionSpec as P

ITERS = 3

ALPHA_PRIOR = 0.5
BETA_TIME = 0.25
GAMMA_DEPTH = 0.25
STEP_SIZE = 0.05
DATA_GAIN = 1.0

CHUNK = 8
VMEM_BYTES = 24 * 1024 * 1024
SETUP_VMEM_BYTES = 60 * 1024 * 1024

SMEM = pl.BlockSpec(memory_space=pltpu.SMEM)
VMEM = pl.BlockSpec(memory_space=pltpu.VMEM)
ANY = pl.BlockSpec(memory_space=pl.ANY)
HBM = pl.BlockSpec(memory_space=pltpu.HBM)


class Order:
    def __init__(self, count, ray_blocks):
        self.half_count = count // 2
        self.owned = ray_blocks // count
        self.half_blocks = ray_blocks // 2
        self.shared = 2 * self.owned

    def here(self):
        index = lax.axis_index("cell")
        return lax.rem(index, 2), lax.div(index, self.half_count)

    def place(self, here, q):
        core, half = here
        owner = lax.div(q, self.owned)
        other_core = lax.rem(owner + core, 2)
        other_half = lax.rem(lax.div(owner, self.half_count) + half, 2)
        chip = lax.div(lax.rem(owner, self.half_count), 2)
        first = other_core * self.half_blocks + chip * self.shared + other_half * self.owned
        return first + lax.rem(q, self.owned)

    def survey(self, here, survey_ref, i):
        core, half = here
        other_core, rest = divmod(i, self.half_blocks)
        chip, rest = divmod(rest, self.shared)
        other_half, offset = divmod(rest, self.owned)
        owner_half = 1 - half if other_half else half
        owner = owner_half * self.half_count + 2 * chip + (1 - core if other_core else core)
        return survey_ref[owner * self.owned + offset]


def forward(order, survey_ref, half_ref, dense_ref, own_ref, away_ref):
    here = order.here()
    half = own_ref.shape[0]
    for i in range(2 * half):
        travel = lax.dot_general(
            half_ref[order.survey(here, survey_ref, i)],
            dense_ref[i],
            (((1,), (1,)), ((), ())),
            preferred_element_type=jnp.float32,
        )
        if i < half:
            own_ref[i] = travel
        else:
            away_ref[i - half] = travel.astype(away_ref.dtype)


def setup_kernel(
    order, count_ref, ray_hbm, cell_hbm, survey_hbm, members_hbm, blocks_hbm,
    dense_ref, half_ref, own_ref, away_ref,
    ray_ref, cell_ref, survey_ref, members_ref, staged, total, small_sems, sems,
):
    slots, rays, width = blocks_hbm.shape
    chunks = slots // CHUNK
    here = order.here()
    small = [
        pltpu.make_async_copy(source, target, small_sems.at[i])
        for i, (source, target) in enumerate(
            (
                (ray_hbm, ray_ref),
                (cell_hbm, cell_ref),
                (survey_hbm, survey_ref),
                (members_hbm, members_ref),
            )
        )
    ]
    large = []
    for i in range(chunks):
        part = pl.ds(i * CHUNK, CHUNK)
        large.append(pltpu.make_async_copy(blocks_hbm.at[part], staged.at[part], sems.at[i]))
    for copy in small + large:
        copy.start()
    total[...] = jnp.zeros_like(total)
    for copy in small:
        copy.wait()
    half_ref[...] = members_ref[...].astype(half_ref.dtype)
    count = count_ref[0]
    for i in range(chunks):
        large[i].wait()

        def add(k, carry):
            b, place = cell_ref[k], order.place(here, ray_ref[k])
            total[b, place] = total[b, place] + staged[k].astype(jnp.float32)
            return carry

        lax.fori_loop(i * CHUNK, jnp.minimum((i + 1) * CHUNK, count), add, 0)
    for b in range(total.shape[0]):
        dense_ref[:, :, b * width : (b + 1) * width] = total[b].astype(dense_ref.dtype)
    forward(order, survey_ref, half_ref, dense_ref, own_ref, away_ref)


def add_kernel(own_ref, received_ref, halo_ref, out_ref):
    del halo_ref
    out_ref[...] = (own_ref[...] + received_ref[...].astype(jnp.float32)).astype(out_ref.dtype)


def sum_kernel(parts_ref, out_ref, sent_ref):
    total = jnp.sum(parts_ref[...].astype(jnp.float32), axis=0)
    out_ref[...] = total
    sent_ref[...] = total.astype(sent_ref.dtype)


def misfit_kernel(total_ref, received_ref, own_ref, other_ref, out_ref):
    owned = own_ref.shape[0]
    ensemble = total_ref.shape[1]
    for side, data_ref in enumerate((own_ref, other_ref)):
        for i in range(owned):
            travel = total_ref[side * owned + i] + received_ref[(1 - side) * owned + i].astype(jnp.float32)
            spread = data_ref[i, ensemble : ensemble + 1, :]
            scaled = (travel - data_ref[i, :ensemble, :]) / spread
            residual = DATA_GAIN * scaled / (spread * (1.0 + scaled * scaled))
            residual = residual.astype(out_ref.dtype)
            for chip in range(out_ref.shape[0]):
                out_ref[chip, side * owned + i] = residual


def regular_kernel(members_ref, prior_ref, chip_ref, link_ref, out_ref):
    surveys = members_ref.shape[0]
    for s in range(surveys):
        m = members_ref[s]
        value = ALPHA_PRIOR * (m - prior_ref[s])
        if s > 0:
            value = value + BETA_TIME * (m - members_ref[s - 1])
        if s < surveys - 1:
            value = value + BETA_TIME * (m - members_ref[s + 1])
        neighbours = chip_ref[s].astype(jnp.float32) + link_ref[s].astype(jnp.float32)
        out_ref[s] = value + GAMMA_DEPTH * (2.0 * m - neighbours)


def gradient_kernel(order, survey_ref, residual_ref, dense_ref, regular_ref, grad_ref):
    here = order.here()
    grad_ref[...] = regular_ref[...]
    for i in range(residual_ref.shape[0]):
        s = order.survey(here, survey_ref, i)
        grad_ref[s] = grad_ref[s] + jnp.dot(
            residual_ref[i], dense_ref[i], preferred_element_type=jnp.float32
        )


def finish_gradient(order, survey_ref, residual_ref, dense_ref, partial_ref, grad):
    here = order.here()
    half = residual_ref.shape[0]
    grad[...] = partial_ref[...]
    for i in range(half):
        s = order.survey(here, survey_ref, half + i)
        grad[s] = grad[s] + jnp.dot(
            residual_ref[i], dense_ref[half + i], preferred_element_type=jnp.float32
        )


def step_kernel(
    order, survey_ref, residual_ref, dense_ref, partial_ref, members_ref,
    out_ref, half_ref, own_ref, away_ref,
    grad,
):
    finish_gradient(order, survey_ref, residual_ref, dense_ref, partial_ref, grad)
    updated = members_ref[...] - STEP_SIZE * grad[...]
    out_ref[...] = updated
    half_ref[...] = updated.astype(half_ref.dtype)
    forward(order, survey_ref, half_ref, dense_ref, own_ref, away_ref)


def last_kernel(
    order, survey_ref, residual_ref, dense_ref, partial_ref, members_ref,
    out_ref, gradient_ref,
    grad,
):
    finish_gradient(order, survey_ref, residual_ref, dense_ref, partial_ref, grad)
    out_ref[...] = members_ref[...] - STEP_SIZE * grad[...]
    gradient_ref[...] = grad[...].astype(gradient_ref.dtype)


def shards(
    prior_members, blocks, block_ray, block_cell, block_count, ray_survey, observed, noise_scale
):
    surveys, ensemble, cells_dev = prior_members.shape
    slots, rays, width = blocks.shape
    ray_blocks = ray_survey.shape[0]
    count = lax.axis_size("cell")
    order = Order(count, ray_blocks)
    half_count, owned, half_blocks, shared = order.half_count, order.owned, order.half_blocks, order.shared
    chips = half_count // 2
    params = pltpu.CompilerParams(vmem_limit_bytes=VMEM_BYTES)

    def bf16(*shape):
        return jax.ShapeDtypeStruct(shape, jnp.bfloat16)

    def f32(*shape):
        return jax.ShapeDtypeStruct(shape, jnp.float32)

    members_f32 = f32(surveys, ensemble, cells_dev)
    members_bf16 = bf16(surveys, ensemble, cells_dev)
    travels = (f32(half_blocks, ensemble, rays), bf16(half_blocks, ensemble, rays))

    dense, half, own, away = pl.pallas_call(
        functools.partial(setup_kernel, order),
        out_shape=(bf16(ray_blocks, rays, cells_dev), members_bf16) + travels,
        in_specs=[SMEM] + [HBM] * 5,
        out_specs=(VMEM,) * 4,
        scratch_shapes=[
            pltpu.SMEM(block_ray.shape, jnp.int32),
            pltpu.SMEM(block_cell.shape, jnp.int32),
            pltpu.SMEM(ray_survey.shape, jnp.int32),
            pltpu.VMEM(prior_members.shape, jnp.float32),
            pltpu.VMEM(blocks.shape, blocks.dtype),
            pltpu.VMEM((cells_dev // width, ray_blocks, rays, width), jnp.float32),
            pltpu.SemaphoreType.DMA((4,)),
            pltpu.SemaphoreType.DMA((slots // CHUNK,)),
        ],
        compiler_params=pltpu.CompilerParams(vmem_limit_bytes=SETUP_VMEM_BYTES),
    )(block_count, block_ray, block_cell, ray_survey, prior_members, blocks)

    chip_pairs = [(i, i ^ 1) for i in range(count)]
    link_pairs = [pair for i in range(1, count - 1, 2) for pair in ((i, i + 1), (i + 1, i))]
    half_pairs = [(i, (i + half_count) % count) for i in range(count)]
    groups = [
        list(range(first + core, first + half_count, 2)) for first in (0, half_count) for core in range(2)
    ]

    own_data = jnp.concatenate(
        [observed, jnp.broadcast_to(noise_scale[:, None, :], (owned, 8, rays))], axis=1
    )
    other_data = lax.ppermute(own_data, "cell", half_pairs)

    def exchange(array):
        return lax.all_to_all(
            array, "cell", split_axis=0, concat_axis=0, axis_index_groups=groups, tiled=True
        )

    members = prior_members
    for iteration in range(ITERS):
        received = lax.ppermute(away, "cell", chip_pairs)
        chip_halo = lax.ppermute(half, "cell", chip_pairs)
        chip_travel = pl.pallas_call(
            add_kernel,
            out_shape=bf16(half_blocks, ensemble, rays),
            in_specs=[VMEM, VMEM, ANY],
            out_specs=VMEM,
            compiler_params=params,
        )(own, received, chip_halo)
        link_halo = lax.ppermute(half, "cell", link_pairs)
        parts = exchange(chip_travel)
        total, sent = pl.pallas_call(
            sum_kernel,
            out_shape=(f32(shared, ensemble, rays), bf16(shared, ensemble, rays)),
            in_specs=[VMEM],
            out_specs=(VMEM, VMEM),
            compiler_params=params,
        )(parts.reshape(chips, shared, ensemble, rays))
        from_half = lax.ppermute(sent, "cell", half_pairs)
        copies = pl.pallas_call(
            misfit_kernel,
            out_shape=bf16(chips, shared, ensemble, rays),
            in_specs=[VMEM] * 4,
            out_specs=VMEM,
            compiler_params=params,
        )(total, from_half, own_data, other_data)
        residual = exchange(copies.reshape(half_blocks, ensemble, rays))
        regular = pl.pallas_call(
            regular_kernel,
            out_shape=members_f32,
            in_specs=[VMEM] * 4,
            out_specs=VMEM,
            compiler_params=params,
        )(members, prior_members, chip_halo, link_halo)
        residual, regular = lax.optimization_barrier((residual, regular))
        other_residual = lax.ppermute(residual, "cell", chip_pairs)
        partial = pl.pallas_call(
            functools.partial(gradient_kernel, order),
            out_shape=members_f32,
            in_specs=[SMEM] + [VMEM] * 3,
            out_specs=VMEM,
            compiler_params=params,
        )(ray_survey, residual, dense, regular)
        last = iteration == ITERS - 1
        outputs = (members_f32, members_bf16) + (() if last else travels)
        results = pl.pallas_call(
            functools.partial(last_kernel if last else step_kernel, order),
            out_shape=outputs,
            in_specs=[SMEM] + [VMEM] * 4,
            out_specs=(VMEM,) * len(outputs),
            scratch_shapes=[pltpu.VMEM(prior_members.shape, jnp.float32)],
            compiler_params=params,
        )(ray_survey, other_residual, dense, partial, members)
        if last:
            return results
        members, half, own, away = results


def solution(mesh):
    placed = (
        P(None, "ens", "cell"),
        P("cell", None, None),
        P("cell"),
        P("cell"),
        P("cell"),
        P(),
        P("cell", "ens", None),
        P("cell", None),
    )
    return jax.shard_map(
        shards,
        mesh=mesh,
        in_specs=placed,
        out_specs=(P(None, "ens", "cell"), P(None, "ens", "cell")),
        check_vma=False,
    )
```

```python
import functools

import jax
import jax.numpy as jnp
from jax import lax
from jax.experimental import pallas as pl
from jax.experimental.pallas import tpu as pltpu
from jax.sharding import PartitionSpec as P

ITERS = 3

ALPHA_PRIOR = 0.5
BETA_TIME = 0.25
GAMMA_DEPTH = 0.25
STEP_SIZE = 0.05
DATA_GAIN = 1.0

CHUNK = 8
VMEM_BYTES = 24 * 1024 * 1024
SETUP_VMEM_BYTES = 60 * 1024 * 1024

SMEM = pl.BlockSpec(memory_space=pltpu.SMEM)
VMEM = pl.BlockSpec(memory_space=pltpu.VMEM)
ANY = pl.BlockSpec(memory_space=pl.ANY)
HBM = pl.BlockSpec(memory_space=pltpu.HBM)


class Order:
    def __init__(self, count, ray_blocks):
        self.half_count = count // 2
        self.owned = ray_blocks // count
        self.half_blocks = ray_blocks // 2
        self.shared = 2 * self.owned

    def here(self):
        index = lax.axis_index("cell")
        return lax.rem(index, 2), lax.div(index, self.half_count)

    def place(self, here, q):
        core, half = here
        owner = lax.div(q, self.owned)
        other_core = lax.rem(owner + core, 2)
        other_half = lax.rem(lax.div(owner, self.half_count) + half, 2)
        chip = lax.div(lax.rem(owner, self.half_count), 2)
        first = other_core * self.half_blocks + chip * self.shared + other_half * self.owned
        return first + lax.rem(q, self.owned)

    def survey(self, here, survey_ref, i):
        core, half = here
        other_core, rest = divmod(i, self.half_blocks)
        chip, rest = divmod(rest, self.shared)
        other_half, offset = divmod(rest, self.owned)
        owner_half = 1 - half if other_half else half
        owner = owner_half * self.half_count + 2 * chip + (1 - core if other_core else core)
        return survey_ref[owner * self.owned + offset]


def forward(order, survey_ref, half_ref, dense_ref, own_ref, away_ref):
    here = order.here()
    half = own_ref.shape[0]
    for i in range(2 * half):
        travel = lax.dot_general(
            half_ref[order.survey(here, survey_ref, i)],
            dense_ref[i],
            (((1,), (1,)), ((), ())),
            preferred_element_type=jnp.float32,
        )
        if i < half:
            own_ref[i] = travel
        else:
            away_ref[i - half] = travel.astype(away_ref.dtype)


def setup_kernel(
    order, count_ref, ray_hbm, cell_hbm, survey_hbm, members_hbm, blocks_hbm,
    dense_ref, half_ref, own_ref, away_ref,
    ray_ref, cell_ref, survey_ref, members_ref, staged, total, small_sems, sems,
):
    slots, rays, width = blocks_hbm.shape
    chunks = slots // CHUNK
    here = order.here()
    small = [
        pltpu.make_async_copy(source, target, small_sems.at[i])
        for i, (source, target) in enumerate(
            (
                (ray_hbm, ray_ref),
                (cell_hbm, cell_ref),
                (survey_hbm, survey_ref),
                (members_hbm, members_ref),
            )
        )
    ]
    large = []
    for i in range(chunks):
        part = pl.ds(i * CHUNK, CHUNK)
        large.append(pltpu.make_async_copy(blocks_hbm.at[part], staged.at[part], sems.at[i]))
    for copy in small + large:
        copy.start()
    total[...] = jnp.zeros_like(total)
    for copy in small:
        copy.wait()
    half_ref[...] = members_ref[...].astype(half_ref.dtype)
    count = count_ref[0]
    for i in range(chunks):
        large[i].wait()

        def add(k, carry):
            b, place = cell_ref[k], order.place(here, ray_ref[k])
            total[b, place] = total[b, place] + staged[k].astype(jnp.float32)
            return carry

        lax.fori_loop(i * CHUNK, jnp.minimum((i + 1) * CHUNK, count), add, 0)
    for b in range(total.shape[0]):
        dense_ref[:, :, b * width : (b + 1) * width] = total[b].astype(dense_ref.dtype)
    forward(order, survey_ref, half_ref, dense_ref, own_ref, away_ref)


def add_kernel(own_ref, received_ref, halo_ref, out_ref):
    del halo_ref
    out_ref[...] = (own_ref[...] + received_ref[...].astype(jnp.float32)).astype(out_ref.dtype)


def sum_kernel(parts_ref, out_ref, sent_ref):
    total = jnp.sum(parts_ref[...].astype(jnp.float32), axis=0)
    out_ref[...] = total
    sent_ref[...] = total.astype(sent_ref.dtype)


def misfit_kernel(total_ref, received_ref, own_ref, other_ref, out_ref):
    owned = own_ref.shape[0]
    ensemble = total_ref.shape[1]
    for side, data_ref in enumerate((own_ref, other_ref)):
        for i in range(owned):
            travel = total_ref[side * owned + i] + received_ref[(1 - side) * owned + i].astype(jnp.float32)
            spread = data_ref[i, ensemble : ensemble + 1, :]
            scaled = (travel - data_ref[i, :ensemble, :]) / spread
            residual = DATA_GAIN * scaled / (spread * (1.0 + scaled * scaled))
            residual = residual.astype(out_ref.dtype)
            for chip in range(out_ref.shape[0]):
                out_ref[chip, side * owned + i] = residual


def regular_kernel(members_ref, prior_ref, chip_ref, link_ref, out_ref):
    surveys = members_ref.shape[0]
    for s in range(surveys):
        m = members_ref[s]
        value = ALPHA_PRIOR * (m - prior_ref[s])
        if s > 0:
            value = value + BETA_TIME * (m - members_ref[s - 1])
        if s < surveys - 1:
            value = value + BETA_TIME * (m - members_ref[s + 1])
        neighbours = chip_ref[s].astype(jnp.float32) + link_ref[s].astype(jnp.float32)
        out_ref[s] = value + GAMMA_DEPTH * (2.0 * m - neighbours)


def gradient_kernel(order, survey_ref, residual_ref, dense_ref, regular_ref, grad_ref):
    here = order.here()
    grad_ref[...] = regular_ref[...]
    for i in range(residual_ref.shape[0]):
        s = order.survey(here, survey_ref, i)
        grad_ref[s] = grad_ref[s] + jnp.dot(
            residual_ref[i], dense_ref[i], preferred_element_type=jnp.float32
        )


def finish_gradient(order, survey_ref, residual_ref, dense_ref, partial_ref, grad):
    here = order.here()
    half = residual_ref.shape[0]
    grad[...] = partial_ref[...]
    for i in range(half):
        s = order.survey(here, survey_ref, half + i)
        grad[s] = grad[s] + jnp.dot(
            residual_ref[i], dense_ref[half + i], preferred_element_type=jnp.float32
        )


def step_kernel(
    order, survey_ref, residual_ref, dense_ref, partial_ref, members_ref,
    out_ref, half_ref, own_ref, away_ref,
    grad,
):
    finish_gradient(order, survey_ref, residual_ref, dense_ref, partial_ref, grad)
    updated = members_ref[...] - STEP_SIZE * grad[...]
    out_ref[...] = updated
    half_ref[...] = updated.astype(half_ref.dtype)
    forward(order, survey_ref, half_ref, dense_ref, own_ref, away_ref)


def last_kernel(
    order, survey_ref, residual_ref, dense_ref, partial_ref, members_ref,
    out_ref, gradient_ref,
    grad,
):
    finish_gradient(order, survey_ref, residual_ref, dense_ref, partial_ref, grad)
    out_ref[...] = members_ref[...] - STEP_SIZE * grad[...]
    gradient_ref[...] = grad[...].astype(gradient_ref.dtype)


def shards(
    prior_members, blocks, block_ray, block_cell, block_count, ray_survey, observed, noise_scale
):
    surveys, ensemble, cells_dev = prior_members.shape
    slots, rays, width = blocks.shape
    ray_blocks = ray_survey.shape[0]
    count = lax.axis_size("cell")
    order = Order(count, ray_blocks)
    half_count, owned, half_blocks, shared = order.half_count, order.owned, order.half_blocks, order.shared
    chips = half_count // 2
    params = pltpu.CompilerParams(vmem_limit_bytes=VMEM_BYTES)

    def bf16(*shape):
        return jax.ShapeDtypeStruct(shape, jnp.bfloat16)

    def f32(*shape):
        return jax.ShapeDtypeStruct(shape, jnp.float32)

    members_f32 = f32(surveys, ensemble, cells_dev)
    members_bf16 = bf16(surveys, ensemble, cells_dev)
    travels = (f32(half_blocks, ensemble, rays), bf16(half_blocks, ensemble, rays))

    dense, half, own, away = pl.pallas_call(
        functools.partial(setup_kernel, order),
        out_shape=(bf16(ray_blocks, rays, cells_dev), members_bf16) + travels,
        in_specs=[SMEM] + [HBM] * 5,
        out_specs=(VMEM,) * 4,
        scratch_shapes=[
            pltpu.SMEM(block_ray.shape, jnp.int32),
            pltpu.SMEM(block_cell.shape, jnp.int32),
            pltpu.SMEM(ray_survey.shape, jnp.int32),
            pltpu.VMEM(prior_members.shape, jnp.float32),
            pltpu.VMEM(blocks.shape, blocks.dtype),
            pltpu.VMEM((cells_dev // width, ray_blocks, rays, width), jnp.float32),
            pltpu.SemaphoreType.DMA((4,)),
            pltpu.SemaphoreType.DMA((slots // CHUNK,)),
        ],
        compiler_params=pltpu.CompilerParams(vmem_limit_bytes=SETUP_VMEM_BYTES),
    )(block_count, block_ray, block_cell, ray_survey, prior_members, blocks)

    chip_pairs = [(i, i ^ 1) for i in range(count)]
    link_pairs = [pair for i in range(1, count - 1, 2) for pair in ((i, i + 1), (i + 1, i))]
    half_pairs = [(i, (i + half_count) % count) for i in range(count)]
    groups = [
        list(range(first + core, first + half_count, 2)) for first in (0, half_count) for core in range(2)
    ]

    own_data = jnp.concatenate(
        [observed, jnp.broadcast_to(noise_scale[:, None, :], (owned, 8, rays))], axis=1
    )
    other_data = lax.ppermute(own_data, "cell", half_pairs)

    def exchange(array):
        return lax.all_to_all(
            array, "cell", split_axis=0, concat_axis=0, axis_index_groups=groups, tiled=True
        )

    members = prior_members
    for iteration in range(ITERS):
        received = lax.ppermute(away, "cell", chip_pairs)
        chip_halo = lax.ppermute(half, "cell", chip_pairs)
        chip_travel = pl.pallas_call(
            add_kernel,
            out_shape=bf16(half_blocks, ensemble, rays),
            in_specs=[VMEM, VMEM, ANY],
            out_specs=VMEM,
            compiler_params=params,
        )(own, received, chip_halo)
        link_halo = lax.ppermute(half, "cell", link_pairs)
        parts = exchange(chip_travel)
        regular = pl.pallas_call(
            regular_kernel,
            out_shape=members_f32,
            in_specs=[VMEM] * 4,
            out_specs=VMEM,
            compiler_params=params,
        )(members, prior_members, chip_halo, link_halo)
        parts, regular = lax.optimization_barrier((parts, regular))
        total, sent = pl.pallas_call(
            sum_kernel,
            out_shape=(f32(shared, ensemble, rays), bf16(shared, ensemble, rays)),
            in_specs=[VMEM],
            out_specs=(VMEM, VMEM),
            compiler_params=params,
        )(parts.reshape(chips, shared, ensemble, rays))
        from_half = lax.ppermute(sent, "cell", half_pairs)
        copies = pl.pallas_call(
            misfit_kernel,
            out_shape=bf16(chips, shared, ensemble, rays),
            in_specs=[VMEM] * 4,
            out_specs=VMEM,
            compiler_params=params,
        )(total, from_half, own_data, other_data)
        residual = exchange(copies.reshape(half_blocks, ensemble, rays))
        other_residual = lax.ppermute(residual, "cell", chip_pairs)
        partial = pl.pallas_call(
            functools.partial(gradient_kernel, order),
            out_shape=members_f32,
            in_specs=[SMEM] + [VMEM] * 3,
            out_specs=VMEM,
            compiler_params=params,
        )(ray_survey, residual, dense, regular)
        last = iteration == ITERS - 1
        outputs = (members_f32, members_bf16) + (() if last else travels)
        results = pl.pallas_call(
            functools.partial(last_kernel if last else step_kernel, order),
            out_shape=outputs,
            in_specs=[SMEM] + [VMEM] * 4,
            out_specs=(VMEM,) * len(outputs),
            scratch_shapes=[pltpu.VMEM(prior_members.shape, jnp.float32)],
            compiler_params=params,
        )(ray_survey, other_residual, dense, partial, members)
        if last:
            return results
        members, half, own, away = results


def solution(mesh):
    placed = (
        P(None, "ens", "cell"),
        P("cell", None, None),
        P("cell"),
        P("cell"),
        P("cell"),
        P(),
        P("cell", "ens", None),
        P("cell", None),
    )
    return jax.shard_map(
        shards,
        mesh=mesh,
        in_specs=placed,
        out_specs=(P(None, "ens", "cell"), P(None, "ens", "cell")),
        check_vma=False,
    )
```

```python
import functools

import jax
import jax.numpy as jnp
from jax import lax
from jax.experimental import pallas as pl
from jax.experimental.pallas import tpu as pltpu
from jax.sharding import PartitionSpec as P

ITERS = 3

ALPHA_PRIOR = 0.5
BETA_TIME = 0.25
GAMMA_DEPTH = 0.25
STEP_SIZE = 0.05
DATA_GAIN = 1.0

CHUNK = 8
VMEM_BYTES = 24 * 1024 * 1024
SETUP_VMEM_BYTES = 60 * 1024 * 1024

SMEM = pl.BlockSpec(memory_space=pltpu.SMEM)
VMEM = pl.BlockSpec(memory_space=pltpu.VMEM)
ANY = pl.BlockSpec(memory_space=pl.ANY)
HBM = pl.BlockSpec(memory_space=pltpu.HBM)


class Order:
    def __init__(self, count, ray_blocks):
        self.half_count = count // 2
        self.owned = ray_blocks // count
        self.half_blocks = ray_blocks // 2
        self.shared = 2 * self.owned

    def here(self):
        index = lax.axis_index("cell")
        return lax.rem(index, 2), lax.div(index, self.half_count)

    def place(self, here, q):
        core, half = here
        owner = lax.div(q, self.owned)
        other_core = lax.rem(owner + core, 2)
        other_half = lax.rem(lax.div(owner, self.half_count) + half, 2)
        chip = lax.div(lax.rem(owner, self.half_count), 2)
        first = other_core * self.half_blocks + chip * self.shared + other_half * self.owned
        return first + lax.rem(q, self.owned)

    def survey(self, here, survey_ref, i):
        core, half = here
        other_core, rest = divmod(i, self.half_blocks)
        chip, rest = divmod(rest, self.shared)
        other_half, offset = divmod(rest, self.owned)
        owner_half = 1 - half if other_half else half
        owner = owner_half * self.half_count + 2 * chip + (1 - core if other_core else core)
        return survey_ref[owner * self.owned + offset]


def forward(order, survey_ref, half_ref, dense_ref, own_ref, away_ref):
    here = order.here()
    half = own_ref.shape[0]
    for i in range(2 * half):
        travel = lax.dot_general(
            half_ref[order.survey(here, survey_ref, i)],
            dense_ref[i],
            (((1,), (1,)), ((), ())),
            preferred_element_type=jnp.float32,
        )
        if i < half:
            own_ref[i] = travel
        else:
            away_ref[i - half] = travel.astype(away_ref.dtype)


def setup_kernel(
    order, count_ref, ray_hbm, cell_hbm, survey_hbm, members_hbm, blocks_hbm,
    dense_ref, half_ref, own_ref, away_ref,
    ray_ref, cell_ref, survey_ref, members_ref, staged, total, small_sems, sems,
):
    slots, rays, width = blocks_hbm.shape
    chunks = slots // CHUNK
    here = order.here()
    small = [
        pltpu.make_async_copy(source, target, small_sems.at[i])
        for i, (source, target) in enumerate(
            (
                (ray_hbm, ray_ref),
                (cell_hbm, cell_ref),
                (survey_hbm, survey_ref),
                (members_hbm, members_ref),
            )
        )
    ]
    large = []
    for i in range(chunks):
        part = pl.ds(i * CHUNK, CHUNK)
        large.append(pltpu.make_async_copy(blocks_hbm.at[part], staged.at[part], sems.at[i]))
    for copy in small + large:
        copy.start()
    total[...] = jnp.zeros_like(total)
    for copy in small:
        copy.wait()
    half_ref[...] = members_ref[...].astype(half_ref.dtype)
    count = count_ref[0]
    spare = dense_ref.shape[0]
    for i in range(chunks):
        large[i].wait()
        for k in range(i * CHUNK, (i + 1) * CHUNK):
            place = jnp.where(k < count, order.place(here, ray_ref[k]), spare)
            b = cell_ref[k]
            total[b, place] = total[b, place] + staged[k].astype(jnp.float32)
    for b in range(total.shape[0]):
        dense_ref[:, :, b * width : (b + 1) * width] = total[b, :spare].astype(dense_ref.dtype)
    forward(order, survey_ref, half_ref, dense_ref, own_ref, away_ref)


def add_kernel(own_ref, received_ref, halo_ref, out_ref):
    del halo_ref
    out_ref[...] = (own_ref[...] + received_ref[...].astype(jnp.float32)).astype(out_ref.dtype)


def sum_kernel(parts_ref, out_ref, sent_ref):
    total = jnp.sum(parts_ref[...].astype(jnp.float32), axis=0)
    out_ref[...] = total
    sent_ref[...] = total.astype(sent_ref.dtype)


def misfit_kernel(total_ref, received_ref, own_ref, other_ref, out_ref):
    owned = own_ref.shape[0]
    ensemble = total_ref.shape[1]
    for side, data_ref in enumerate((own_ref, other_ref)):
        for i in range(owned):
            travel = total_ref[side * owned + i] + received_ref[(1 - side) * owned + i].astype(jnp.float32)
            spread = data_ref[i, ensemble : ensemble + 1, :]
            scaled = (travel - data_ref[i, :ensemble, :]) / spread
            residual = DATA_GAIN * scaled / (spread * (1.0 + scaled * scaled))
            residual = residual.astype(out_ref.dtype)
            for chip in range(out_ref.shape[0]):
                out_ref[chip, side * owned + i] = residual


def regular_kernel(members_ref, prior_ref, chip_ref, link_ref, out_ref):
    surveys = members_ref.shape[0]
    for s in range(surveys):
        m = members_ref[s]
        value = ALPHA_PRIOR * (m - prior_ref[s])
        if s > 0:
            value = value + BETA_TIME * (m - members_ref[s - 1])
        if s < surveys - 1:
            value = value + BETA_TIME * (m - members_ref[s + 1])
        neighbours = chip_ref[s].astype(jnp.float32) + link_ref[s].astype(jnp.float32)
        out_ref[s] = value + GAMMA_DEPTH * (2.0 * m - neighbours)


def gradient_kernel(order, survey_ref, residual_ref, dense_ref, regular_ref, grad_ref):
    here = order.here()
    products = [
        jnp.dot(residual_ref[i], dense_ref[i], preferred_element_type=jnp.float32)
        for i in range(residual_ref.shape[0])
    ]
    grad_ref[...] = regular_ref[...]
    for i, product in enumerate(products):
        s = order.survey(here, survey_ref, i)
        grad_ref[s] = grad_ref[s] + product


def finish_gradient(order, survey_ref, residual_ref, dense_ref, partial_ref, grad):
    here = order.here()
    half = residual_ref.shape[0]
    products = [
        jnp.dot(residual_ref[i], dense_ref[half + i], preferred_element_type=jnp.float32)
        for i in range(half)
    ]
    grad[...] = partial_ref[...]
    for i, product in enumerate(products):
        s = order.survey(here, survey_ref, half + i)
        grad[s] = grad[s] + product


def step_kernel(
    order, survey_ref, residual_ref, dense_ref, partial_ref, members_ref,
    out_ref, half_ref, own_ref, away_ref,
    grad,
):
    finish_gradient(order, survey_ref, residual_ref, dense_ref, partial_ref, grad)
    updated = members_ref[...] - STEP_SIZE * grad[...]
    out_ref[...] = updated
    half_ref[...] = updated.astype(half_ref.dtype)
    forward(order, survey_ref, half_ref, dense_ref, own_ref, away_ref)


def last_kernel(
    order, survey_ref, residual_ref, dense_ref, partial_ref, members_ref,
    out_ref, gradient_ref,
    grad,
):
    finish_gradient(order, survey_ref, residual_ref, dense_ref, partial_ref, grad)
    out_ref[...] = members_ref[...] - STEP_SIZE * grad[...]
    gradient_ref[...] = grad[...].astype(gradient_ref.dtype)


def shards(
    prior_members, blocks, block_ray, block_cell, block_count, ray_survey, observed, noise_scale
):
    surveys, ensemble, cells_dev = prior_members.shape
    slots, rays, width = blocks.shape
    ray_blocks = ray_survey.shape[0]
    count = lax.axis_size("cell")
    order = Order(count, ray_blocks)
    half_count, owned, half_blocks, shared = order.half_count, order.owned, order.half_blocks, order.shared
    chips = half_count // 2
    params = pltpu.CompilerParams(vmem_limit_bytes=VMEM_BYTES)

    def bf16(*shape):
        return jax.ShapeDtypeStruct(shape, jnp.bfloat16)

    def f32(*shape):
        return jax.ShapeDtypeStruct(shape, jnp.float32)

    members_f32 = f32(surveys, ensemble, cells_dev)
    members_bf16 = bf16(surveys, ensemble, cells_dev)
    travels = (f32(half_blocks, ensemble, rays), bf16(half_blocks, ensemble, rays))

    in_hbm = [
        pltpu.with_memory_space_constraint(array, pltpu.HBM)
        for array in (block_ray, block_cell, ray_survey, prior_members, blocks)
    ]
    dense, half, own, away = pl.pallas_call(
        functools.partial(setup_kernel, order),
        out_shape=(bf16(ray_blocks, rays, cells_dev), members_bf16) + travels,
        in_specs=[SMEM] + [HBM] * 5,
        out_specs=(VMEM,) * 4,
        scratch_shapes=[
            pltpu.SMEM(block_ray.shape, jnp.int32),
            pltpu.SMEM(block_cell.shape, jnp.int32),
            pltpu.SMEM(ray_survey.shape, jnp.int32),
            pltpu.VMEM(prior_members.shape, jnp.float32),
            pltpu.VMEM(blocks.shape, blocks.dtype),
            pltpu.VMEM((cells_dev // width, ray_blocks + 1, rays, width), jnp.float32),
            pltpu.SemaphoreType.DMA((4,)),
            pltpu.SemaphoreType.DMA((slots // CHUNK,)),
        ],
        compiler_params=pltpu.CompilerParams(vmem_limit_bytes=VMEM_BYTES),
    )(block_count, *in_hbm)

    chip_pairs = [(i, i ^ 1) for i in range(count)]
    link_pairs = [pair for i in range(1, count - 1, 2) for pair in ((i, i + 1), (i + 1, i))]
    half_pairs = [(i, (i + half_count) % count) for i in range(count)]
    groups = [
        list(range(first + core, first + half_count, 2)) for first in (0, half_count) for core in range(2)
    ]

    own_data = jnp.concatenate(
        [observed, jnp.broadcast_to(noise_scale[:, None, :], (owned, 8, rays))], axis=1
    )
    other_data = lax.ppermute(own_data, "cell", half_pairs)

    def exchange(array):
        return lax.all_to_all(
            array, "cell", split_axis=0, concat_axis=0, axis_index_groups=groups, tiled=True
        )

    members = prior_members
    for iteration in range(ITERS):
        received = lax.ppermute(away, "cell", chip_pairs)
        chip_halo = lax.ppermute(half, "cell", chip_pairs)
        chip_travel = pl.pallas_call(
            add_kernel,
            out_shape=bf16(half_blocks, ensemble, rays),
            in_specs=[VMEM, VMEM, ANY],
            out_specs=VMEM,
            compiler_params=params,
        )(own, received, chip_halo)
        link_halo = lax.ppermute(half, "cell", link_pairs)
        parts = exchange(chip_travel)
        regular = pl.pallas_call(
            regular_kernel,
            out_shape=members_f32,
            in_specs=[VMEM] * 4,
            out_specs=VMEM,
            compiler_params=params,
        )(members, prior_members, chip_halo, link_halo)
        parts, regular = lax.optimization_barrier((parts, regular))
        total, sent = pl.pallas_call(
            sum_kernel,
            out_shape=(f32(shared, ensemble, rays), bf16(shared, ensemble, rays)),
            in_specs=[VMEM],
            out_specs=(VMEM, VMEM),
            compiler_params=params,
        )(parts.reshape(chips, shared, ensemble, rays))
        from_half = lax.ppermute(sent, "cell", half_pairs)
        copies = pl.pallas_call(
            misfit_kernel,
            out_shape=bf16(chips, shared, ensemble, rays),
            in_specs=[VMEM] * 4,
            out_specs=VMEM,
            compiler_params=params,
        )(total, from_half, own_data, other_data)
        residual = exchange(copies.reshape(half_blocks, ensemble, rays))
        other_residual = lax.ppermute(residual, "cell", chip_pairs)
        partial = pl.pallas_call(
            functools.partial(gradient_kernel, order),
            out_shape=members_f32,
            in_specs=[SMEM] + [VMEM] * 3,
            out_specs=VMEM,
            compiler_params=params,
        )(ray_survey, residual, dense, regular)
        last = iteration == ITERS - 1
        outputs = (members_f32, members_bf16) + (() if last else travels)
        results = pl.pallas_call(
            functools.partial(last_kernel if last else step_kernel, order),
            out_shape=outputs,
            in_specs=[SMEM] + [VMEM] * 4,
            out_specs=(VMEM,) * len(outputs),
            scratch_shapes=[pltpu.VMEM(prior_members.shape, jnp.float32)],
            compiler_params=params,
        )(ray_survey, other_residual, dense, partial, members)
        if last:
            return results
        members, half, own, away = results


def solution(mesh):
    placed = (
        P(None, "ens", "cell"),
        P("cell", None, None),
        P("cell"),
        P("cell"),
        P("cell"),
        P(),
        P("cell", "ens", None),
        P("cell", None),
    )
    return jax.shard_map(
        shards,
        mesh=mesh,
        in_specs=placed,
        out_specs=(P(None, "ens", "cell"), P(None, "ens", "cell")),
        check_vma=False,
    )
```

```python
import functools

import jax
import jax.numpy as jnp
from jax import lax
from jax.experimental import pallas as pl
from jax.experimental.pallas import tpu as pltpu
from jax.sharding import PartitionSpec as P

ITERS = 3

ALPHA_PRIOR = 0.5
BETA_TIME = 0.25
GAMMA_DEPTH = 0.25
STEP_SIZE = 0.05
DATA_GAIN = 1.0

CHUNK = 8
VMEM_BYTES = 24 * 1024 * 1024
SETUP_VMEM_BYTES = 60 * 1024 * 1024

SMEM = pl.BlockSpec(memory_space=pltpu.SMEM)
VMEM = pl.BlockSpec(memory_space=pltpu.VMEM)
ANY = pl.BlockSpec(memory_space=pl.ANY)
HBM = pl.BlockSpec(memory_space=pltpu.HBM)


class Order:
    def __init__(self, count, ray_blocks):
        self.half_count = count // 2
        self.owned = ray_blocks // count
        self.half_blocks = ray_blocks // 2
        self.shared = 2 * self.owned

    def here(self):
        index = lax.axis_index("cell")
        return lax.rem(index, 2), lax.div(index, self.half_count)

    def place(self, here, q):
        core, half = here
        owner = lax.div(q, self.owned)
        other_core = lax.rem(owner + core, 2)
        other_half = lax.rem(lax.div(owner, self.half_count) + half, 2)
        chip = lax.div(lax.rem(owner, self.half_count), 2)
        first = other_core * self.half_blocks + chip * self.shared + other_half * self.owned
        return first + lax.rem(q, self.owned)

    def survey(self, here, survey_ref, i):
        core, half = here
        other_core, rest = divmod(i, self.half_blocks)
        chip, rest = divmod(rest, self.shared)
        other_half, offset = divmod(rest, self.owned)
        owner_half = 1 - half if other_half else half
        owner = owner_half * self.half_count + 2 * chip + (1 - core if other_core else core)
        return survey_ref[owner * self.owned + offset]


def forward(order, survey_ref, half_ref, dense_ref, own_ref, away_ref):
    here = order.here()
    half = own_ref.shape[0]
    for i in range(2 * half):
        travel = lax.dot_general(
            half_ref[order.survey(here, survey_ref, i)],
            dense_ref[i],
            (((1,), (1,)), ((), ())),
            preferred_element_type=jnp.float32,
        )
        if i < half:
            own_ref[i] = travel
        else:
            away_ref[i - half] = travel.astype(away_ref.dtype)


def store_half(half, half_ref, first_ref, second_ref):
    split = first_ref.shape[0]
    half_ref[...] = half
    first_ref[...] = half[:split]
    second_ref[...] = half[split:]


def setup_kernel(
    order, count_ref, ray_hbm, cell_hbm, survey_hbm, members_hbm, blocks_hbm,
    dense_ref, half_ref, first_ref, second_ref, own_ref, away_ref,
    ray_ref, cell_ref, survey_ref, members_ref, staged, total, small_sems, sems,
):
    slots, rays, width = blocks_hbm.shape
    chunks = slots // CHUNK
    here = order.here()
    small = [
        pltpu.make_async_copy(source, target, small_sems.at[i])
        for i, (source, target) in enumerate(
            (
                (ray_hbm, ray_ref),
                (cell_hbm, cell_ref),
                (survey_hbm, survey_ref),
                (members_hbm, members_ref),
            )
        )
    ]
    large = []
    for i in range(chunks):
        part = pl.ds(i * CHUNK, CHUNK)
        large.append(pltpu.make_async_copy(blocks_hbm.at[part], staged.at[part], sems.at[i]))
    for copy in small + large:
        copy.start()
    total[...] = jnp.zeros_like(total)
    for copy in small:
        copy.wait()
    store_half(members_ref[...].astype(half_ref.dtype), half_ref, first_ref, second_ref)
    count = count_ref[0]
    spare = dense_ref.shape[0]
    for i in range(chunks):
        large[i].wait()
        for k in range(i * CHUNK, (i + 1) * CHUNK):
            place = jnp.where(k < count, order.place(here, ray_ref[k]), spare)
            b = cell_ref[k]
            total[b, place] = total[b, place] + staged[k].astype(jnp.float32)
    for b in range(total.shape[0]):
        dense_ref[:, :, b * width : (b + 1) * width] = total[b, :spare].astype(dense_ref.dtype)
    forward(order, survey_ref, half_ref, dense_ref, own_ref, away_ref)


def add_kernel(own_ref, received_ref, halo_ref, out_ref):
    del halo_ref
    out_ref[...] = (own_ref[...] + received_ref[...].astype(jnp.float32)).astype(out_ref.dtype)


def sum_kernel(parts_ref, out_ref, sent_ref):
    total = jnp.sum(parts_ref[...].astype(jnp.float32), axis=0)
    out_ref[...] = total
    sent_ref[...] = total.astype(sent_ref.dtype)


def misfit_kernel(total_ref, received_ref, own_ref, other_ref, out_ref):
    owned = own_ref.shape[0]
    ensemble = total_ref.shape[1]
    for side, data_ref in enumerate((own_ref, other_ref)):
        for i in range(owned):
            travel = total_ref[side * owned + i] + received_ref[(1 - side) * owned + i].astype(jnp.float32)
            spread = data_ref[i, ensemble : ensemble + 1, :]
            scaled = (travel - data_ref[i, :ensemble, :]) / spread
            residual = DATA_GAIN * scaled / (spread * (1.0 + scaled * scaled))
            residual = residual.astype(out_ref.dtype)
            for chip in range(out_ref.shape[0]):
                out_ref[chip, side * owned + i] = residual


def regular_kernel(low, members_ref, prior_ref, chip_ref, link_ref, out_ref):
    surveys = members_ref.shape[0]
    for i in range(out_ref.shape[0]):
        s = low + i
        m = members_ref[s]
        value = ALPHA_PRIOR * (m - prior_ref[s])
        if s > 0:
            value = value + BETA_TIME * (m - members_ref[s - 1])
        if s < surveys - 1:
            value = value + BETA_TIME * (m - members_ref[s + 1])
        neighbours = chip_ref[s].astype(jnp.float32) + link_ref[i].astype(jnp.float32)
        out_ref[i] = value + GAMMA_DEPTH * (2.0 * m - neighbours)


def gradient_kernel(order, survey_ref, residual_ref, dense_ref, first_ref, second_ref, grad_ref):
    here = order.here()
    products = [
        jnp.dot(residual_ref[i], dense_ref[i], preferred_element_type=jnp.float32)
        for i in range(residual_ref.shape[0])
    ]
    split = first_ref.shape[0]
    grad_ref[:split] = first_ref[...]
    grad_ref[split:] = second_ref[...]
    for i, product in enumerate(products):
        s = order.survey(here, survey_ref, i)
        grad_ref[s] = grad_ref[s] + product


def finish_gradient(order, survey_ref, residual_ref, dense_ref, partial_ref, grad):
    here = order.here()
    half = residual_ref.shape[0]
    products = [
        jnp.dot(residual_ref[i], dense_ref[half + i], preferred_element_type=jnp.float32)
        for i in range(half)
    ]
    grad[...] = partial_ref[...]
    for i, product in enumerate(products):
        s = order.survey(here, survey_ref, half + i)
        grad[s] = grad[s] + product


def step_kernel(
    order, survey_ref, residual_ref, dense_ref, partial_ref, members_ref,
    out_ref, half_ref, first_ref, second_ref, own_ref, away_ref,
    grad,
):
    finish_gradient(order, survey_ref, residual_ref, dense_ref, partial_ref, grad)
    updated = members_ref[...] - STEP_SIZE * grad[...]
    out_ref[...] = updated
    store_half(updated.astype(half_ref.dtype), half_ref, first_ref, second_ref)
    forward(order, survey_ref, half_ref, dense_ref, own_ref, away_ref)


def last_kernel(
    order, survey_ref, residual_ref, dense_ref, partial_ref, members_ref,
    out_ref, gradient_ref,
    grad,
):
    finish_gradient(order, survey_ref, residual_ref, dense_ref, partial_ref, grad)
    out_ref[...] = members_ref[...] - STEP_SIZE * grad[...]
    gradient_ref[...] = grad[...].astype(gradient_ref.dtype)


def shards(
    prior_members, blocks, block_ray, block_cell, block_count, ray_survey, observed, noise_scale
):
    surveys, ensemble, cells_dev = prior_members.shape
    slots, rays, width = blocks.shape
    ray_blocks = ray_survey.shape[0]
    count = lax.axis_size("cell")
    order = Order(count, ray_blocks)
    half_count, owned, half_blocks, shared = order.half_count, order.owned, order.half_blocks, order.shared
    chips = half_count // 2
    params = pltpu.CompilerParams(vmem_limit_bytes=VMEM_BYTES)

    def bf16(*shape):
        return jax.ShapeDtypeStruct(shape, jnp.bfloat16)

    def f32(*shape):
        return jax.ShapeDtypeStruct(shape, jnp.float32)

    members_f32 = f32(surveys, ensemble, cells_dev)
    split = surveys // 2
    halves = (
        bf16(surveys, ensemble, cells_dev),
        bf16(split, ensemble, cells_dev),
        bf16(surveys - split, ensemble, cells_dev),
    )
    travels = (f32(half_blocks, ensemble, rays), bf16(half_blocks, ensemble, rays))

    in_hbm = [
        pltpu.with_memory_space_constraint(array, pltpu.HBM)
        for array in (block_ray, block_cell, ray_survey, prior_members, blocks)
    ]
    dense, half, first, second, own, away = pl.pallas_call(
        functools.partial(setup_kernel, order),
        out_shape=(bf16(ray_blocks, rays, cells_dev),) + halves + travels,
        in_specs=[SMEM] + [HBM] * 5,
        out_specs=(VMEM,) * 6,
        scratch_shapes=[
            pltpu.SMEM(block_ray.shape, jnp.int32),
            pltpu.SMEM(block_cell.shape, jnp.int32),
            pltpu.SMEM(ray_survey.shape, jnp.int32),
            pltpu.VMEM(prior_members.shape, jnp.float32),
            pltpu.VMEM(blocks.shape, blocks.dtype),
            pltpu.VMEM((cells_dev // width, ray_blocks + 1, rays, width), jnp.float32),
            pltpu.SemaphoreType.DMA((4,)),
            pltpu.SemaphoreType.DMA((slots // CHUNK,)),
        ],
        compiler_params=pltpu.CompilerParams(vmem_limit_bytes=VMEM_BYTES),
    )(block_count, *in_hbm)

    chip_pairs = [(i, i ^ 1) for i in range(count)]
    link_pairs = [pair for i in range(1, count - 1, 2) for pair in ((i, i + 1), (i + 1, i))]
    half_pairs = [(i, (i + half_count) % count) for i in range(count)]
    groups = [
        list(range(first + core, first + half_count, 2)) for first in (0, half_count) for core in range(2)
    ]

    own_data = jnp.concatenate(
        [observed, jnp.broadcast_to(noise_scale[:, None, :], (owned, 8, rays))], axis=1
    )
    other_data = lax.ppermute(own_data, "cell", half_pairs)

    def exchange(array):
        return lax.all_to_all(
            array, "cell", split_axis=0, concat_axis=0, axis_index_groups=groups, tiled=True
        )

    members = prior_members
    for iteration in range(ITERS):
        received = lax.ppermute(away, "cell", chip_pairs)
        chip_halo = lax.ppermute(half, "cell", chip_pairs)
        chip_travel = pl.pallas_call(
            add_kernel,
            out_shape=bf16(half_blocks, ensemble, rays),
            in_specs=[VMEM, VMEM, ANY],
            out_specs=VMEM,
            compiler_params=params,
        )(own, received, chip_halo)
        def regular(low, link_halo):
            return pl.pallas_call(
                functools.partial(regular_kernel, low),
                out_shape=f32(*link_halo.shape),
                in_specs=[VMEM] * 4,
                out_specs=VMEM,
                compiler_params=params,
            )(members, prior_members, chip_halo, link_halo)

        first_regular = regular(0, lax.ppermute(first, "cell", link_pairs))
        parts = exchange(chip_travel)
        parts, first_regular = lax.optimization_barrier((parts, first_regular))
        total, sent = pl.pallas_call(
            sum_kernel,
            out_shape=(f32(shared, ensemble, rays), bf16(shared, ensemble, rays)),
            in_specs=[VMEM],
            out_specs=(VMEM, VMEM),
            compiler_params=params,
        )(parts.reshape(chips, shared, ensemble, rays))
        sent, second = lax.optimization_barrier((sent, second))
        from_half = lax.ppermute(sent, "cell", half_pairs)
        second_regular = regular(split, lax.ppermute(second, "cell", link_pairs))
        copies = pl.pallas_call(
            misfit_kernel,
            out_shape=bf16(chips, shared, ensemble, rays),
            in_specs=[VMEM] * 4,
            out_specs=VMEM,
            compiler_params=params,
        )(total, from_half, own_data, other_data)
        residual = exchange(copies.reshape(half_blocks, ensemble, rays))
        residual, second_regular = lax.optimization_barrier((residual, second_regular))
        other_residual = lax.ppermute(residual, "cell", chip_pairs)
        partial = pl.pallas_call(
            functools.partial(gradient_kernel, order),
            out_shape=members_f32,
            in_specs=[SMEM] + [VMEM] * 4,
            out_specs=VMEM,
            compiler_params=params,
        )(ray_survey, residual, dense, first_regular, second_regular)
        last = iteration == ITERS - 1
        outputs = (members_f32, halves[0]) if last else (members_f32,) + halves + travels
        results = pl.pallas_call(
            functools.partial(last_kernel if last else step_kernel, order),
            out_shape=outputs,
            in_specs=[SMEM] + [VMEM] * 4,
            out_specs=(VMEM,) * len(outputs),
            scratch_shapes=[pltpu.VMEM(prior_members.shape, jnp.float32)],
            compiler_params=params,
        )(ray_survey, other_residual, dense, partial, members)
        if last:
            return results
        members, half, first, second, own, away = results


def solution(mesh):
    placed = (
        P(None, "ens", "cell"),
        P("cell", None, None),
        P("cell"),
        P("cell"),
        P("cell"),
        P(),
        P("cell", "ens", None),
        P("cell", None),
    )
    return jax.shard_map(
        shards,
        mesh=mesh,
        in_specs=placed,
        out_specs=(P(None, "ens", "cell"), P(None, "ens", "cell")),
        check_vma=False,
    )
```

```python
import functools

import jax
import jax.numpy as jnp
from jax import lax
from jax.experimental import pallas as pl
from jax.experimental.pallas import tpu as pltpu
from jax.sharding import PartitionSpec as P

ITERS = 3

ALPHA_PRIOR = 0.5
BETA_TIME = 0.25
GAMMA_DEPTH = 0.25
STEP_SIZE = 0.05
DATA_GAIN = 1.0

CHUNK = 8
VMEM_BYTES = 24 * 1024 * 1024
SETUP_VMEM_BYTES = 60 * 1024 * 1024

REGULAR_COST = pl.CostEstimate(flops=1_700_000_000, bytes_accessed=0, transcendentals=0)

SMEM = pl.BlockSpec(memory_space=pltpu.SMEM)
VMEM = pl.BlockSpec(memory_space=pltpu.VMEM)
ANY = pl.BlockSpec(memory_space=pl.ANY)
HBM = pl.BlockSpec(memory_space=pltpu.HBM)


class Order:
    def __init__(self, count, ray_blocks):
        self.half_count = count // 2
        self.owned = ray_blocks // count
        self.half_blocks = ray_blocks // 2
        self.shared = 2 * self.owned

    def here(self):
        index = lax.axis_index("cell")
        return lax.rem(index, 2), lax.div(index, self.half_count)

    def place(self, here, q):
        core, half = here
        owner = lax.div(q, self.owned)
        other_core = lax.rem(owner + core, 2)
        other_half = lax.rem(lax.div(owner, self.half_count) + half, 2)
        chip = lax.div(lax.rem(owner, self.half_count), 2)
        first = other_core * self.half_blocks + chip * self.shared + other_half * self.owned
        return first + lax.rem(q, self.owned)

    def survey(self, here, survey_ref, i):
        core, half = here
        other_core, rest = divmod(i, self.half_blocks)
        chip, rest = divmod(rest, self.shared)
        other_half, offset = divmod(rest, self.owned)
        owner_half = 1 - half if other_half else half
        owner = owner_half * self.half_count + 2 * chip + (1 - core if other_core else core)
        return survey_ref[owner * self.owned + offset]


def forward(order, survey_ref, half_ref, dense_ref, own_ref, away_ref):
    here = order.here()
    half = own_ref.shape[0]
    for i in range(2 * half):
        travel = lax.dot_general(
            half_ref[order.survey(here, survey_ref, i)],
            dense_ref[i],
            (((1,), (1,)), ((), ())),
            preferred_element_type=jnp.float32,
        )
        if i < half:
            own_ref[i] = travel
        else:
            away_ref[i - half] = travel.astype(away_ref.dtype)


def store_half(half, half_ref, first_ref, second_ref):
    split = first_ref.shape[0]
    half_ref[...] = half
    first_ref[...] = half[:split]
    second_ref[...] = half[split:]


def setup_kernel(
    order, count_ref, ray_hbm, cell_hbm, survey_hbm, members_hbm, blocks_hbm,
    dense_ref, half_ref, first_ref, second_ref, own_ref, away_ref,
    ray_ref, cell_ref, survey_ref, members_ref, staged, total, small_sems, sems,
):
    slots, rays, width = blocks_hbm.shape
    chunks = slots // CHUNK
    here = order.here()
    small = [
        pltpu.make_async_copy(source, target, small_sems.at[i])
        for i, (source, target) in enumerate(
            (
                (ray_hbm, ray_ref),
                (cell_hbm, cell_ref),
                (survey_hbm, survey_ref),
                (members_hbm, members_ref),
            )
        )
    ]
    large = []
    for i in range(chunks):
        part = pl.ds(i * CHUNK, CHUNK)
        large.append(pltpu.make_async_copy(blocks_hbm.at[part], staged.at[part], sems.at[i]))
    for copy in small + large:
        copy.start()
    total[...] = jnp.zeros_like(total)
    for copy in small:
        copy.wait()
    store_half(members_ref[...].astype(half_ref.dtype), half_ref, first_ref, second_ref)
    count = count_ref[0]
    spare = dense_ref.shape[0]
    for i in range(chunks):
        large[i].wait()
        for k in range(i * CHUNK, (i + 1) * CHUNK):
            place = jnp.where(k < count, order.place(here, ray_ref[k]), spare)
            b = cell_ref[k]
            total[b, place] = total[b, place] + staged[k].astype(jnp.float32)
    for b in range(total.shape[0]):
        dense_ref[:, :, b * width : (b + 1) * width] = total[b, :spare].astype(dense_ref.dtype)
    forward(order, survey_ref, half_ref, dense_ref, own_ref, away_ref)


def add_kernel(own_ref, received_ref, halo_ref, out_ref):
    del halo_ref
    out_ref[...] = (own_ref[...] + received_ref[...].astype(jnp.float32)).astype(out_ref.dtype)


def sum_kernel(parts_ref, out_ref, sent_ref):
    total = jnp.sum(parts_ref[...].astype(jnp.float32), axis=0)
    out_ref[...] = total
    sent_ref[...] = total.astype(sent_ref.dtype)


def misfit_kernel(total_ref, received_ref, own_ref, other_ref, out_ref):
    owned = own_ref.shape[0]
    ensemble = total_ref.shape[1]
    for side, data_ref in enumerate((own_ref, other_ref)):
        for i in range(owned):
            travel = total_ref[side * owned + i] + received_ref[(1 - side) * owned + i].astype(jnp.float32)
            spread = data_ref[i, ensemble : ensemble + 1, :]
            scaled = (travel - data_ref[i, :ensemble, :]) / spread
            residual = DATA_GAIN * scaled / (spread * (1.0 + scaled * scaled))
            residual = residual.astype(out_ref.dtype)
            for chip in range(out_ref.shape[0]):
                out_ref[chip, side * owned + i] = residual


def regular_kernel(low, members_ref, prior_ref, chip_ref, link_ref, out_ref):
    surveys = members_ref.shape[0]
    for i in range(out_ref.shape[0]):
        s = low + i
        m = members_ref[s]
        value = ALPHA_PRIOR * (m - prior_ref[s])
        if s > 0:
            value = value + BETA_TIME * (m - members_ref[s - 1])
        if s < surveys - 1:
            value = value + BETA_TIME * (m - members_ref[s + 1])
        neighbours = chip_ref[s].astype(jnp.float32) + link_ref[i].astype(jnp.float32)
        out_ref[i] = value + GAMMA_DEPTH * (2.0 * m - neighbours)


def gradient_kernel(order, survey_ref, residual_ref, dense_ref, first_ref, second_ref, grad_ref):
    here = order.here()
    products = [
        jnp.dot(residual_ref[i], dense_ref[i], preferred_element_type=jnp.float32)
        for i in range(residual_ref.shape[0])
    ]
    split = first_ref.shape[0]
    grad_ref[:split] = first_ref[...]
    grad_ref[split:] = second_ref[...]
    for i, product in enumerate(products):
        s = order.survey(here, survey_ref, i)
        grad_ref[s] = grad_ref[s] + product


def finish_gradient(order, survey_ref, residual_ref, dense_ref, partial_ref, grad):
    here = order.here()
    half = residual_ref.shape[0]
    products = [
        jnp.dot(residual_ref[i], dense_ref[half + i], preferred_element_type=jnp.float32)
        for i in range(half)
    ]
    grad[...] = partial_ref[...]
    for i, product in enumerate(products):
        s = order.survey(here, survey_ref, half + i)
        grad[s] = grad[s] + product


def step_kernel(
    order, survey_ref, residual_ref, dense_ref, partial_ref, members_ref,
    out_ref, half_ref, first_ref, second_ref, own_ref, away_ref,
    grad,
):
    finish_gradient(order, survey_ref, residual_ref, dense_ref, partial_ref, grad)
    updated = members_ref[...] - STEP_SIZE * grad[...]
    out_ref[...] = updated
    store_half(updated.astype(half_ref.dtype), half_ref, first_ref, second_ref)
    forward(order, survey_ref, half_ref, dense_ref, own_ref, away_ref)


def last_kernel(
    order, survey_ref, residual_ref, dense_ref, partial_ref, members_ref,
    out_ref, gradient_ref,
    grad,
):
    finish_gradient(order, survey_ref, residual_ref, dense_ref, partial_ref, grad)
    out_ref[...] = members_ref[...] - STEP_SIZE * grad[...]
    gradient_ref[...] = grad[...].astype(gradient_ref.dtype)


def shards(
    prior_members, blocks, block_ray, block_cell, block_count, ray_survey, observed, noise_scale
):
    surveys, ensemble, cells_dev = prior_members.shape
    slots, rays, width = blocks.shape
    ray_blocks = ray_survey.shape[0]
    count = lax.axis_size("cell")
    order = Order(count, ray_blocks)
    half_count, owned, half_blocks, shared = order.half_count, order.owned, order.half_blocks, order.shared
    chips = half_count // 2
    params = pltpu.CompilerParams(vmem_limit_bytes=VMEM_BYTES)

    def bf16(*shape):
        return jax.ShapeDtypeStruct(shape, jnp.bfloat16)

    def f32(*shape):
        return jax.ShapeDtypeStruct(shape, jnp.float32)

    members_f32 = f32(surveys, ensemble, cells_dev)
    split = surveys // 2
    halves = (
        bf16(surveys, ensemble, cells_dev),
        bf16(split, ensemble, cells_dev),
        bf16(surveys - split, ensemble, cells_dev),
    )
    travels = (f32(half_blocks, ensemble, rays), bf16(half_blocks, ensemble, rays))

    in_hbm = [
        pltpu.with_memory_space_constraint(array, pltpu.HBM)
        for array in (block_ray, block_cell, ray_survey, prior_members, blocks)
    ]
    dense, half, first, second, own, away = pl.pallas_call(
        functools.partial(setup_kernel, order),
        out_shape=(bf16(ray_blocks, rays, cells_dev),) + halves + travels,
        in_specs=[SMEM] + [HBM] * 5,
        out_specs=(VMEM,) * 6,
        scratch_shapes=[
            pltpu.SMEM(block_ray.shape, jnp.int32),
            pltpu.SMEM(block_cell.shape, jnp.int32),
            pltpu.SMEM(ray_survey.shape, jnp.int32),
            pltpu.VMEM(prior_members.shape, jnp.float32),
            pltpu.VMEM(blocks.shape, blocks.dtype),
            pltpu.VMEM((cells_dev // width, ray_blocks + 1, rays, width), jnp.float32),
            pltpu.SemaphoreType.DMA((4,)),
            pltpu.SemaphoreType.DMA((slots // CHUNK,)),
        ],
        compiler_params=pltpu.CompilerParams(vmem_limit_bytes=VMEM_BYTES),
    )(block_count, *in_hbm)

    chip_pairs = [(i, i ^ 1) for i in range(count)]
    link_pairs = [pair for i in range(1, count - 1, 2) for pair in ((i, i + 1), (i + 1, i))]
    half_pairs = [(i, (i + half_count) % count) for i in range(count)]
    groups = [
        list(range(first + core, first + half_count, 2)) for first in (0, half_count) for core in range(2)
    ]

    own_data = jnp.concatenate(
        [observed, jnp.broadcast_to(noise_scale[:, None, :], (owned, 8, rays))], axis=1
    )
    other_data = lax.ppermute(own_data, "cell", half_pairs)

    def exchange(array):
        return lax.all_to_all(
            array, "cell", split_axis=0, concat_axis=0, axis_index_groups=groups, tiled=True
        )

    members = prior_members
    for iteration in range(ITERS):
        received = lax.ppermute(away, "cell", chip_pairs)
        chip_halo = lax.ppermute(half, "cell", chip_pairs)
        chip_travel = pl.pallas_call(
            add_kernel,
            out_shape=bf16(half_blocks, ensemble, rays),
            in_specs=[VMEM, VMEM, ANY],
            out_specs=VMEM,
            compiler_params=params,
        )(own, received, chip_halo)
        def regular(low, link_halo):
            return pl.pallas_call(
                functools.partial(regular_kernel, low),
                out_shape=f32(*link_halo.shape),
                in_specs=[VMEM] * 4,
                out_specs=VMEM,
                compiler_params=params,
                cost_estimate=REGULAR_COST,
            )(members, prior_members, chip_halo, link_halo)

        first_regular = regular(0, lax.ppermute(first, "cell", link_pairs))
        parts = exchange(chip_travel)
        parts, first_regular = lax.optimization_barrier((parts, first_regular))
        total, sent = pl.pallas_call(
            sum_kernel,
            out_shape=(f32(shared, ensemble, rays), bf16(shared, ensemble, rays)),
            in_specs=[VMEM],
            out_specs=(VMEM, VMEM),
            compiler_params=params,
        )(parts.reshape(chips, shared, ensemble, rays))
        sent, second = lax.optimization_barrier((sent, second))
        from_half = lax.ppermute(sent, "cell", half_pairs)
        second_regular = regular(split, lax.ppermute(second, "cell", link_pairs))
        copies = pl.pallas_call(
            misfit_kernel,
            out_shape=bf16(chips, shared, ensemble, rays),
            in_specs=[VMEM] * 4,
            out_specs=VMEM,
            compiler_params=params,
        )(total, from_half, own_data, other_data)
        residual = exchange(copies.reshape(half_blocks, ensemble, rays))
        residual, second_regular = lax.optimization_barrier((residual, second_regular))
        other_residual = lax.ppermute(residual, "cell", chip_pairs)
        partial = pl.pallas_call(
            functools.partial(gradient_kernel, order),
            out_shape=members_f32,
            in_specs=[SMEM] + [VMEM] * 4,
            out_specs=VMEM,
            compiler_params=params,
        )(ray_survey, residual, dense, first_regular, second_regular)
        last = iteration == ITERS - 1
        outputs = (members_f32, halves[0]) if last else (members_f32,) + halves + travels
        results = pl.pallas_call(
            functools.partial(last_kernel if last else step_kernel, order),
            out_shape=outputs,
            in_specs=[SMEM] + [VMEM] * 4,
            out_specs=(VMEM,) * len(outputs),
            scratch_shapes=[pltpu.VMEM(prior_members.shape, jnp.float32)],
            compiler_params=params,
        )(ray_survey, other_residual, dense, partial, members)
        if last:
            return results
        members, half, first, second, own, away = results


def solution(mesh):
    placed = (
        P(None, "ens", "cell"),
        P("cell", None, None),
        P("cell"),
        P("cell"),
        P("cell"),
        P(),
        P("cell", "ens", None),
        P("cell", None),
    )
    return jax.shard_map(
        shards,
        mesh=mesh,
        in_specs=placed,
        out_specs=(P(None, "ens", "cell"), P(None, "ens", "cell")),
        check_vma=False,
    )
```

```python
import functools

import jax
import jax.numpy as jnp
from jax import lax
from jax.experimental import pallas as pl
from jax.experimental.pallas import tpu as pltpu
from jax.sharding import PartitionSpec as P

ITERS = 3

ALPHA_PRIOR = 0.5
BETA_TIME = 0.25
GAMMA_DEPTH = 0.25
STEP_SIZE = 0.05
DATA_GAIN = 1.0

CHUNK = 8
VMEM_BYTES = 24 * 1024 * 1024
SETUP_VMEM_BYTES = 60 * 1024 * 1024

SMEM = pl.BlockSpec(memory_space=pltpu.SMEM)
VMEM = pl.BlockSpec(memory_space=pltpu.VMEM)
ANY = pl.BlockSpec(memory_space=pl.ANY)
HBM = pl.BlockSpec(memory_space=pltpu.HBM)


class Order:
    def __init__(self, count, ray_blocks):
        self.owned = ray_blocks // count
        self.half_blocks = ray_blocks // 2
        self.shared = 2 * self.owned

    def here(self):
        index = lax.axis_index("cell")
        return lax.rem(index, 2), lax.rem(lax.div(index, 2), 2)

    def place(self, here, q):
        core, side = here
        owner = lax.div(q, self.owned)
        other_core = lax.rem(owner + core, 2)
        other_side = lax.rem(lax.div(owner, 2) + side, 2)
        pair = lax.div(owner, 4)
        first = other_core * self.half_blocks + pair * self.shared + other_side * self.owned
        return first + lax.rem(q, self.owned)

    def survey(self, here, survey_ref, i):
        core, side = here
        other_core, rest = divmod(i, self.half_blocks)
        pair, rest = divmod(rest, self.shared)
        other_side, offset = divmod(rest, self.owned)
        owner = 4 * pair + 2 * (1 - side if other_side else side) + (1 - core if other_core else core)
        return survey_ref[owner * self.owned + offset]


def forward(order, survey_ref, half_ref, dense_ref, own_ref, away_ref):
    here = order.here()
    half = own_ref.shape[0]
    for i in range(2 * half):
        travel = lax.dot_general(
            half_ref[order.survey(here, survey_ref, i)],
            dense_ref[i],
            (((1,), (1,)), ((), ())),
            preferred_element_type=jnp.float32,
        )
        if i < half:
            own_ref[i] = travel
        else:
            away_ref[i - half] = travel.astype(away_ref.dtype)


def setup_kernel(
    order, count_ref, ray_hbm, cell_hbm, survey_hbm, members_hbm, blocks_hbm,
    dense_ref, half_ref, own_ref, away_ref,
    ray_ref, cell_ref, survey_ref, members_ref, staged, total, small_sems, sems,
):
    slots, rays, width = blocks_hbm.shape
    chunks = slots // CHUNK
    here = order.here()
    small = [
        pltpu.make_async_copy(source, target, small_sems.at[i])
        for i, (source, target) in enumerate(
            (
                (ray_hbm, ray_ref),
                (cell_hbm, cell_ref),
                (survey_hbm, survey_ref),
                (members_hbm, members_ref),
            )
        )
    ]
    large = []
    for i in range(chunks):
        part = pl.ds(i * CHUNK, CHUNK)
        large.append(pltpu.make_async_copy(blocks_hbm.at[part], staged.at[part], sems.at[i]))
    for copy in small + large:
        copy.start()
    total[...] = jnp.zeros_like(total)
    for copy in small:
        copy.wait()
    half_ref[...] = members_ref[...].astype(half_ref.dtype)
    count = count_ref[0]
    spare = dense_ref.shape[0]
    for i in range(chunks):
        large[i].wait()
        for k in range(i * CHUNK, (i + 1) * CHUNK):
            place = jnp.where(k < count, order.place(here, ray_ref[k]), spare)
            b = cell_ref[k]
            total[b, place] = total[b, place] + staged[k].astype(jnp.float32)
    for b in range(total.shape[0]):
        dense_ref[:, :, b * width : (b + 1) * width] = total[b, :spare].astype(dense_ref.dtype)
    forward(order, survey_ref, half_ref, dense_ref, own_ref, away_ref)


def add_kernel(own_ref, received_ref, halo_ref, out_ref):
    del halo_ref
    out_ref[...] = (own_ref[...] + received_ref[...].astype(jnp.float32)).astype(out_ref.dtype)


def sum_kernel(parts_ref, out_ref, sent_ref):
    total = jnp.sum(parts_ref[...].astype(jnp.float32), axis=0)
    out_ref[...] = total
    sent_ref[...] = total.astype(sent_ref.dtype)


def misfit_kernel(total_ref, received_ref, own_ref, other_ref, out_ref):
    owned = own_ref.shape[0]
    ensemble = total_ref.shape[1]
    for side, data_ref in enumerate((own_ref, other_ref)):
        for i in range(owned):
            travel = total_ref[side * owned + i] + received_ref[(1 - side) * owned + i].astype(jnp.float32)
            spread = data_ref[i, ensemble : ensemble + 1, :]
            scaled = (travel - data_ref[i, :ensemble, :]) / spread
            residual = DATA_GAIN * scaled / (spread * (1.0 + scaled * scaled))
            residual = residual.astype(out_ref.dtype)
            for pair in range(out_ref.shape[0]):
                out_ref[pair, side * owned + i] = residual


def regular_kernel(members_ref, prior_ref, chip_ref, link_ref, out_ref):
    surveys = members_ref.shape[0]
    for s in range(surveys):
        m = members_ref[s]
        value = ALPHA_PRIOR * (m - prior_ref[s])
        if s > 0:
            value = value + BETA_TIME * (m - members_ref[s - 1])
        if s < surveys - 1:
            value = value + BETA_TIME * (m - members_ref[s + 1])
        neighbours = chip_ref[s].astype(jnp.float32) + link_ref[s].astype(jnp.float32)
        out_ref[s] = value + GAMMA_DEPTH * (2.0 * m - neighbours)


def gradient_kernel(order, survey_ref, residual_ref, dense_ref, regular_ref, grad_ref):
    here = order.here()
    products = [
        jnp.dot(residual_ref[i], dense_ref[i], preferred_element_type=jnp.float32)
        for i in range(residual_ref.shape[0])
    ]
    grad_ref[...] = regular_ref[...]
    for i, product in enumerate(products):
        s = order.survey(here, survey_ref, i)
        grad_ref[s] = grad_ref[s] + product


def finish_gradient(order, survey_ref, residual_ref, dense_ref, partial_ref, grad):
    here = order.here()
    half = residual_ref.shape[0]
    products = [
        jnp.dot(residual_ref[i], dense_ref[half + i], preferred_element_type=jnp.float32)
        for i in range(half)
    ]
    grad[...] = partial_ref[...]
    for i, product in enumerate(products):
        s = order.survey(here, survey_ref, half + i)
        grad[s] = grad[s] + product


def step_kernel(
    order, survey_ref, residual_ref, dense_ref, partial_ref, members_ref,
    out_ref, half_ref, own_ref, away_ref,
    grad,
):
    finish_gradient(order, survey_ref, residual_ref, dense_ref, partial_ref, grad)
    updated = members_ref[...] - STEP_SIZE * grad[...]
    out_ref[...] = updated
    half_ref[...] = updated.astype(half_ref.dtype)
    forward(order, survey_ref, half_ref, dense_ref, own_ref, away_ref)


def last_kernel(
    order, survey_ref, residual_ref, dense_ref, partial_ref, members_ref,
    out_ref, gradient_ref,
    grad,
):
    finish_gradient(order, survey_ref, residual_ref, dense_ref, partial_ref, grad)
    out_ref[...] = members_ref[...] - STEP_SIZE * grad[...]
    gradient_ref[...] = grad[...].astype(gradient_ref.dtype)


def shards(
    prior_members, blocks, block_ray, block_cell, block_count, ray_survey, observed, noise_scale
):
    surveys, ensemble, cells_dev = prior_members.shape
    slots, rays, width = blocks.shape
    ray_blocks = ray_survey.shape[0]
    count = lax.axis_size("cell")
    order = Order(count, ray_blocks)
    owned, half_blocks, shared = order.owned, order.half_blocks, order.shared
    pairs = count // 4
    params = pltpu.CompilerParams(vmem_limit_bytes=VMEM_BYTES)

    def bf16(*shape):
        return jax.ShapeDtypeStruct(shape, jnp.bfloat16)

    def f32(*shape):
        return jax.ShapeDtypeStruct(shape, jnp.float32)

    members_f32 = f32(surveys, ensemble, cells_dev)
    members_bf16 = bf16(surveys, ensemble, cells_dev)
    travels = (f32(half_blocks, ensemble, rays), bf16(half_blocks, ensemble, rays))

    in_hbm = [
        pltpu.with_memory_space_constraint(array, pltpu.HBM)
        for array in (block_ray, block_cell, ray_survey, prior_members, blocks)
    ]
    dense, half, own, away = pl.pallas_call(
        functools.partial(setup_kernel, order),
        out_shape=(bf16(ray_blocks, rays, cells_dev), members_bf16) + travels,
        in_specs=[SMEM] + [HBM] * 5,
        out_specs=(VMEM,) * 4,
        scratch_shapes=[
            pltpu.SMEM(block_ray.shape, jnp.int32),
            pltpu.SMEM(block_cell.shape, jnp.int32),
            pltpu.SMEM(ray_survey.shape, jnp.int32),
            pltpu.VMEM(prior_members.shape, jnp.float32),
            pltpu.VMEM(blocks.shape, blocks.dtype),
            pltpu.VMEM((cells_dev // width, ray_blocks + 1, rays, width), jnp.float32),
            pltpu.SemaphoreType.DMA((4,)),
            pltpu.SemaphoreType.DMA((slots // CHUNK,)),
        ],
        compiler_params=pltpu.CompilerParams(vmem_limit_bytes=VMEM_BYTES),
    )(block_count, *in_hbm)

    chip_pairs = [(i, i ^ 1) for i in range(count)]
    link_pairs = [pair for i in range(1, count - 1, 2) for pair in ((i, i + 1), (i + 1, i))]
    side_pairs = [(i, i ^ 2) for i in range(count)]
    groups = [list(range(first, count, 4)) for first in range(4)]

    own_data = jnp.concatenate(
        [observed, jnp.broadcast_to(noise_scale[:, None, :], (owned, 8, rays))], axis=1
    )
    other_data = lax.ppermute(own_data, "cell", side_pairs)

    def exchange(array):
        return lax.all_to_all(
            array, "cell", split_axis=0, concat_axis=0, axis_index_groups=groups, tiled=True
        )

    members = prior_members
    for iteration in range(ITERS):
        received = lax.ppermute(away, "cell", chip_pairs)
        chip_halo = lax.ppermute(half, "cell", chip_pairs)
        chip_travel = pl.pallas_call(
            add_kernel,
            out_shape=bf16(half_blocks, ensemble, rays),
            in_specs=[VMEM, VMEM, ANY],
            out_specs=VMEM,
            compiler_params=params,
        )(own, received, chip_halo)
        link_halo = lax.ppermute(half, "cell", link_pairs)
        parts = exchange(chip_travel)
        total, sent = pl.pallas_call(
            sum_kernel,
            out_shape=(f32(shared, ensemble, rays), bf16(shared, ensemble, rays)),
            in_specs=[VMEM],
            out_specs=(VMEM, VMEM),
            compiler_params=params,
        )(parts.reshape(pairs, shared, ensemble, rays))
        from_side = lax.ppermute(sent, "cell", side_pairs)
        regular = pl.pallas_call(
            regular_kernel,
            out_shape=members_f32,
            in_specs=[VMEM] * 4,
            out_specs=VMEM,
            compiler_params=params,
        )(members, prior_members, chip_halo, link_halo)
        from_side, regular = lax.optimization_barrier((from_side, regular))
        copies = pl.pallas_call(
            misfit_kernel,
            out_shape=bf16(pairs, shared, ensemble, rays),
            in_specs=[VMEM] * 4,
            out_specs=VMEM,
            compiler_params=params,
        )(total, from_side, own_data, other_data)
        residual = exchange(copies.reshape(half_blocks, ensemble, rays))
        other_residual = lax.ppermute(residual, "cell", chip_pairs)
        partial = pl.pallas_call(
            functools.partial(gradient_kernel, order),
            out_shape=members_f32,
            in_specs=[SMEM] + [VMEM] * 3,
            out_specs=VMEM,
            compiler_params=params,
        )(ray_survey, residual, dense, regular)
        last = iteration == ITERS - 1
        outputs = (members_f32, members_bf16) + (() if last else travels)
        results = pl.pallas_call(
            functools.partial(last_kernel if last else step_kernel, order),
            out_shape=outputs,
            in_specs=[SMEM] + [VMEM] * 4,
            out_specs=(VMEM,) * len(outputs),
            scratch_shapes=[pltpu.VMEM(prior_members.shape, jnp.float32)],
            compiler_params=params,
        )(ray_survey, other_residual, dense, partial, members)
        if last:
            return results
        members, half, own, away = results


def solution(mesh):
    placed = (
        P(None, "ens", "cell"),
        P("cell", None, None),
        P("cell"),
        P("cell"),
        P("cell"),
        P(),
        P("cell", "ens", None),
        P("cell", None),
    )
    return jax.shard_map(
        shards,
        mesh=mesh,
        in_specs=placed,
        out_specs=(P(None, "ens", "cell"), P(None, "ens", "cell")),
        check_vma=False,
    )
```

```python
import functools

import jax
import jax.numpy as jnp
from jax import lax
from jax.experimental import pallas as pl
from jax.experimental.pallas import tpu as pltpu
from jax.sharding import PartitionSpec as P

ITERS = 3

ALPHA_PRIOR = 0.5
BETA_TIME = 0.25
GAMMA_DEPTH = 0.25
STEP_SIZE = 0.05
DATA_GAIN = 1.0

SENT_SCALE = 1.0 / 32.0

CHUNK = 8
VMEM_BYTES = 24 * 1024 * 1024
SETUP_VMEM_BYTES = 60 * 1024 * 1024

SMEM = pl.BlockSpec(memory_space=pltpu.SMEM)
VMEM = pl.BlockSpec(memory_space=pltpu.VMEM)
ANY = pl.BlockSpec(memory_space=pl.ANY)
HBM = pl.BlockSpec(memory_space=pltpu.HBM)


class Order:
    def __init__(self, count, ray_blocks):
        self.owned = ray_blocks // count
        self.half_blocks = ray_blocks // 2

    def core(self):
        return lax.rem(lax.axis_index("cell"), 2)

    def place(self, core, q):
        owner = lax.div(q, self.owned)
        other_core = lax.rem(owner + core, 2)
        first = other_core * self.half_blocks + lax.div(owner, 2) * self.owned
        return first + lax.rem(q, self.owned)

    def survey(self, core, survey_ref, i):
        other_core, rest = divmod(i, self.half_blocks)
        chip, offset = divmod(rest, self.owned)
        owner = 2 * chip + (1 - core if other_core else core)
        return survey_ref[owner * self.owned + offset]


def forward(order, survey_ref, half_ref, dense_ref, own_ref, away_ref):
    core = order.core()
    half = own_ref.shape[0]
    for i in range(2 * half):
        travel = lax.dot_general(
            half_ref[order.survey(core, survey_ref, i)],
            dense_ref[i],
            (((1,), (1,)), ((), ())),
            preferred_element_type=jnp.float32,
        )
        if i < half:
            own_ref[i] = travel
        else:
            away_ref[i - half] = travel


def setup_kernel(
    order, count_ref, ray_hbm, cell_hbm, survey_hbm, members_hbm, blocks_hbm,
    dense_ref, half_ref, own_ref, away_ref,
    ray_ref, cell_ref, survey_ref, members_ref, staged, total, small_sems, sems,
):
    slots, rays, width = blocks_hbm.shape
    chunks = slots // CHUNK
    core = order.core()
    small = [
        pltpu.make_async_copy(source, target, small_sems.at[i])
        for i, (source, target) in enumerate(
            (
                (ray_hbm, ray_ref),
                (cell_hbm, cell_ref),
                (survey_hbm, survey_ref),
                (members_hbm, members_ref),
            )
        )
    ]
    large = []
    for i in range(chunks):
        part = pl.ds(i * CHUNK, CHUNK)
        large.append(pltpu.make_async_copy(blocks_hbm.at[part], staged.at[part], sems.at[i]))
    for copy in small + large:
        copy.start()
    total[...] = jnp.zeros_like(total)
    for copy in small:
        copy.wait()
    half_ref[...] = members_ref[...].astype(half_ref.dtype)
    count = count_ref[0]
    spare = dense_ref.shape[0]
    for i in range(chunks):
        large[i].wait()
        for k in range(i * CHUNK, (i + 1) * CHUNK):
            place = jnp.where(k < count, order.place(core, ray_ref[k]), spare)
            b = cell_ref[k]
            total[b, place] = total[b, place] + staged[k].astype(jnp.float32)
    for b in range(total.shape[0]):
        dense_ref[:, :, b * width : (b + 1) * width] = total[b, :spare].astype(dense_ref.dtype)
    forward(order, survey_ref, half_ref, dense_ref, own_ref, away_ref)


def misfit_kernel(travel_ref, observed_ref, noise_ref, out_ref):
    travel = travel_ref[...]
    spread = noise_ref[...][:, None, :]
    scaled = (travel - observed_ref[...]) / spread
    residual = DATA_GAIN * scaled / (spread * (1.0 + scaled * scaled))
    out_ref[...] = jnp.broadcast_to(residual.astype(out_ref.dtype)[None], out_ref.shape)


def regular_kernel(members_ref, prior_ref, chip_ref, link_ref, out_ref):
    surveys = members_ref.shape[0]
    for s in range(surveys):
        m = members_ref[s]
        value = ALPHA_PRIOR * (m - prior_ref[s])
        if s > 0:
            value = value + BETA_TIME * (m - members_ref[s - 1])
        if s < surveys - 1:
            value = value + BETA_TIME * (m - members_ref[s + 1])
        neighbours = chip_ref[s].astype(jnp.float32) + link_ref[s].astype(jnp.float32)
        out_ref[s] = value + GAMMA_DEPTH * (2.0 * m - neighbours)


def gradient_kernel(order, survey_ref, residual_ref, dense_ref, regular_ref, grad_ref):
    core = order.core()
    products = [
        jnp.dot(residual_ref[i], dense_ref[i], preferred_element_type=jnp.float32)
        for i in range(residual_ref.shape[0])
    ]
    grad_ref[...] = regular_ref[...]
    for i, product in enumerate(products):
        s = order.survey(core, survey_ref, i)
        grad_ref[s] = grad_ref[s] + product


def finish_gradient(order, survey_ref, residual_ref, dense_ref, partial_ref, grad):
    core = order.core()
    half = residual_ref.shape[0]
    products = [
        jnp.dot(residual_ref[i], dense_ref[half + i], preferred_element_type=jnp.float32)
        for i in range(half)
    ]
    grad[...] = partial_ref[...]
    for i, product in enumerate(products):
        s = order.survey(core, survey_ref, half + i)
        grad[s] = grad[s] + product


def step_kernel(
    order, survey_ref, residual_ref, dense_ref, partial_ref, members_ref,
    out_ref, half_ref, own_ref, away_ref,
    grad,
):
    finish_gradient(order, survey_ref, residual_ref, dense_ref, partial_ref, grad)
    updated = members_ref[...] - STEP_SIZE * grad[...]
    out_ref[...] = updated
    half_ref[...] = updated.astype(half_ref.dtype)
    forward(order, survey_ref, half_ref, dense_ref, own_ref, away_ref)


def last_kernel(
    order, survey_ref, residual_ref, dense_ref, partial_ref, members_ref,
    out_ref, gradient_ref,
    grad,
):
    finish_gradient(order, survey_ref, residual_ref, dense_ref, partial_ref, grad)
    out_ref[...] = members_ref[...] - STEP_SIZE * grad[...]
    gradient_ref[...] = grad[...].astype(gradient_ref.dtype)


def shards(
    prior_members, blocks, block_ray, block_cell, block_count, ray_survey, observed, noise_scale
):
    surveys, ensemble, cells_dev = prior_members.shape
    slots, rays, width = blocks.shape
    ray_blocks = ray_survey.shape[0]
    count = lax.axis_size("cell")
    order = Order(count, ray_blocks)
    owned, half_blocks = order.owned, order.half_blocks
    chips = count // 2
    params = pltpu.CompilerParams(vmem_limit_bytes=VMEM_BYTES)

    def bf16(*shape):
        return jax.ShapeDtypeStruct(shape, jnp.bfloat16)

    def f32(*shape):
        return jax.ShapeDtypeStruct(shape, jnp.float32)

    members_f32 = f32(surveys, ensemble, cells_dev)
    members_bf16 = bf16(surveys, ensemble, cells_dev)
    travels = (f32(half_blocks, ensemble, rays),) * 2

    in_hbm = [
        pltpu.with_memory_space_constraint(array, pltpu.HBM)
        for array in (block_ray, block_cell, ray_survey, prior_members, blocks)
    ]
    dense, half, own, away = pl.pallas_call(
        functools.partial(setup_kernel, order),
        out_shape=(bf16(ray_blocks, rays, cells_dev), members_bf16) + travels,
        in_specs=[SMEM] + [HBM] * 5,
        out_specs=(VMEM,) * 4,
        scratch_shapes=[
            pltpu.SMEM(block_ray.shape, jnp.int32),
            pltpu.SMEM(block_cell.shape, jnp.int32),
            pltpu.SMEM(ray_survey.shape, jnp.int32),
            pltpu.VMEM(prior_members.shape, jnp.float32),
            pltpu.VMEM(blocks.shape, blocks.dtype),
            pltpu.VMEM((cells_dev // width, ray_blocks + 1, rays, width), jnp.float32),
            pltpu.SemaphoreType.DMA((4,)),
            pltpu.SemaphoreType.DMA((slots // CHUNK,)),
        ],
        compiler_params=pltpu.CompilerParams(vmem_limit_bytes=VMEM_BYTES),
    )(block_count, *in_hbm)

    chip_pairs = [(i, i ^ 1) for i in range(count)]
    link_pairs = [pair for i in range(1, count - 1, 2) for pair in ((i, i + 1), (i + 1, i))]
    same_core = [list(range(core, count, 2)) for core in range(2)]

    def exchange(array):
        return lax.all_to_all(
            array, "cell", split_axis=0, concat_axis=0, axis_index_groups=same_core, tiled=True
        )

    members = prior_members
    for iteration in range(ITERS):
        received = lax.ppermute(away, "cell", chip_pairs)
        chip_halo = lax.ppermute(half, "cell", chip_pairs)
        received, chip_halo = lax.optimization_barrier((received, chip_halo))
        chip_travel = ((own + received) * SENT_SCALE).astype(jnp.float16)
        link_halo = lax.ppermute(half, "cell", link_pairs)
        parts = exchange(chip_travel)
        parts, moved_members = lax.optimization_barrier((parts, members))
        regular = pl.pallas_call(
            regular_kernel,
            out_shape=members_f32,
            in_specs=[VMEM] * 4,
            out_specs=VMEM,
            compiler_params=params,
        )(moved_members, prior_members, chip_halo, link_halo)
        parts, regular = lax.optimization_barrier((parts, regular))
        parts = parts.reshape(chips, owned, ensemble, rays).astype(jnp.float32)
        travel = jnp.sum(parts, axis=0) / SENT_SCALE
        copies = pl.pallas_call(
            misfit_kernel,
            out_shape=bf16(chips, owned, ensemble, rays),
            in_specs=[VMEM] * 3,
            out_specs=VMEM,
            compiler_params=params,
        )(travel, observed, noise_scale)
        residual = exchange(copies.reshape(half_blocks, ensemble, rays))
        other_residual = lax.ppermute(residual, "cell", chip_pairs)
        partial = pl.pallas_call(
            functools.partial(gradient_kernel, order),
            out_shape=members_f32,
            in_specs=[SMEM] + [VMEM] * 3,
            out_specs=VMEM,
            compiler_params=params,
        )(ray_survey, residual, dense, regular)
        last = iteration == ITERS - 1
        outputs = (members_f32, members_bf16) + (() if last else travels)
        results = pl.pallas_call(
            functools.partial(last_kernel if last else step_kernel, order),
            out_shape=outputs,
            in_specs=[SMEM] + [VMEM] * 4,
            out_specs=(VMEM,) * len(outputs),
            scratch_shapes=[pltpu.VMEM(prior_members.shape, jnp.float32)],
            compiler_params=params,
        )(ray_survey, other_residual, dense, partial, members)
        if last:
            return results
        members, half, own, away = results


def solution(mesh):
    placed = (
        P(None, "ens", "cell"),
        P("cell", None, None),
        P("cell"),
        P("cell"),
        P("cell"),
        P(),
        P("cell", "ens", None),
        P("cell", None),
    )
    return jax.shard_map(
        shards,
        mesh=mesh,
        in_specs=placed,
        out_specs=(P(None, "ens", "cell"), P(None, "ens", "cell")),
        check_vma=False,
    )
```

```python
import functools

import jax
import jax.numpy as jnp
from jax import lax
from jax.experimental import pallas as pl
from jax.experimental.pallas import tpu as pltpu
from jax.sharding import PartitionSpec as P

ITERS = 3

ALPHA_PRIOR = 0.5
BETA_TIME = 0.25
GAMMA_DEPTH = 0.25
STEP_SIZE = 0.05
DATA_GAIN = 1.0

SENT_SCALE = 1.0 / 32.0

CHUNK = 8
VMEM_BYTES = 24 * 1024 * 1024
SETUP_VMEM_BYTES = 60 * 1024 * 1024

SMEM = pl.BlockSpec(memory_space=pltpu.SMEM)
VMEM = pl.BlockSpec(memory_space=pltpu.VMEM)
ANY = pl.BlockSpec(memory_space=pl.ANY)
HBM = pl.BlockSpec(memory_space=pltpu.HBM)


class Order:
    def __init__(self, count, ray_blocks):
        self.owned = ray_blocks // count
        self.half_blocks = ray_blocks // 2

    def core(self):
        return lax.rem(lax.axis_index("cell"), 2)

    def place(self, core, q):
        owner = lax.div(q, self.owned)
        other_core = lax.rem(owner + core, 2)
        first = other_core * self.half_blocks + lax.div(owner, 2) * self.owned
        return first + lax.rem(q, self.owned)

    def survey(self, core, survey_ref, i):
        other_core, rest = divmod(i, self.half_blocks)
        chip, offset = divmod(rest, self.owned)
        owner = 2 * chip + (1 - core if other_core else core)
        return survey_ref[owner * self.owned + offset]


def forward(order, survey_ref, half_ref, dense_ref, own_ref, away_ref):
    core = order.core()
    half = own_ref.shape[0]
    for i in range(2 * half):
        travel = lax.dot_general(
            half_ref[order.survey(core, survey_ref, i)],
            dense_ref[i],
            (((1,), (1,)), ((), ())),
            preferred_element_type=jnp.float32,
        )
        if i < half:
            own_ref[i] = travel
        else:
            away_ref[i - half] = travel


def setup_kernel(
    order, count_ref, ray_hbm, cell_hbm, survey_hbm, members_hbm, blocks_hbm,
    dense_ref, half_ref, own_ref, away_ref,
    ray_ref, cell_ref, survey_ref, members_ref, staged, total, small_sems, sems,
):
    slots, rays, width = blocks_hbm.shape
    chunks = slots // CHUNK
    core = order.core()
    small = [
        pltpu.make_async_copy(source, target, small_sems.at[i])
        for i, (source, target) in enumerate(
            (
                (ray_hbm, ray_ref),
                (cell_hbm, cell_ref),
                (survey_hbm, survey_ref),
                (members_hbm, members_ref),
            )
        )
    ]
    large = []
    for i in range(chunks):
        part = pl.ds(i * CHUNK, CHUNK)
        large.append(pltpu.make_async_copy(blocks_hbm.at[part], staged.at[part], sems.at[i]))
    for copy in small + large:
        copy.start()
    total[...] = jnp.zeros_like(total)
    for copy in small:
        copy.wait()
    half_ref[...] = members_ref[...].astype(half_ref.dtype)
    count = count_ref[0]
    spare = dense_ref.shape[0]
    for i in range(chunks):
        large[i].wait()
        for k in range(i * CHUNK, (i + 1) * CHUNK):
            place = jnp.where(k < count, order.place(core, ray_ref[k]), spare)
            b = cell_ref[k]
            total[b, place] = total[b, place] + staged[k].astype(jnp.float32)
    for b in range(total.shape[0]):
        dense_ref[:, :, b * width : (b + 1) * width] = total[b, :spare].astype(dense_ref.dtype)
    forward(order, survey_ref, half_ref, dense_ref, own_ref, away_ref)


def misfit_kernel(travel_ref, observed_ref, noise_ref, out_ref):
    travel = travel_ref[...]
    spread = noise_ref[...][:, None, :]
    scaled = (travel - observed_ref[...]) / spread
    residual = DATA_GAIN * scaled / (spread * (1.0 + scaled * scaled))
    out_ref[...] = jnp.broadcast_to(residual.astype(out_ref.dtype)[None], out_ref.shape)


def gradient_kernel(
    order, survey_ref, residual_ref, dense_ref, members_ref, prior_ref, chip_ref, link_ref, grad_ref
):
    core = order.core()
    products = [
        jnp.dot(residual_ref[i], dense_ref[i], preferred_element_type=jnp.float32)
        for i in range(residual_ref.shape[0])
    ]
    surveys = members_ref.shape[0]
    for s in range(surveys):
        m = members_ref[s]
        value = ALPHA_PRIOR * (m - prior_ref[s])
        if s > 0:
            value = value + BETA_TIME * (m - members_ref[s - 1])
        if s < surveys - 1:
            value = value + BETA_TIME * (m - members_ref[s + 1])
        neighbours = chip_ref[s].astype(jnp.float32) + link_ref[s].astype(jnp.float32)
        grad_ref[s] = value + GAMMA_DEPTH * (2.0 * m - neighbours)
    for i, product in enumerate(products):
        s = order.survey(core, survey_ref, i)
        grad_ref[s] = grad_ref[s] + product


def finish_gradient(order, survey_ref, residual_ref, dense_ref, partial_ref, grad):
    core = order.core()
    half = residual_ref.shape[0]
    products = [
        jnp.dot(residual_ref[i], dense_ref[half + i], preferred_element_type=jnp.float32)
        for i in range(half)
    ]
    grad[...] = partial_ref[...]
    for i, product in enumerate(products):
        s = order.survey(core, survey_ref, half + i)
        grad[s] = grad[s] + product


def step_kernel(
    order, survey_ref, residual_ref, dense_ref, partial_ref, members_ref,
    out_ref, half_ref, own_ref, away_ref,
    grad,
):
    finish_gradient(order, survey_ref, residual_ref, dense_ref, partial_ref, grad)
    updated = members_ref[...] - STEP_SIZE * grad[...]
    out_ref[...] = updated
    half_ref[...] = updated.astype(half_ref.dtype)
    forward(order, survey_ref, half_ref, dense_ref, own_ref, away_ref)


def last_kernel(
    order, survey_ref, residual_ref, dense_ref, partial_ref, members_ref,
    out_hbm, gradient_hbm,
    grad, updated, rounded, sems,
):
    finish_gradient(order, survey_ref, residual_ref, dense_ref, partial_ref, grad)
    surveys = members_ref.shape[0]
    copies = []
    for s in range(surveys):
        updated[s] = members_ref[s] - STEP_SIZE * grad[s]
        rounded[s] = grad[s].astype(rounded.dtype)
        for i, (source, target) in enumerate(((updated, out_hbm), (rounded, gradient_hbm))):
            copies.append(pltpu.make_async_copy(source.at[s], target.at[s], sems.at[i, s]))
            copies[-1].start()
    for copy in copies:
        copy.wait()


def shards(
    prior_members, blocks, block_ray, block_cell, block_count, ray_survey, observed, noise_scale
):
    surveys, ensemble, cells_dev = prior_members.shape
    slots, rays, width = blocks.shape
    ray_blocks = ray_survey.shape[0]
    count = lax.axis_size("cell")
    order = Order(count, ray_blocks)
    owned, half_blocks = order.owned, order.half_blocks
    chips = count // 2
    params = pltpu.CompilerParams(vmem_limit_bytes=VMEM_BYTES)

    def bf16(*shape):
        return jax.ShapeDtypeStruct(shape, jnp.bfloat16)

    def f32(*shape):
        return jax.ShapeDtypeStruct(shape, jnp.float32)

    members_f32 = f32(surveys, ensemble, cells_dev)
    members_bf16 = bf16(surveys, ensemble, cells_dev)
    travels = (f32(half_blocks, ensemble, rays),) * 2

    in_hbm = [
        pltpu.with_memory_space_constraint(array, pltpu.HBM)
        for array in (block_ray, block_cell, ray_survey, prior_members, blocks)
    ]
    dense, half, own, away = pl.pallas_call(
        functools.partial(setup_kernel, order),
        out_shape=(bf16(ray_blocks, rays, cells_dev), members_bf16) + travels,
        in_specs=[SMEM] + [HBM] * 5,
        out_specs=(VMEM,) * 4,
        scratch_shapes=[
            pltpu.SMEM(block_ray.shape, jnp.int32),
            pltpu.SMEM(block_cell.shape, jnp.int32),
            pltpu.SMEM(ray_survey.shape, jnp.int32),
            pltpu.VMEM(prior_members.shape, jnp.float32),
            pltpu.VMEM(blocks.shape, blocks.dtype),
            pltpu.VMEM((cells_dev // width, ray_blocks + 1, rays, width), jnp.float32),
            pltpu.SemaphoreType.DMA((4,)),
            pltpu.SemaphoreType.DMA((slots // CHUNK,)),
        ],
        compiler_params=pltpu.CompilerParams(vmem_limit_bytes=VMEM_BYTES),
    )(block_count, *in_hbm)

    chip_pairs = [(i, i ^ 1) for i in range(count)]
    link_pairs = [pair for i in range(1, count - 1, 2) for pair in ((i, i + 1), (i + 1, i))]
    same_core = [list(range(core, count, 2)) for core in range(2)]

    def exchange(array):
        return lax.all_to_all(
            array, "cell", split_axis=0, concat_axis=0, axis_index_groups=same_core, tiled=True
        )

    last_scratch = [
        pltpu.VMEM(prior_members.shape, jnp.float32),
        pltpu.VMEM(prior_members.shape, jnp.bfloat16),
        pltpu.SemaphoreType.DMA((2, surveys)),
    ]
    members = prior_members
    for iteration in range(ITERS):
        received = lax.ppermute(away, "cell", chip_pairs)
        chip_halo = lax.ppermute(half, "cell", chip_pairs)
        received, chip_halo = lax.optimization_barrier((received, chip_halo))
        chip_travel = ((own + received) * SENT_SCALE).astype(jnp.float16)
        link_halo = lax.ppermute(half, "cell", link_pairs)
        parts = exchange(chip_travel)
        parts, link_halo = lax.optimization_barrier((parts, link_halo))
        parts = parts.reshape(chips, owned, ensemble, rays).astype(jnp.float32)
        travel = jnp.sum(parts, axis=0) / SENT_SCALE
        copies = pl.pallas_call(
            misfit_kernel,
            out_shape=bf16(chips, owned, ensemble, rays),
            in_specs=[VMEM] * 3,
            out_specs=VMEM,
            compiler_params=params,
        )(travel, observed, noise_scale)
        residual = exchange(copies.reshape(half_blocks, ensemble, rays))
        other_residual = lax.ppermute(residual, "cell", chip_pairs)
        partial = pl.pallas_call(
            functools.partial(gradient_kernel, order),
            out_shape=members_f32,
            in_specs=[SMEM] + [VMEM] * 6,
            out_specs=VMEM,
            compiler_params=params,
        )(ray_survey, residual, dense, members, prior_members, chip_halo, link_halo)
        last = iteration == ITERS - 1
        outputs = (members_f32, members_bf16) + (() if last else travels)
        results = pl.pallas_call(
            functools.partial(last_kernel if last else step_kernel, order),
            out_shape=outputs,
            in_specs=[SMEM] + [VMEM] * 4,
            out_specs=(HBM, HBM) if last else (VMEM,) * len(outputs),
            scratch_shapes=[pltpu.VMEM(prior_members.shape, jnp.float32)]
            + (last_scratch if last else []),
            compiler_params=params,
        )(ray_survey, other_residual, dense, partial, members)
        if last:
            return results
        members, half, own, away = results


def solution(mesh):
    placed = (
        P(None, "ens", "cell"),
        P("cell", None, None),
        P("cell"),
        P("cell"),
        P("cell"),
        P(),
        P("cell", "ens", None),
        P("cell", None),
    )
    return jax.shard_map(
        shards,
        mesh=mesh,
        in_specs=placed,
        out_specs=(P(None, "ens", "cell"), P(None, "ens", "cell")),
        check_vma=False,
    )
```

```python
import functools

import jax
import jax.numpy as jnp
from jax import lax
from jax.experimental import pallas as pl
from jax.experimental.pallas import tpu as pltpu
from jax.sharding import PartitionSpec as P

ITERS = 3

ALPHA_PRIOR = 0.5
BETA_TIME = 0.25
GAMMA_DEPTH = 0.25
STEP_SIZE = 0.05
DATA_GAIN = 1.0

SENT_SCALE = 1.0 / 32.0

CHUNK = 8
VMEM_BYTES = 24 * 1024 * 1024
SETUP_VMEM_BYTES = 60 * 1024 * 1024

SMEM = pl.BlockSpec(memory_space=pltpu.SMEM)
VMEM = pl.BlockSpec(memory_space=pltpu.VMEM)
ANY = pl.BlockSpec(memory_space=pl.ANY)
HBM = pl.BlockSpec(memory_space=pltpu.HBM)


class Order:
    def __init__(self, count, ray_blocks):
        self.owned = ray_blocks // count
        self.half_blocks = ray_blocks // 2

    def core(self):
        return lax.rem(lax.axis_index("cell"), 2)

    def place(self, core, q):
        owner = lax.div(q, self.owned)
        other_core = lax.rem(owner + core, 2)
        first = other_core * self.half_blocks + lax.div(owner, 2) * self.owned
        return first + lax.rem(q, self.owned)

    def survey(self, core, survey_ref, i):
        other_core, rest = divmod(i, self.half_blocks)
        chip, offset = divmod(rest, self.owned)
        owner = 2 * chip + (1 - core if other_core else core)
        return survey_ref[owner * self.owned + offset]


def forward(order, survey_ref, half_ref, dense_ref, own_ref, away_ref):
    core = order.core()
    half = own_ref.shape[0]
    for i in range(2 * half):
        travel = lax.dot_general(
            half_ref[order.survey(core, survey_ref, i)],
            dense_ref[i],
            (((1,), (1,)), ((), ())),
            preferred_element_type=jnp.float32,
        )
        if i < half:
            own_ref[i] = travel
        else:
            away_ref[i - half] = travel


def setup_kernel(
    order, count_ref, ray_hbm, cell_hbm, survey_hbm, members_hbm, blocks_hbm,
    dense_ref, half_ref, own_ref, away_ref,
    ray_ref, cell_ref, survey_ref, members_ref, staged, total, small_sems, sems,
):
    slots, rays, width = blocks_hbm.shape
    chunks = slots // CHUNK
    core = order.core()
    small = [
        pltpu.make_async_copy(source, target, small_sems.at[i])
        for i, (source, target) in enumerate(
            (
                (ray_hbm, ray_ref),
                (cell_hbm, cell_ref),
                (survey_hbm, survey_ref),
                (members_hbm, members_ref),
            )
        )
    ]
    large = []
    for i in range(chunks):
        part = pl.ds(i * CHUNK, CHUNK)
        large.append(pltpu.make_async_copy(blocks_hbm.at[part], staged.at[part], sems.at[i]))
    for copy in small + large:
        copy.start()
    total[...] = jnp.zeros_like(total)
    for copy in small:
        copy.wait()
    half_ref[...] = members_ref[...].astype(half_ref.dtype)
    count = count_ref[0]
    spare = dense_ref.shape[0]
    for i in range(chunks):
        large[i].wait()
        for k in range(i * CHUNK, (i + 1) * CHUNK):
            place = jnp.where(k < count, order.place(core, ray_ref[k]), spare)
            b = cell_ref[k]
            total[b, place] = total[b, place] + staged[k].astype(jnp.float32)
    for b in range(total.shape[0]):
        dense_ref[:, :, b * width : (b + 1) * width] = total[b, :spare].astype(dense_ref.dtype)
    forward(order, survey_ref, half_ref, dense_ref, own_ref, away_ref)


def misfit_kernel(travel_ref, observed_ref, noise_ref, halo_ref, out_ref):
    del halo_ref
    travel = travel_ref[...]
    spread = noise_ref[...][:, None, :]
    scaled = (travel - observed_ref[...]) / spread
    residual = DATA_GAIN * scaled / (spread * (1.0 + scaled * scaled))
    out_ref[...] = jnp.broadcast_to(residual.astype(out_ref.dtype)[None], out_ref.shape)


def gradient_kernel(
    order, survey_ref, residual_ref, dense_ref, members_ref, prior_ref, chip_ref, link_ref, grad_ref
):
    core = order.core()
    products = [
        jnp.dot(residual_ref[i], dense_ref[i], preferred_element_type=jnp.float32)
        for i in range(residual_ref.shape[0])
    ]
    surveys = members_ref.shape[0]
    for s in range(surveys):
        m = members_ref[s]
        value = ALPHA_PRIOR * (m - prior_ref[s])
        if s > 0:
            value = value + BETA_TIME * (m - members_ref[s - 1])
        if s < surveys - 1:
            value = value + BETA_TIME * (m - members_ref[s + 1])
        neighbours = chip_ref[s].astype(jnp.float32) + link_ref[s].astype(jnp.float32)
        grad_ref[s] = value + GAMMA_DEPTH * (2.0 * m - neighbours)
    for i, product in enumerate(products):
        s = order.survey(core, survey_ref, i)
        grad_ref[s] = grad_ref[s] + product


def finish_gradient(order, survey_ref, residual_ref, dense_ref, partial_ref, grad):
    core = order.core()
    half = residual_ref.shape[0]
    products = [
        jnp.dot(residual_ref[i], dense_ref[half + i], preferred_element_type=jnp.float32)
        for i in range(half)
    ]
    grad[...] = partial_ref[...]
    for i, product in enumerate(products):
        s = order.survey(core, survey_ref, half + i)
        grad[s] = grad[s] + product


def step_kernel(
    order, survey_ref, residual_ref, dense_ref, partial_ref, members_ref,
    out_ref, half_ref, own_ref, away_ref,
    grad,
):
    finish_gradient(order, survey_ref, residual_ref, dense_ref, partial_ref, grad)
    updated = members_ref[...] - STEP_SIZE * grad[...]
    out_ref[...] = updated
    half_ref[...] = updated.astype(half_ref.dtype)
    forward(order, survey_ref, half_ref, dense_ref, own_ref, away_ref)


def last_kernel(
    order, survey_ref, residual_ref, dense_ref, partial_ref, members_ref,
    out_ref, gradient_ref,
    grad,
):
    finish_gradient(order, survey_ref, residual_ref, dense_ref, partial_ref, grad)
    out_ref[...] = members_ref[...] - STEP_SIZE * grad[...]
    gradient_ref[...] = grad[...].astype(gradient_ref.dtype)


def shards(
    prior_members, blocks, block_ray, block_cell, block_count, ray_survey, observed, noise_scale
):
    surveys, ensemble, cells_dev = prior_members.shape
    slots, rays, width = blocks.shape
    ray_blocks = ray_survey.shape[0]
    count = lax.axis_size("cell")
    order = Order(count, ray_blocks)
    owned, half_blocks = order.owned, order.half_blocks
    chips = count // 2
    params = pltpu.CompilerParams(vmem_limit_bytes=VMEM_BYTES)

    def bf16(*shape):
        return jax.ShapeDtypeStruct(shape, jnp.bfloat16)

    def f32(*shape):
        return jax.ShapeDtypeStruct(shape, jnp.float32)

    members_f32 = f32(surveys, ensemble, cells_dev)
    members_bf16 = bf16(surveys, ensemble, cells_dev)
    travels = (f32(half_blocks, ensemble, rays),) * 2

    in_hbm = [
        pltpu.with_memory_space_constraint(array, pltpu.HBM)
        for array in (block_ray, block_cell, ray_survey, prior_members, blocks)
    ]
    dense, half, own, away = pl.pallas_call(
        functools.partial(setup_kernel, order),
        out_shape=(bf16(ray_blocks, rays, cells_dev), members_bf16) + travels,
        in_specs=[SMEM] + [HBM] * 5,
        out_specs=(VMEM,) * 4,
        scratch_shapes=[
            pltpu.SMEM(block_ray.shape, jnp.int32),
            pltpu.SMEM(block_cell.shape, jnp.int32),
            pltpu.SMEM(ray_survey.shape, jnp.int32),
            pltpu.VMEM(prior_members.shape, jnp.float32),
            pltpu.VMEM(blocks.shape, blocks.dtype),
            pltpu.VMEM((cells_dev // width, ray_blocks + 1, rays, width), jnp.float32),
            pltpu.SemaphoreType.DMA((4,)),
            pltpu.SemaphoreType.DMA((slots // CHUNK,)),
        ],
        compiler_params=pltpu.CompilerParams(vmem_limit_bytes=VMEM_BYTES),
    )(block_count, *in_hbm)

    chip_pairs = [(i, i ^ 1) for i in range(count)]
    link_pairs = [pair for i in range(1, count - 1, 2) for pair in ((i, i + 1), (i + 1, i))]
    same_core = [list(range(core, count, 2)) for core in range(2)]

    def exchange(array):
        return lax.all_to_all(
            array, "cell", split_axis=0, concat_axis=0, axis_index_groups=same_core, tiled=True
        )

    members = prior_members
    for iteration in range(ITERS):
        received = lax.ppermute(away, "cell", chip_pairs)
        chip_halo = lax.ppermute(half, "cell", chip_pairs)
        received, chip_halo = lax.optimization_barrier((received, chip_halo))
        chip_travel = ((own + received) * SENT_SCALE).astype(jnp.float16)
        link_halo = lax.ppermute(half, "cell", link_pairs)
        parts = exchange(chip_travel)
        parts = parts.reshape(chips, owned, ensemble, rays).astype(jnp.float32)
        travel = jnp.sum(parts, axis=0) / SENT_SCALE
        copies = pl.pallas_call(
            misfit_kernel,
            out_shape=bf16(chips, owned, ensemble, rays),
            in_specs=[VMEM] * 3 + [ANY],
            out_specs=VMEM,
            compiler_params=params,
        )(travel, observed, noise_scale, link_halo)
        residual = exchange(copies.reshape(half_blocks, ensemble, rays))
        other_residual = lax.ppermute(residual, "cell", chip_pairs)
        partial = pl.pallas_call(
            functools.partial(gradient_kernel, order),
            out_shape=members_f32,
            in_specs=[SMEM] + [VMEM] * 6,
            out_specs=VMEM,
            compiler_params=params,
        )(ray_survey, residual, dense, members, prior_members, chip_halo, link_halo)
        last = iteration == ITERS - 1
        outputs = (members_f32, members_bf16) + (() if last else travels)
        results = pl.pallas_call(
            functools.partial(last_kernel if last else step_kernel, order),
            out_shape=outputs,
            in_specs=[SMEM] + [VMEM] * 4,
            out_specs=(VMEM,) * len(outputs),
            scratch_shapes=[pltpu.VMEM(prior_members.shape, jnp.float32)],
            compiler_params=params,
        )(ray_survey, other_residual, dense, partial, members)
        if last:
            return results
        members, half, own, away = results


def solution(mesh):
    placed = (
        P(None, "ens", "cell"),
        P("cell", None, None),
        P("cell"),
        P("cell"),
        P("cell"),
        P(),
        P("cell", "ens", None),
        P("cell", None),
    )
    return jax.shard_map(
        shards,
        mesh=mesh,
        in_specs=placed,
        out_specs=(P(None, "ens", "cell"), P(None, "ens", "cell")),
        check_vma=False,
    )
```

```python
import functools

import jax
import jax.numpy as jnp
from jax import lax
from jax.experimental import pallas as pl
from jax.experimental.pallas import tpu as pltpu
from jax.sharding import PartitionSpec as P

ITERS = 3

ALPHA_PRIOR = 0.5
BETA_TIME = 0.25
GAMMA_DEPTH = 0.25
STEP_SIZE = 0.05
DATA_GAIN = 1.0

SENT_SCALE = 1.0 / 32.0

CHUNK = 8
VMEM_BYTES = 24 * 1024 * 1024
SETUP_VMEM_BYTES = 60 * 1024 * 1024

SMEM = pl.BlockSpec(memory_space=pltpu.SMEM)
VMEM = pl.BlockSpec(memory_space=pltpu.VMEM)
ANY = pl.BlockSpec(memory_space=pl.ANY)
HBM = pl.BlockSpec(memory_space=pltpu.HBM)


class Order:
    def __init__(self, count, ray_blocks):
        self.owned = ray_blocks // count
        self.half_blocks = ray_blocks // 2

    def core(self):
        return lax.rem(lax.axis_index("cell"), 2)

    def place(self, core, q):
        owner = lax.div(q, self.owned)
        other_core = lax.rem(owner + core, 2)
        first = other_core * self.half_blocks + lax.div(owner, 2) * self.owned
        return first + lax.rem(q, self.owned)

    def survey(self, core, survey_ref, i):
        other_core, rest = divmod(i, self.half_blocks)
        chip, offset = divmod(rest, self.owned)
        owner = 2 * chip + (1 - core if other_core else core)
        return survey_ref[owner * self.owned + offset]


def forward(order, survey_ref, half_ref, dense_ref, own_ref, away_ref):
    core = order.core()
    half = own_ref.shape[0]
    for i in range(2 * half):
        travel = lax.dot_general(
            half_ref[order.survey(core, survey_ref, i)],
            dense_ref[i],
            (((1,), (1,)), ((), ())),
            preferred_element_type=jnp.float32,
        )
        if i < half:
            own_ref[i] = travel
        else:
            away_ref[i - half] = travel


def setup_kernel(
    order, count_ref, ray_hbm, cell_hbm, survey_hbm, members_hbm, blocks_hbm,
    dense_ref, half_ref, own_ref, away_ref,
    ray_ref, cell_ref, survey_ref, members_ref, staged, total, small_sems, sems,
):
    slots, rays, width = blocks_hbm.shape
    chunks = slots // CHUNK
    core = order.core()
    small = [
        pltpu.make_async_copy(source, target, small_sems.at[i])
        for i, (source, target) in enumerate(
            (
                (ray_hbm, ray_ref),
                (cell_hbm, cell_ref),
                (survey_hbm, survey_ref),
                (members_hbm, members_ref),
            )
        )
    ]
    large = []
    for i in range(chunks):
        part = pl.ds(i * CHUNK, CHUNK)
        large.append(pltpu.make_async_copy(blocks_hbm.at[part], staged.at[part], sems.at[i]))
    for copy in small + large:
        copy.start()
    total[...] = jnp.zeros_like(total)
    for copy in small:
        copy.wait()
    half_ref[...] = members_ref[...].astype(half_ref.dtype)
    count = count_ref[0]
    spare = dense_ref.shape[0]
    for i in range(chunks):
        large[i].wait()
        for k in range(i * CHUNK, (i + 1) * CHUNK):
            place = jnp.where(k < count, order.place(core, ray_ref[k]), spare)
            b = cell_ref[k]
            total[b, place] = total[b, place] + staged[k].astype(jnp.float32)
    for b in range(total.shape[0]):
        dense_ref[:, :, b * width : (b + 1) * width] = total[b, :spare].astype(dense_ref.dtype)
    forward(order, survey_ref, half_ref, dense_ref, own_ref, away_ref)


def misfit_kernel(travel_ref, observed_ref, noise_ref, token_ref, out_ref):
    del token_ref
    travel = travel_ref[...]
    spread = noise_ref[...][:, None, :]
    scaled = (travel - observed_ref[...]) / spread
    residual = DATA_GAIN * scaled / (spread * (1.0 + scaled * scaled))
    out_ref[...] = jnp.broadcast_to(residual.astype(out_ref.dtype)[None], out_ref.shape)


def arrival_kernel(observed_ref, halo_ref, token_ref):
    del observed_ref, halo_ref
    token_ref[...] = jnp.zeros_like(token_ref)


def gradient_kernel(
    order, survey_ref, residual_ref, dense_ref, members_ref, prior_ref, chip_ref, link_ref, grad_ref
):
    core = order.core()
    products = [
        jnp.dot(residual_ref[i], dense_ref[i], preferred_element_type=jnp.float32)
        for i in range(residual_ref.shape[0])
    ]
    surveys = members_ref.shape[0]
    for s in range(surveys):
        m = members_ref[s]
        value = ALPHA_PRIOR * (m - prior_ref[s])
        if s > 0:
            value = value + BETA_TIME * (m - members_ref[s - 1])
        if s < surveys - 1:
            value = value + BETA_TIME * (m - members_ref[s + 1])
        neighbours = chip_ref[s].astype(jnp.float32) + link_ref[s].astype(jnp.float32)
        grad_ref[s] = value + GAMMA_DEPTH * (2.0 * m - neighbours)
    for i, product in enumerate(products):
        s = order.survey(core, survey_ref, i)
        grad_ref[s] = grad_ref[s] + product


def finish_gradient(order, survey_ref, residual_ref, dense_ref, partial_ref, grad):
    core = order.core()
    half = residual_ref.shape[0]
    products = [
        jnp.dot(residual_ref[i], dense_ref[half + i], preferred_element_type=jnp.float32)
        for i in range(half)
    ]
    grad[...] = partial_ref[...]
    for i, product in enumerate(products):
        s = order.survey(core, survey_ref, half + i)
        grad[s] = grad[s] + product


def step_kernel(
    order, survey_ref, residual_ref, dense_ref, partial_ref, members_ref,
    out_ref, half_ref, own_ref, away_ref,
    grad,
):
    finish_gradient(order, survey_ref, residual_ref, dense_ref, partial_ref, grad)
    updated = members_ref[...] - STEP_SIZE * grad[...]
    out_ref[...] = updated
    half_ref[...] = updated.astype(half_ref.dtype)
    forward(order, survey_ref, half_ref, dense_ref, own_ref, away_ref)


def last_kernel(
    order, survey_ref, residual_ref, dense_ref, partial_ref, members_ref,
    out_ref, gradient_ref,
    grad,
):
    finish_gradient(order, survey_ref, residual_ref, dense_ref, partial_ref, grad)
    out_ref[...] = members_ref[...] - STEP_SIZE * grad[...]
    gradient_ref[...] = grad[...].astype(gradient_ref.dtype)


def shards(
    prior_members, blocks, block_ray, block_cell, block_count, ray_survey, observed, noise_scale
):
    surveys, ensemble, cells_dev = prior_members.shape
    slots, rays, width = blocks.shape
    ray_blocks = ray_survey.shape[0]
    count = lax.axis_size("cell")
    order = Order(count, ray_blocks)
    owned, half_blocks = order.owned, order.half_blocks
    chips = count // 2
    params = pltpu.CompilerParams(vmem_limit_bytes=VMEM_BYTES)

    def bf16(*shape):
        return jax.ShapeDtypeStruct(shape, jnp.bfloat16)

    def f32(*shape):
        return jax.ShapeDtypeStruct(shape, jnp.float32)

    members_f32 = f32(surveys, ensemble, cells_dev)
    members_bf16 = bf16(surveys, ensemble, cells_dev)
    travels = (f32(half_blocks, ensemble, rays),) * 2

    in_hbm = [
        pltpu.with_memory_space_constraint(array, pltpu.HBM)
        for array in (block_ray, block_cell, ray_survey, prior_members, blocks)
    ]
    dense, half, own, away = pl.pallas_call(
        functools.partial(setup_kernel, order),
        out_shape=(bf16(ray_blocks, rays, cells_dev), members_bf16) + travels,
        in_specs=[SMEM] + [HBM] * 5,
        out_specs=(VMEM,) * 4,
        scratch_shapes=[
            pltpu.SMEM(block_ray.shape, jnp.int32),
            pltpu.SMEM(block_cell.shape, jnp.int32),
            pltpu.SMEM(ray_survey.shape, jnp.int32),
            pltpu.VMEM(prior_members.shape, jnp.float32),
            pltpu.VMEM(blocks.shape, blocks.dtype),
            pltpu.VMEM((cells_dev // width, ray_blocks + 1, rays, width), jnp.float32),
            pltpu.SemaphoreType.DMA((4,)),
            pltpu.SemaphoreType.DMA((slots // CHUNK,)),
        ],
        compiler_params=pltpu.CompilerParams(vmem_limit_bytes=VMEM_BYTES),
    )(block_count, *in_hbm)

    chip_pairs = [(i, i ^ 1) for i in range(count)]
    link_pairs = [pair for i in range(1, count - 1, 2) for pair in ((i, i + 1), (i + 1, i))]
    same_core = [list(range(core, count, 2)) for core in range(2)]

    def exchange(array):
        return lax.all_to_all(
            array, "cell", split_axis=0, concat_axis=0, axis_index_groups=same_core, tiled=True
        )

    members = prior_members
    for iteration in range(ITERS):
        received = lax.ppermute(away, "cell", chip_pairs)
        chip_halo = lax.ppermute(half, "cell", chip_pairs)
        received, chip_halo = lax.optimization_barrier((received, chip_halo))
        chip_travel = ((own + received) * SENT_SCALE).astype(jnp.float16)
        link_halo = lax.ppermute(half, "cell", link_pairs)
        parts = exchange(chip_travel)
        parts, after_parts = lax.optimization_barrier((parts, observed))
        token = pl.pallas_call(
            arrival_kernel,
            out_shape=f32(8, 128),
            in_specs=[ANY] * 2,
            out_specs=VMEM,
            compiler_params=params,
        )(after_parts, link_halo)
        parts, token = lax.optimization_barrier((parts, token))
        parts = parts.reshape(chips, owned, ensemble, rays).astype(jnp.float32)
        travel = jnp.sum(parts, axis=0) / SENT_SCALE
        copies = pl.pallas_call(
            misfit_kernel,
            out_shape=bf16(chips, owned, ensemble, rays),
            in_specs=[VMEM] * 3 + [ANY],
            out_specs=VMEM,
            compiler_params=params,
        )(travel, observed, noise_scale, token)
        residual = exchange(copies.reshape(half_blocks, ensemble, rays))
        other_residual = lax.ppermute(residual, "cell", chip_pairs)
        partial = pl.pallas_call(
            functools.partial(gradient_kernel, order),
            out_shape=members_f32,
            in_specs=[SMEM] + [VMEM] * 6,
            out_specs=VMEM,
            compiler_params=params,
        )(ray_survey, residual, dense, members, prior_members, chip_halo, link_halo)
        last = iteration == ITERS - 1
        outputs = (members_f32, members_bf16) + (() if last else travels)
        results = pl.pallas_call(
            functools.partial(last_kernel if last else step_kernel, order),
            out_shape=outputs,
            in_specs=[SMEM] + [VMEM] * 4,
            out_specs=(VMEM,) * len(outputs),
            scratch_shapes=[pltpu.VMEM(prior_members.shape, jnp.float32)],
            compiler_params=params,
        )(ray_survey, other_residual, dense, partial, members)
        if last:
            return results
        members, half, own, away = results


def solution(mesh):
    placed = (
        P(None, "ens", "cell"),
        P("cell", None, None),
        P("cell"),
        P("cell"),
        P("cell"),
        P(),
        P("cell", "ens", None),
        P("cell", None),
    )
    return jax.shard_map(
        shards,
        mesh=mesh,
        in_specs=placed,
        out_specs=(P(None, "ens", "cell"), P(None, "ens", "cell")),
        check_vma=False,
    )
```

```python
import functools

import jax
import jax.numpy as jnp
from jax import lax
from jax.experimental import pallas as pl
from jax.experimental.pallas import tpu as pltpu
from jax.sharding import PartitionSpec as P

ITERS = 3

ALPHA_PRIOR = 0.5
BETA_TIME = 0.25
GAMMA_DEPTH = 0.25
STEP_SIZE = 0.05
DATA_GAIN = 1.0

SENT_SCALE = 1.0 / 32.0

CHUNK = 8
VMEM_BYTES = 24 * 1024 * 1024
SETUP_VMEM_BYTES = 60 * 1024 * 1024

SMEM = pl.BlockSpec(memory_space=pltpu.SMEM)
VMEM = pl.BlockSpec(memory_space=pltpu.VMEM)
ANY = pl.BlockSpec(memory_space=pl.ANY)
HBM = pl.BlockSpec(memory_space=pltpu.HBM)


class Order:
    def __init__(self, count, ray_blocks):
        self.owned = ray_blocks // count
        self.half_blocks = ray_blocks // 2

    def core(self):
        return lax.rem(lax.axis_index("cell"), 2)

    def place(self, core, q):
        owner = lax.div(q, self.owned)
        other_core = lax.rem(owner + core, 2)
        first = other_core * self.half_blocks + lax.div(owner, 2) * self.owned
        return first + lax.rem(q, self.owned)

    def survey(self, core, survey_ref, i):
        other_core, rest = divmod(i, self.half_blocks)
        chip, offset = divmod(rest, self.owned)
        owner = 2 * chip + (1 - core if other_core else core)
        return survey_ref[owner * self.owned + offset]


def forward(order, survey_ref, half_ref, dense_ref, own_ref, away_ref):
    core = order.core()
    half = own_ref.shape[0]
    for i in range(2 * half):
        travel = lax.dot_general(
            half_ref[order.survey(core, survey_ref, i)],
            dense_ref[i],
            (((1,), (1,)), ((), ())),
            preferred_element_type=jnp.float32,
        )
        if i < half:
            own_ref[i] = travel
        else:
            away_ref[i - half] = travel


def setup_kernel(
    order, count_ref, ray_hbm, cell_hbm, survey_hbm, members_hbm, blocks_hbm,
    dense_ref, half_ref, own_ref, away_ref,
    ray_ref, cell_ref, survey_ref, members_ref, staged, upper, lower, small_sems, sems,
):
    slots, rays, width = blocks_hbm.shape
    chunks = slots // CHUNK
    core = order.core()
    small = [
        pltpu.make_async_copy(source, target, small_sems.at[i])
        for i, (source, target) in enumerate(
            (
                (ray_hbm, ray_ref),
                (cell_hbm, cell_ref),
                (survey_hbm, survey_ref),
                (members_hbm, members_ref),
            )
        )
    ]
    large = []
    for i in range(chunks):
        part = pl.ds(i * CHUNK, CHUNK)
        large.append(pltpu.make_async_copy(blocks_hbm.at[part], staged.at[part], sems.at[i]))
    for copy in small + large:
        copy.start()
    upper[...] = jnp.zeros_like(upper)
    lower[...] = jnp.zeros_like(lower)
    middle = rays // 2
    for copy in small:
        copy.wait()
    half_ref[...] = members_ref[...].astype(half_ref.dtype)
    count = count_ref[0]
    spare = dense_ref.shape[0]
    for i in range(chunks):
        large[i].wait()
        for k in range(i * CHUNK, (i + 1) * CHUNK):
            place = jnp.where(k < count, order.place(core, ray_ref[k]), spare)
            b = cell_ref[k]
            upper[b, place] = upper[b, place] + staged[k, :middle].astype(jnp.float32)
            lower[b, place] = lower[b, place] + staged[k, middle:].astype(jnp.float32)
    for b in range(upper.shape[0]):
        cells = slice(b * width, (b + 1) * width)
        dense_ref[:, :middle, cells] = upper[b, :spare].astype(dense_ref.dtype)
        dense_ref[:, middle:, cells] = lower[b, :spare].astype(dense_ref.dtype)
    forward(order, survey_ref, half_ref, dense_ref, own_ref, away_ref)


def misfit_kernel(travel_ref, observed_ref, noise_ref, token_ref, out_ref):
    del token_ref
    travel = travel_ref[...]
    spread = noise_ref[...][:, None, :]
    scaled = (travel - observed_ref[...]) / spread
    residual = DATA_GAIN * scaled / (spread * (1.0 + scaled * scaled))
    out_ref[...] = jnp.broadcast_to(residual.astype(out_ref.dtype)[None], out_ref.shape)


def arrival_kernel(observed_ref, halo_ref, token_ref):
    del observed_ref, halo_ref
    token_ref[...] = jnp.zeros_like(token_ref)


def add_products(order, survey_ref, low, products, upper, lower):
    core = order.core()
    middle = upper.shape[1]
    for i, product in enumerate(products):
        s = order.survey(core, survey_ref, low + i)
        upper[s] = upper[s] + product[:middle]
        lower[s] = lower[s] + product[middle:]


def gradient_kernel(
    order, survey_ref, residual_ref, dense_ref, members_ref, prior_ref, chip_ref, link_ref,
    upper, lower,
):
    products = [
        jnp.dot(residual_ref[i], dense_ref[i], preferred_element_type=jnp.float32)
        for i in range(residual_ref.shape[0])
    ]
    surveys = members_ref.shape[0]
    middle = upper.shape[1]
    for s in range(surveys):
        m = members_ref[s]
        value = ALPHA_PRIOR * (m - prior_ref[s])
        if s > 0:
            value = value + BETA_TIME * (m - members_ref[s - 1])
        if s < surveys - 1:
            value = value + BETA_TIME * (m - members_ref[s + 1])
        neighbours = chip_ref[s].astype(jnp.float32) + link_ref[s].astype(jnp.float32)
        value = value + GAMMA_DEPTH * (2.0 * m - neighbours)
        upper[s] = value[:middle]
        lower[s] = value[middle:]
    add_products(order, survey_ref, 0, products, upper, lower)


def finish_gradient(
    order, survey_ref, residual_ref, dense_ref, upper_ref, lower_ref, upper, lower
):
    half = residual_ref.shape[0]
    products = [
        jnp.dot(residual_ref[i], dense_ref[half + i], preferred_element_type=jnp.float32)
        for i in range(half)
    ]
    upper[...] = upper_ref[...]
    lower[...] = lower_ref[...]
    add_products(order, survey_ref, half, products, upper, lower)


def step_kernel(
    order, survey_ref, residual_ref, dense_ref, upper_ref, lower_ref, members_ref,
    out_ref, half_ref, own_ref, away_ref,
    upper, lower,
):
    finish_gradient(order, survey_ref, residual_ref, dense_ref, upper_ref, lower_ref, upper, lower)
    middle = upper.shape[1]
    for rows, grad in ((slice(0, middle), upper), (slice(middle, None), lower)):
        updated = members_ref[:, rows] - STEP_SIZE * grad[...]
        out_ref[:, rows] = updated
        half_ref[:, rows] = updated.astype(half_ref.dtype)
    forward(order, survey_ref, half_ref, dense_ref, own_ref, away_ref)


def last_kernel(
    order, survey_ref, residual_ref, dense_ref, upper_ref, lower_ref, members_ref,
    out_ref, gradient_ref,
    upper, lower,
):
    finish_gradient(order, survey_ref, residual_ref, dense_ref, upper_ref, lower_ref, upper, lower)
    middle = upper.shape[1]
    for rows, grad in ((slice(0, middle), upper), (slice(middle, None), lower)):
        out_ref[:, rows] = members_ref[:, rows] - STEP_SIZE * grad[...]
        gradient_ref[:, rows] = grad[...].astype(gradient_ref.dtype)


def shards(
    prior_members, blocks, block_ray, block_cell, block_count, ray_survey, observed, noise_scale
):
    surveys, ensemble, cells_dev = prior_members.shape
    slots, rays, width = blocks.shape
    ray_blocks = ray_survey.shape[0]
    count = lax.axis_size("cell")
    order = Order(count, ray_blocks)
    owned, half_blocks = order.owned, order.half_blocks
    chips = count // 2
    params = pltpu.CompilerParams(vmem_limit_bytes=VMEM_BYTES)

    def bf16(*shape):
        return jax.ShapeDtypeStruct(shape, jnp.bfloat16)

    def f32(*shape):
        return jax.ShapeDtypeStruct(shape, jnp.float32)

    members_f32 = f32(surveys, ensemble, cells_dev)
    part_f32 = f32(surveys, ensemble // 2, cells_dev)
    members_bf16 = bf16(surveys, ensemble, cells_dev)
    travels = (f32(half_blocks, ensemble, rays),) * 2

    in_hbm = [
        pltpu.with_memory_space_constraint(array, pltpu.HBM)
        for array in (block_ray, block_cell, ray_survey, prior_members, blocks)
    ]
    dense, half, own, away = pl.pallas_call(
        functools.partial(setup_kernel, order),
        out_shape=(bf16(ray_blocks, rays, cells_dev), members_bf16) + travels,
        in_specs=[SMEM] + [HBM] * 5,
        out_specs=(VMEM,) * 4,
        scratch_shapes=[
            pltpu.SMEM(block_ray.shape, jnp.int32),
            pltpu.SMEM(block_cell.shape, jnp.int32),
            pltpu.SMEM(ray_survey.shape, jnp.int32),
            pltpu.VMEM(prior_members.shape, jnp.float32),
            pltpu.VMEM(blocks.shape, blocks.dtype),
            pltpu.VMEM((cells_dev // width, ray_blocks + 1, rays // 2, width), jnp.float32),
            pltpu.VMEM((cells_dev // width, ray_blocks + 1, rays // 2, width), jnp.float32),
            pltpu.SemaphoreType.DMA((4,)),
            pltpu.SemaphoreType.DMA((slots // CHUNK,)),
        ],
        compiler_params=pltpu.CompilerParams(vmem_limit_bytes=VMEM_BYTES),
    )(block_count, *in_hbm)

    chip_pairs = [(i, i ^ 1) for i in range(count)]
    link_pairs = [pair for i in range(1, count - 1, 2) for pair in ((i, i + 1), (i + 1, i))]
    same_core = [list(range(core, count, 2)) for core in range(2)]

    def exchange(array):
        return lax.all_to_all(
            array, "cell", split_axis=0, concat_axis=0, axis_index_groups=same_core, tiled=True
        )

    members = prior_members
    for iteration in range(ITERS):
        received = lax.ppermute(away, "cell", chip_pairs)
        chip_halo = lax.ppermute(half, "cell", chip_pairs)
        received, chip_halo = lax.optimization_barrier((received, chip_halo))
        chip_travel = ((own + received) * SENT_SCALE).astype(jnp.float16)
        link_halo = lax.ppermute(half, "cell", link_pairs)
        parts = exchange(chip_travel)
        parts, after_parts = lax.optimization_barrier((parts, observed))
        token = pl.pallas_call(
            arrival_kernel,
            out_shape=f32(8, 128),
            in_specs=[ANY] * 2,
            out_specs=VMEM,
            compiler_params=params,
        )(after_parts, link_halo)
        parts, token = lax.optimization_barrier((parts, token))
        parts = parts.reshape(chips, owned, ensemble, rays).astype(jnp.float32)
        travel = jnp.sum(parts, axis=0) / SENT_SCALE
        copies = pl.pallas_call(
            misfit_kernel,
            out_shape=bf16(chips, owned, ensemble, rays),
            in_specs=[VMEM] * 3 + [ANY],
            out_specs=VMEM,
            compiler_params=params,
        )(travel, observed, noise_scale, token)
        residual = exchange(copies.reshape(half_blocks, ensemble, rays))
        other_residual = lax.ppermute(residual, "cell", chip_pairs)
        partial = pl.pallas_call(
            functools.partial(gradient_kernel, order),
            out_shape=(part_f32, part_f32),
            in_specs=[SMEM] + [VMEM] * 6,
            out_specs=(VMEM, VMEM),
            compiler_params=params,
        )(ray_survey, residual, dense, members, prior_members, chip_halo, link_halo)
        last = iteration == ITERS - 1
        outputs = (members_f32, members_bf16) + (() if last else travels)
        results = pl.pallas_call(
            functools.partial(last_kernel if last else step_kernel, order),
            out_shape=outputs,
            in_specs=[SMEM] + [VMEM] * 5,
            out_specs=(VMEM,) * len(outputs),
            scratch_shapes=[pltpu.VMEM(part_f32.shape, jnp.float32)] * 2,
            compiler_params=params,
        )(ray_survey, other_residual, dense, *partial, members)
        if last:
            return results
        members, half, own, away = results


def solution(mesh):
    placed = (
        P(None, "ens", "cell"),
        P("cell", None, None),
        P("cell"),
        P("cell"),
        P("cell"),
        P(),
        P("cell", "ens", None),
        P("cell", None),
    )
    return jax.shard_map(
        shards,
        mesh=mesh,
        in_specs=placed,
        out_specs=(P(None, "ens", "cell"), P(None, "ens", "cell")),
        check_vma=False,
    )
```

```python
import functools

import jax
import jax.numpy as jnp
from jax import lax
from jax.experimental import pallas as pl
from jax.experimental.pallas import tpu as pltpu
from jax.sharding import PartitionSpec as P

ITERS = 3

ALPHA_PRIOR = 0.5
BETA_TIME = 0.25
GAMMA_DEPTH = 0.25
STEP_SIZE = 0.05
DATA_GAIN = 1.0

SENT_SCALE = 1.0 / 32.0

CHUNK = 8
VMEM_BYTES = 24 * 1024 * 1024
SETUP_VMEM_BYTES = 60 * 1024 * 1024

SMEM = pl.BlockSpec(memory_space=pltpu.SMEM)
VMEM = pl.BlockSpec(memory_space=pltpu.VMEM)
ANY = pl.BlockSpec(memory_space=pl.ANY)
HBM = pl.BlockSpec(memory_space=pltpu.HBM)


class Order:
    def __init__(self, count, ray_blocks):
        self.owned = ray_blocks // count
        self.half_blocks = ray_blocks // 2
        self.upper = count // 4
        self.ring = [chip + side * self.upper for chip in range(self.upper) for side in range(2)]

    def core(self):
        return lax.rem(lax.axis_index("cell"), 2)

    def place(self, core, q):
        owner = lax.div(q, self.owned)
        other_core = lax.rem(owner + core, 2)
        chip = lax.div(owner, 2)
        position = 2 * lax.rem(chip, self.upper) + lax.div(chip, self.upper)
        return other_core * self.half_blocks + position * self.owned + lax.rem(q, self.owned)

    def survey(self, core, survey_ref, i):
        other_core, rest = divmod(i, self.half_blocks)
        position, offset = divmod(rest, self.owned)
        owner = 2 * self.ring[position] + (1 - core if other_core else core)
        return survey_ref[owner * self.owned + offset]


def forward(order, survey_ref, half_ref, dense_ref, own_ref, away_ref):
    core = order.core()
    half = own_ref.shape[0]
    for i in range(2 * half):
        travel = lax.dot_general(
            half_ref[order.survey(core, survey_ref, i)],
            dense_ref[i],
            (((1,), (1,)), ((), ())),
            preferred_element_type=jnp.float32,
        )
        if i < half:
            own_ref[i] = travel
        else:
            away_ref[i - half] = travel


def setup_kernel(
    order, count_ref, ray_hbm, cell_hbm, survey_hbm, members_hbm, blocks_hbm,
    dense_ref, half_ref, own_ref, away_ref,
    ray_ref, cell_ref, survey_ref, members_ref, staged, total, small_sems, sems,
):
    slots, rays, width = blocks_hbm.shape
    chunks = slots // CHUNK
    core = order.core()
    small = [
        pltpu.make_async_copy(source, target, small_sems.at[i])
        for i, (source, target) in enumerate(
            (
                (ray_hbm, ray_ref),
                (cell_hbm, cell_ref),
                (survey_hbm, survey_ref),
                (members_hbm, members_ref),
            )
        )
    ]
    large = []
    for i in range(chunks):
        part = pl.ds(i * CHUNK, CHUNK)
        large.append(pltpu.make_async_copy(blocks_hbm.at[part], staged.at[part], sems.at[i]))
    for copy in small + large:
        copy.start()
    total[...] = jnp.zeros_like(total)
    for copy in small:
        copy.wait()
    half_ref[...] = members_ref[...].astype(half_ref.dtype)
    count = count_ref[0]
    spare = dense_ref.shape[0]
    for i in range(chunks):
        large[i].wait()
        for k in range(i * CHUNK, (i + 1) * CHUNK):
            place = jnp.where(k < count, order.place(core, ray_ref[k]), spare)
            b = cell_ref[k]
            total[b, place] = total[b, place] + staged[k].astype(jnp.float32)
    for b in range(total.shape[0]):
        dense_ref[:, :, b * width : (b + 1) * width] = total[b, :spare].astype(dense_ref.dtype)
    forward(order, survey_ref, half_ref, dense_ref, own_ref, away_ref)


def misfit_kernel(travel_ref, observed_ref, noise_ref, token_ref, out_ref):
    del token_ref
    travel = travel_ref[...]
    spread = noise_ref[...][:, None, :]
    scaled = (travel - observed_ref[...]) / spread
    residual = DATA_GAIN * scaled / (spread * (1.0 + scaled * scaled))
    out_ref[...] = jnp.broadcast_to(residual.astype(out_ref.dtype)[None], out_ref.shape)


def arrival_kernel(observed_ref, halo_ref, token_ref):
    del observed_ref, halo_ref
    token_ref[...] = jnp.zeros_like(token_ref)


def gradient_kernel(
    order, survey_ref, residual_ref, dense_ref, members_ref, prior_ref, chip_ref, link_ref, grad_ref
):
    core = order.core()
    products = [
        jnp.dot(residual_ref[i], dense_ref[i], preferred_element_type=jnp.float32)
        for i in range(residual_ref.shape[0])
    ]
    surveys = members_ref.shape[0]
    for s in range(surveys):
        m = members_ref[s]
        value = ALPHA_PRIOR * (m - prior_ref[s])
        if s > 0:
            value = value + BETA_TIME * (m - members_ref[s - 1])
        if s < surveys - 1:
            value = value + BETA_TIME * (m - members_ref[s + 1])
        neighbours = chip_ref[s].astype(jnp.float32) + link_ref[s].astype(jnp.float32)
        grad_ref[s] = value + GAMMA_DEPTH * (2.0 * m - neighbours)
    for i, product in enumerate(products):
        s = order.survey(core, survey_ref, i)
        grad_ref[s] = grad_ref[s] + product


def finish_gradient(order, survey_ref, residual_ref, dense_ref, partial_ref, grad):
    core = order.core()
    half = residual_ref.shape[0]
    products = [
        jnp.dot(residual_ref[i], dense_ref[half + i], preferred_element_type=jnp.float32)
        for i in range(half)
    ]
    grad[...] = partial_ref[...]
    for i, product in enumerate(products):
        s = order.survey(core, survey_ref, half + i)
        grad[s] = grad[s] + product


def step_kernel(
    order, survey_ref, residual_ref, dense_ref, partial_ref, members_ref,
    out_ref, half_ref, own_ref, away_ref,
    grad,
):
    finish_gradient(order, survey_ref, residual_ref, dense_ref, partial_ref, grad)
    updated = members_ref[...] - STEP_SIZE * grad[...]
    out_ref[...] = updated
    half_ref[...] = updated.astype(half_ref.dtype)
    forward(order, survey_ref, half_ref, dense_ref, own_ref, away_ref)


def last_kernel(
    order, survey_ref, residual_ref, dense_ref, partial_ref, members_ref,
    out_ref, gradient_ref,
    grad,
):
    finish_gradient(order, survey_ref, residual_ref, dense_ref, partial_ref, grad)
    out_ref[...] = members_ref[...] - STEP_SIZE * grad[...]
    gradient_ref[...] = grad[...].astype(gradient_ref.dtype)


def shards(
    prior_members, blocks, block_ray, block_cell, block_count, ray_survey, observed, noise_scale
):
    surveys, ensemble, cells_dev = prior_members.shape
    slots, rays, width = blocks.shape
    ray_blocks = ray_survey.shape[0]
    count = lax.axis_size("cell")
    order = Order(count, ray_blocks)
    owned, half_blocks = order.owned, order.half_blocks
    chips = count // 2
    params = pltpu.CompilerParams(vmem_limit_bytes=VMEM_BYTES)

    def bf16(*shape):
        return jax.ShapeDtypeStruct(shape, jnp.bfloat16)

    def f32(*shape):
        return jax.ShapeDtypeStruct(shape, jnp.float32)

    members_f32 = f32(surveys, ensemble, cells_dev)
    members_bf16 = bf16(surveys, ensemble, cells_dev)
    travels = (f32(half_blocks, ensemble, rays),) * 2

    in_hbm = [
        pltpu.with_memory_space_constraint(array, pltpu.HBM)
        for array in (block_ray, block_cell, ray_survey, prior_members, blocks)
    ]
    dense, half, own, away = pl.pallas_call(
        functools.partial(setup_kernel, order),
        out_shape=(bf16(ray_blocks, rays, cells_dev), members_bf16) + travels,
        in_specs=[SMEM] + [HBM] * 5,
        out_specs=(VMEM,) * 4,
        scratch_shapes=[
            pltpu.SMEM(block_ray.shape, jnp.int32),
            pltpu.SMEM(block_cell.shape, jnp.int32),
            pltpu.SMEM(ray_survey.shape, jnp.int32),
            pltpu.VMEM(prior_members.shape, jnp.float32),
            pltpu.VMEM(blocks.shape, blocks.dtype),
            pltpu.VMEM((cells_dev // width, ray_blocks + 1, rays, width), jnp.float32),
            pltpu.SemaphoreType.DMA((4,)),
            pltpu.SemaphoreType.DMA((slots // CHUNK,)),
        ],
        compiler_params=pltpu.CompilerParams(vmem_limit_bytes=VMEM_BYTES),
    )(block_count, *in_hbm)

    chip_pairs = [(i, i ^ 1) for i in range(count)]
    link_pairs = [pair for i in range(1, count - 1, 2) for pair in ((i, i + 1), (i + 1, i))]
    same_core = [[2 * chip + core for chip in order.ring] for core in range(2)]

    def exchange(array):
        return lax.all_to_all(
            array, "cell", split_axis=0, concat_axis=0, axis_index_groups=same_core, tiled=True
        )

    members = prior_members
    for iteration in range(ITERS):
        received = lax.ppermute(away, "cell", chip_pairs)
        chip_halo = lax.ppermute(half, "cell", chip_pairs)
        received, chip_halo = lax.optimization_barrier((received, chip_halo))
        chip_travel = ((own + received) * SENT_SCALE).astype(jnp.float16)
        link_halo = lax.ppermute(half, "cell", link_pairs)
        parts = exchange(chip_travel)
        parts, after_parts = lax.optimization_barrier((parts, observed))
        token = pl.pallas_call(
            arrival_kernel,
            out_shape=f32(8, 128),
            in_specs=[ANY] * 2,
            out_specs=VMEM,
            compiler_params=params,
        )(after_parts, link_halo)
        parts, token = lax.optimization_barrier((parts, token))
        parts = parts.reshape(chips, owned, ensemble, rays).astype(jnp.float32)
        travel = jnp.sum(parts, axis=0) / SENT_SCALE
        copies = pl.pallas_call(
            misfit_kernel,
            out_shape=bf16(chips, owned, ensemble, rays),
            in_specs=[VMEM] * 3 + [ANY],
            out_specs=VMEM,
            compiler_params=params,
        )(travel, observed, noise_scale, token)
        residual = exchange(copies.reshape(half_blocks, ensemble, rays))
        other_residual = lax.ppermute(residual, "cell", chip_pairs)
        partial = pl.pallas_call(
            functools.partial(gradient_kernel, order),
            out_shape=members_f32,
            in_specs=[SMEM] + [VMEM] * 6,
            out_specs=VMEM,
            compiler_params=params,
        )(ray_survey, residual, dense, members, prior_members, chip_halo, link_halo)
        last = iteration == ITERS - 1
        outputs = (members_f32, members_bf16) + (() if last else travels)
        results = pl.pallas_call(
            functools.partial(last_kernel if last else step_kernel, order),
            out_shape=outputs,
            in_specs=[SMEM] + [VMEM] * 4,
            out_specs=(VMEM,) * len(outputs),
            scratch_shapes=[pltpu.VMEM(prior_members.shape, jnp.float32)],
            compiler_params=params,
        )(ray_survey, other_residual, dense, partial, members)
        if last:
            return results
        members, half, own, away = results


def solution(mesh):
    placed = (
        P(None, "ens", "cell"),
        P("cell", None, None),
        P("cell"),
        P("cell"),
        P("cell"),
        P(),
        P("cell", "ens", None),
        P("cell", None),
    )
    return jax.shard_map(
        shards,
        mesh=mesh,
        in_specs=placed,
        out_specs=(P(None, "ens", "cell"), P(None, "ens", "cell")),
        check_vma=False,
    )
```

```python
import functools

import jax
import jax.numpy as jnp
from jax import lax
from jax.experimental import pallas as pl
from jax.experimental.pallas import tpu as pltpu
from jax.sharding import PartitionSpec as P

ITERS = 3

ALPHA_PRIOR = 0.5
BETA_TIME = 0.25
GAMMA_DEPTH = 0.25
STEP_SIZE = 0.05
DATA_GAIN = 1.0

SENT_SCALE = 1.0 / 32.0

CHUNK = 8
VMEM_BYTES = 24 * 1024 * 1024
SETUP_VMEM_BYTES = 60 * 1024 * 1024

SMEM = pl.BlockSpec(memory_space=pltpu.SMEM)
VMEM = pl.BlockSpec(memory_space=pltpu.VMEM)
ANY = pl.BlockSpec(memory_space=pl.ANY)
HBM = pl.BlockSpec(memory_space=pltpu.HBM)


class Order:
    def __init__(self, count, ray_blocks):
        self.owned = ray_blocks // count
        self.half_blocks = ray_blocks // 2
        self.upper = count // 4
        self.ring = [chip + side * self.upper for chip in range(self.upper) for side in range(2)]

    def core(self):
        return lax.rem(lax.axis_index("cell"), 2)

    def place(self, core, q):
        owner, offset = (q, 0) if self.owned == 1 else (lax.div(q, self.owned), lax.rem(q, self.owned))
        other_core = (owner ^ core) & 1
        chip = owner >> 1
        upper = (chip >= self.upper).astype(jnp.int32)
        position = 2 * chip - upper * (2 * self.upper - 1)
        return other_core * self.half_blocks + position * self.owned + offset

    def survey(self, core, survey_ref, i):
        other_core, rest = divmod(i, self.half_blocks)
        position, offset = divmod(rest, self.owned)
        owner = 2 * self.ring[position] + (1 - core if other_core else core)
        return survey_ref[owner * self.owned + offset]


def forward(order, survey_ref, half_ref, dense_ref, own_ref, away_ref):
    core = order.core()
    half = own_ref.shape[0]
    for i in range(2 * half):
        travel = lax.dot_general(
            half_ref[order.survey(core, survey_ref, i)],
            dense_ref[i],
            (((1,), (1,)), ((), ())),
            preferred_element_type=jnp.float32,
        )
        if i < half:
            own_ref[i] = travel
        else:
            away_ref[i - half] = travel


def setup_kernel(
    order, count_ref, ray_hbm, cell_hbm, survey_hbm, members_hbm, blocks_hbm,
    dense_ref, half_ref, own_ref, away_ref,
    ray_ref, cell_ref, survey_ref, members_ref, staged, total, small_sems, sems,
):
    slots, rays, width = blocks_hbm.shape
    chunks = slots // CHUNK
    core = order.core()
    small = [
        pltpu.make_async_copy(source, target, small_sems.at[i])
        for i, (source, target) in enumerate(
            (
                (ray_hbm, ray_ref),
                (cell_hbm, cell_ref),
                (survey_hbm, survey_ref),
                (members_hbm, members_ref),
            )
        )
    ]
    large = []
    for i in range(chunks):
        part = pl.ds(i * CHUNK, CHUNK)
        large.append(pltpu.make_async_copy(blocks_hbm.at[part], staged.at[part], sems.at[i]))
    for copy in small + large:
        copy.start()
    total[...] = jnp.zeros_like(total)
    for copy in small:
        copy.wait()
    half_ref[...] = members_ref[...].astype(half_ref.dtype)
    count = count_ref[0]
    spare = dense_ref.shape[0]
    targets = [
        (cell_ref[k], jnp.where(k < count, order.place(core, ray_ref[k]), spare)) for k in range(slots)
    ]
    for i in range(chunks):
        large[i].wait()
        for k in range(i * CHUNK, (i + 1) * CHUNK):
            total[targets[k]] = total[targets[k]] + staged[k].astype(jnp.float32)
    for b in range(total.shape[0]):
        dense_ref[:, :, b * width : (b + 1) * width] = total[b, :spare].astype(dense_ref.dtype)
    forward(order, survey_ref, half_ref, dense_ref, own_ref, away_ref)


def misfit_kernel(travel_ref, observed_ref, noise_ref, token_ref, out_ref):
    del token_ref
    travel = travel_ref[...]
    spread = noise_ref[...][:, None, :]
    scaled = (travel - observed_ref[...]) / spread
    residual = DATA_GAIN * scaled / (spread * (1.0 + scaled * scaled))
    out_ref[...] = jnp.broadcast_to(residual.astype(out_ref.dtype)[None], out_ref.shape)


def arrival_kernel(observed_ref, halo_ref, token_ref):
    del observed_ref, halo_ref
    token_ref[...] = jnp.zeros_like(token_ref)


def gradient_kernel(
    order, survey_ref, residual_ref, dense_ref, members_ref, prior_ref, chip_ref, link_ref, grad_ref
):
    core = order.core()
    products = [
        jnp.dot(residual_ref[i], dense_ref[i], preferred_element_type=jnp.float32)
        for i in range(residual_ref.shape[0])
    ]
    surveys = members_ref.shape[0]
    for s in range(surveys):
        m = members_ref[s]
        value = ALPHA_PRIOR * (m - prior_ref[s])
        if s > 0:
            value = value + BETA_TIME * (m - members_ref[s - 1])
        if s < surveys - 1:
            value = value + BETA_TIME * (m - members_ref[s + 1])
        neighbours = chip_ref[s].astype(jnp.float32) + link_ref[s].astype(jnp.float32)
        grad_ref[s] = value + GAMMA_DEPTH * (2.0 * m - neighbours)
    for i, product in enumerate(products):
        s = order.survey(core, survey_ref, i)
        grad_ref[s] = grad_ref[s] + product


def finish_gradient(order, survey_ref, residual_ref, dense_ref, partial_ref, grad):
    core = order.core()
    half = residual_ref.shape[0]
    products = [
        jnp.dot(residual_ref[i], dense_ref[half + i], preferred_element_type=jnp.float32)
        for i in range(half)
    ]
    grad[...] = partial_ref[...]
    for i, product in enumerate(products):
        s = order.survey(core, survey_ref, half + i)
        grad[s] = grad[s] + product


def step_kernel(
    order, survey_ref, residual_ref, dense_ref, partial_ref, members_ref,
    out_ref, half_ref, own_ref, away_ref,
    grad,
):
    finish_gradient(order, survey_ref, residual_ref, dense_ref, partial_ref, grad)
    updated = members_ref[...] - STEP_SIZE * grad[...]
    out_ref[...] = updated
    half_ref[...] = updated.astype(half_ref.dtype)
    forward(order, survey_ref, half_ref, dense_ref, own_ref, away_ref)


def last_kernel(
    order, survey_ref, residual_ref, dense_ref, partial_ref, members_ref,
    out_ref, gradient_ref,
    grad,
):
    finish_gradient(order, survey_ref, residual_ref, dense_ref, partial_ref, grad)
    out_ref[...] = members_ref[...] - STEP_SIZE * grad[...]
    gradient_ref[...] = grad[...].astype(gradient_ref.dtype)


def shards(
    prior_members, blocks, block_ray, block_cell, block_count, ray_survey, observed, noise_scale
):
    surveys, ensemble, cells_dev = prior_members.shape
    slots, rays, width = blocks.shape
    ray_blocks = ray_survey.shape[0]
    count = lax.axis_size("cell")
    order = Order(count, ray_blocks)
    owned, half_blocks = order.owned, order.half_blocks
    chips = count // 2
    params = pltpu.CompilerParams(vmem_limit_bytes=VMEM_BYTES)

    def bf16(*shape):
        return jax.ShapeDtypeStruct(shape, jnp.bfloat16)

    def f32(*shape):
        return jax.ShapeDtypeStruct(shape, jnp.float32)

    members_f32 = f32(surveys, ensemble, cells_dev)
    members_bf16 = bf16(surveys, ensemble, cells_dev)
    travels = (f32(half_blocks, ensemble, rays),) * 2

    in_hbm = [
        pltpu.with_memory_space_constraint(array, pltpu.HBM)
        for array in (block_ray, block_cell, ray_survey, prior_members, blocks)
    ]
    dense, half, own, away = pl.pallas_call(
        functools.partial(setup_kernel, order),
        out_shape=(bf16(ray_blocks, rays, cells_dev), members_bf16) + travels,
        in_specs=[SMEM] + [HBM] * 5,
        out_specs=(VMEM,) * 4,
        scratch_shapes=[
            pltpu.SMEM(block_ray.shape, jnp.int32),
            pltpu.SMEM(block_cell.shape, jnp.int32),
            pltpu.SMEM(ray_survey.shape, jnp.int32),
            pltpu.VMEM(prior_members.shape, jnp.float32),
            pltpu.VMEM(blocks.shape, blocks.dtype),
            pltpu.VMEM((cells_dev // width, ray_blocks + 1, rays, width), jnp.float32),
            pltpu.SemaphoreType.DMA((4,)),
            pltpu.SemaphoreType.DMA((slots // CHUNK,)),
        ],
        compiler_params=pltpu.CompilerParams(vmem_limit_bytes=VMEM_BYTES),
    )(block_count, *in_hbm)

    chip_pairs = [(i, i ^ 1) for i in range(count)]
    link_pairs = [pair for i in range(1, count - 1, 2) for pair in ((i, i + 1), (i + 1, i))]
    same_core = [[2 * chip + core for chip in order.ring] for core in range(2)]

    def exchange(array):
        return lax.all_to_all(
            array, "cell", split_axis=0, concat_axis=0, axis_index_groups=same_core, tiled=True
        )

    members = prior_members
    for iteration in range(ITERS):
        received = lax.ppermute(away, "cell", chip_pairs)
        chip_halo = lax.ppermute(half, "cell", chip_pairs)
        received, chip_halo = lax.optimization_barrier((received, chip_halo))
        chip_travel = ((own + received) * SENT_SCALE).astype(jnp.float16)
        link_halo = lax.ppermute(half, "cell", link_pairs)
        parts = exchange(chip_travel)
        parts, after_parts = lax.optimization_barrier((parts, observed))
        token = pl.pallas_call(
            arrival_kernel,
            out_shape=f32(8, 128),
            in_specs=[ANY] * 2,
            out_specs=VMEM,
            compiler_params=params,
        )(after_parts, link_halo)
        parts, token = lax.optimization_barrier((parts, token))
        parts = parts.reshape(chips, owned, ensemble, rays).astype(jnp.float32)
        travel = jnp.sum(parts, axis=0) / SENT_SCALE
        copies = pl.pallas_call(
            misfit_kernel,
            out_shape=bf16(chips, owned, ensemble, rays),
            in_specs=[VMEM] * 3 + [ANY],
            out_specs=VMEM,
            compiler_params=params,
        )(travel, observed, noise_scale, token)
        residual = exchange(copies.reshape(half_blocks, ensemble, rays))
        other_residual = lax.ppermute(residual, "cell", chip_pairs)
        partial = pl.pallas_call(
            functools.partial(gradient_kernel, order),
            out_shape=members_f32,
            in_specs=[SMEM] + [VMEM] * 6,
            out_specs=VMEM,
            compiler_params=params,
        )(ray_survey, residual, dense, members, prior_members, chip_halo, link_halo)
        last = iteration == ITERS - 1
        outputs = (members_f32, members_bf16) + (() if last else travels)
        results = pl.pallas_call(
            functools.partial(last_kernel if last else step_kernel, order),
            out_shape=outputs,
            in_specs=[SMEM] + [VMEM] * 4,
            out_specs=(VMEM,) * len(outputs),
            scratch_shapes=[pltpu.VMEM(prior_members.shape, jnp.float32)],
            compiler_params=params,
        )(ray_survey, other_residual, dense, partial, members)
        if last:
            return results
        members, half, own, away = results


def solution(mesh):
    placed = (
        P(None, "ens", "cell"),
        P("cell", None, None),
        P("cell"),
        P("cell"),
        P("cell"),
        P(),
        P("cell", "ens", None),
        P("cell", None),
    )
    return jax.shard_map(
        shards,
        mesh=mesh,
        in_specs=placed,
        out_specs=(P(None, "ens", "cell"), P(None, "ens", "cell")),
        check_vma=False,
    )
```

```python
import functools

import jax
import jax.numpy as jnp
from jax import lax
from jax.experimental import pallas as pl
from jax.experimental.pallas import tpu as pltpu
from jax.sharding import PartitionSpec as P

ITERS = 3

ALPHA_PRIOR = 0.5
BETA_TIME = 0.25
GAMMA_DEPTH = 0.25
STEP_SIZE = 0.05
DATA_GAIN = 1.0

SENT_SCALE = 1.0 / 32.0

CHUNK = 8
VMEM_BYTES = 24 * 1024 * 1024
SETUP_VMEM_BYTES = 60 * 1024 * 1024

SMEM = pl.BlockSpec(memory_space=pltpu.SMEM)
VMEM = pl.BlockSpec(memory_space=pltpu.VMEM)
ANY = pl.BlockSpec(memory_space=pl.ANY)
HBM = pl.BlockSpec(memory_space=pltpu.HBM)


class Order:
    def __init__(self, count, ray_blocks):
        self.owned = ray_blocks // count
        self.half_blocks = ray_blocks // 2
        self.upper = count // 4
        self.rings = (
            [chip + side * self.upper for chip in range(self.upper) for side in range(2)],
            list(range(count // 2)),
        )

    def core(self):
        return lax.rem(lax.axis_index("cell"), 2)

    def place(self, core, q):
        owner = lax.div(q, self.owned)
        owner_core = lax.rem(owner, 2)
        other_core = lax.rem(owner + core, 2)
        chip = lax.div(owner, 2)
        alternating = 2 * lax.rem(chip, self.upper) + lax.div(chip, self.upper)
        position = jnp.where(owner_core == 0, alternating, chip)
        return other_core * self.half_blocks + position * self.owned + lax.rem(q, self.owned)

    def survey(self, core, survey_ref, i):
        other_core, rest = divmod(i, self.half_blocks)
        position, offset = divmod(rest, self.owned)
        owner_core = 1 - core if other_core else core
        chip = jnp.where(owner_core == 0, self.rings[0][position], self.rings[1][position])
        return survey_ref[(2 * chip + owner_core) * self.owned + offset]


def forward(order, survey_ref, half_ref, dense_ref, own_ref, away_ref):
    core = order.core()
    half = own_ref.shape[0]
    for i in range(2 * half):
        travel = lax.dot_general(
            half_ref[order.survey(core, survey_ref, i)],
            dense_ref[i],
            (((1,), (1,)), ((), ())),
            preferred_element_type=jnp.float32,
        )
        if i < half:
            own_ref[i] = travel
        else:
            away_ref[i - half] = travel


def setup_kernel(
    order, count_ref, ray_hbm, cell_hbm, survey_hbm, members_hbm, blocks_hbm,
    dense_ref, half_ref, own_ref, away_ref,
    ray_ref, cell_ref, survey_ref, members_ref, staged, total, small_sems, sems,
):
    slots, rays, width = blocks_hbm.shape
    chunks = slots // CHUNK
    core = order.core()
    small = [
        pltpu.make_async_copy(source, target, small_sems.at[i])
        for i, (source, target) in enumerate(
            (
                (ray_hbm, ray_ref),
                (cell_hbm, cell_ref),
                (survey_hbm, survey_ref),
                (members_hbm, members_ref),
            )
        )
    ]
    large = []
    for i in range(chunks):
        part = pl.ds(i * CHUNK, CHUNK)
        large.append(pltpu.make_async_copy(blocks_hbm.at[part], staged.at[part], sems.at[i]))
    for copy in small + large:
        copy.start()
    total[...] = jnp.zeros_like(total)
    for copy in small:
        copy.wait()
    half_ref[...] = members_ref[...].astype(half_ref.dtype)
    count = count_ref[0]
    spare = dense_ref.shape[0]
    for i in range(chunks):
        large[i].wait()
        for k in range(i * CHUNK, (i + 1) * CHUNK):
            place = jnp.where(k < count, order.place(core, ray_ref[k]), spare)
            b = cell_ref[k]
            total[b, place] = total[b, place] + staged[k].astype(jnp.float32)
    for b in range(total.shape[0]):
        dense_ref[:, :, b * width : (b + 1) * width] = total[b, :spare].astype(dense_ref.dtype)
    forward(order, survey_ref, half_ref, dense_ref, own_ref, away_ref)


def misfit_kernel(travel_ref, observed_ref, noise_ref, token_ref, out_ref):
    del token_ref
    travel = travel_ref[...]
    spread = noise_ref[...][:, None, :]
    scaled = (travel - observed_ref[...]) / spread
    residual = DATA_GAIN * scaled / (spread * (1.0 + scaled * scaled))
    out_ref[...] = jnp.broadcast_to(residual.astype(out_ref.dtype)[None], out_ref.shape)


def arrival_kernel(observed_ref, halo_ref, token_ref):
    del observed_ref, halo_ref
    token_ref[...] = jnp.zeros_like(token_ref)


def gradient_kernel(
    order, survey_ref, residual_ref, dense_ref, members_ref, prior_ref, chip_ref, link_ref, grad_ref
):
    core = order.core()
    products = [
        jnp.dot(residual_ref[i], dense_ref[i], preferred_element_type=jnp.float32)
        for i in range(residual_ref.shape[0])
    ]
    surveys = members_ref.shape[0]
    for s in range(surveys):
        m = members_ref[s]
        value = ALPHA_PRIOR * (m - prior_ref[s])
        if s > 0:
            value = value + BETA_TIME * (m - members_ref[s - 1])
        if s < surveys - 1:
            value = value + BETA_TIME * (m - members_ref[s + 1])
        neighbours = chip_ref[s].astype(jnp.float32) + link_ref[s].astype(jnp.float32)
        grad_ref[s] = value + GAMMA_DEPTH * (2.0 * m - neighbours)
    for i, product in enumerate(products):
        s = order.survey(core, survey_ref, i)
        grad_ref[s] = grad_ref[s] + product


def finish_gradient(order, survey_ref, residual_ref, dense_ref, partial_ref, grad):
    core = order.core()
    half = residual_ref.shape[0]
    products = [
        jnp.dot(residual_ref[i], dense_ref[half + i], preferred_element_type=jnp.float32)
        for i in range(half)
    ]
    grad[...] = partial_ref[...]
    for i, product in enumerate(products):
        s = order.survey(core, survey_ref, half + i)
        grad[s] = grad[s] + product


def step_kernel(
    order, survey_ref, residual_ref, dense_ref, partial_ref, members_ref,
    out_ref, half_ref, own_ref, away_ref,
    grad,
):
    finish_gradient(order, survey_ref, residual_ref, dense_ref, partial_ref, grad)
    updated = members_ref[...] - STEP_SIZE * grad[...]
    out_ref[...] = updated
    half_ref[...] = updated.astype(half_ref.dtype)
    forward(order, survey_ref, half_ref, dense_ref, own_ref, away_ref)


def last_kernel(
    order, survey_ref, residual_ref, dense_ref, partial_ref, members_ref,
    out_ref, gradient_ref,
    grad,
):
    finish_gradient(order, survey_ref, residual_ref, dense_ref, partial_ref, grad)
    out_ref[...] = members_ref[...] - STEP_SIZE * grad[...]
    gradient_ref[...] = grad[...].astype(gradient_ref.dtype)


def shards(
    prior_members, blocks, block_ray, block_cell, block_count, ray_survey, observed, noise_scale
):
    surveys, ensemble, cells_dev = prior_members.shape
    slots, rays, width = blocks.shape
    ray_blocks = ray_survey.shape[0]
    count = lax.axis_size("cell")
    order = Order(count, ray_blocks)
    owned, half_blocks = order.owned, order.half_blocks
    chips = count // 2
    params = pltpu.CompilerParams(vmem_limit_bytes=VMEM_BYTES)

    def bf16(*shape):
        return jax.ShapeDtypeStruct(shape, jnp.bfloat16)

    def f32(*shape):
        return jax.ShapeDtypeStruct(shape, jnp.float32)

    members_f32 = f32(surveys, ensemble, cells_dev)
    members_bf16 = bf16(surveys, ensemble, cells_dev)
    travels = (f32(half_blocks, ensemble, rays),) * 2

    in_hbm = [
        pltpu.with_memory_space_constraint(array, pltpu.HBM)
        for array in (block_ray, block_cell, ray_survey, prior_members, blocks)
    ]
    dense, half, own, away = pl.pallas_call(
        functools.partial(setup_kernel, order),
        out_shape=(bf16(ray_blocks, rays, cells_dev), members_bf16) + travels,
        in_specs=[SMEM] + [HBM] * 5,
        out_specs=(VMEM,) * 4,
        scratch_shapes=[
            pltpu.SMEM(block_ray.shape, jnp.int32),
            pltpu.SMEM(block_cell.shape, jnp.int32),
            pltpu.SMEM(ray_survey.shape, jnp.int32),
            pltpu.VMEM(prior_members.shape, jnp.float32),
            pltpu.VMEM(blocks.shape, blocks.dtype),
            pltpu.VMEM((cells_dev // width, ray_blocks + 1, rays, width), jnp.float32),
            pltpu.SemaphoreType.DMA((4,)),
            pltpu.SemaphoreType.DMA((slots // CHUNK,)),
        ],
        compiler_params=pltpu.CompilerParams(vmem_limit_bytes=VMEM_BYTES),
    )(block_count, *in_hbm)

    chip_pairs = [(i, i ^ 1) for i in range(count)]
    link_pairs = [pair for i in range(1, count - 1, 2) for pair in ((i, i + 1), (i + 1, i))]
    same_core = [[2 * chip + core for chip in ring] for core, ring in enumerate(order.rings)]

    def exchange(array):
        return lax.all_to_all(
            array, "cell", split_axis=0, concat_axis=0, axis_index_groups=same_core, tiled=True
        )

    members = prior_members
    for iteration in range(ITERS):
        received = lax.ppermute(away, "cell", chip_pairs)
        chip_halo = lax.ppermute(half, "cell", chip_pairs)
        received, chip_halo = lax.optimization_barrier((received, chip_halo))
        chip_travel = ((own + received) * SENT_SCALE).astype(jnp.float16)
        link_halo = lax.ppermute(half, "cell", link_pairs)
        parts = exchange(chip_travel)
        parts, after_parts = lax.optimization_barrier((parts, observed))
        token = pl.pallas_call(
            arrival_kernel,
            out_shape=f32(8, 128),
            in_specs=[ANY] * 2,
            out_specs=VMEM,
            compiler_params=params,
        )(after_parts, link_halo)
        parts, token = lax.optimization_barrier((parts, token))
        parts = parts.reshape(chips, owned, ensemble, rays).astype(jnp.float32)
        travel = jnp.sum(parts, axis=0) / SENT_SCALE
        copies = pl.pallas_call(
            misfit_kernel,
            out_shape=bf16(chips, owned, ensemble, rays),
            in_specs=[VMEM] * 3 + [ANY],
            out_specs=VMEM,
            compiler_params=params,
        )(travel, observed, noise_scale, token)
        residual = exchange(copies.reshape(half_blocks, ensemble, rays))
        other_residual = lax.ppermute(residual, "cell", chip_pairs)
        partial = pl.pallas_call(
            functools.partial(gradient_kernel, order),
            out_shape=members_f32,
            in_specs=[SMEM] + [VMEM] * 6,
            out_specs=VMEM,
            compiler_params=params,
        )(ray_survey, residual, dense, members, prior_members, chip_halo, link_halo)
        last = iteration == ITERS - 1
        outputs = (members_f32, members_bf16) + (() if last else travels)
        results = pl.pallas_call(
            functools.partial(last_kernel if last else step_kernel, order),
            out_shape=outputs,
            in_specs=[SMEM] + [VMEM] * 4,
            out_specs=(VMEM,) * len(outputs),
            scratch_shapes=[pltpu.VMEM(prior_members.shape, jnp.float32)],
            compiler_params=params,
        )(ray_survey, other_residual, dense, partial, members)
        if last:
            return results
        members, half, own, away = results


def solution(mesh):
    placed = (
        P(None, "ens", "cell"),
        P("cell", None, None),
        P("cell"),
        P("cell"),
        P("cell"),
        P(),
        P("cell", "ens", None),
        P("cell", None),
    )
    return jax.shard_map(
        shards,
        mesh=mesh,
        in_specs=placed,
        out_specs=(P(None, "ens", "cell"), P(None, "ens", "cell")),
        check_vma=False,
    )
```

```python
import functools

import jax
import jax.numpy as jnp
from jax import lax
from jax.experimental import pallas as pl
from jax.experimental.pallas import tpu as pltpu
from jax.sharding import PartitionSpec as P

ITERS = 3

ALPHA_PRIOR = 0.5
BETA_TIME = 0.25
GAMMA_DEPTH = 0.25
STEP_SIZE = 0.05
DATA_GAIN = 1.0

SENT_SCALE = 1.0 / 32.0

CHUNK = 8
VMEM_BYTES = 24 * 1024 * 1024
SETUP_VMEM_BYTES = 60 * 1024 * 1024

SMEM = pl.BlockSpec(memory_space=pltpu.SMEM)
VMEM = pl.BlockSpec(memory_space=pltpu.VMEM)
ANY = pl.BlockSpec(memory_space=pl.ANY)
HBM = pl.BlockSpec(memory_space=pltpu.HBM)


class Order:
    def __init__(self, count, ray_blocks):
        self.owned = ray_blocks // count
        self.half_blocks = ray_blocks // 2

    def core(self):
        return lax.rem(lax.axis_index("cell"), 2)

    def place(self, core, q):
        owner = lax.div(q, self.owned)
        other_core = lax.rem(owner + core, 2)
        first = other_core * self.half_blocks + lax.div(owner, 2) * self.owned
        return first + lax.rem(q, self.owned)

    def survey(self, core, survey_ref, i):
        other_core, rest = divmod(i, self.half_blocks)
        chip, offset = divmod(rest, self.owned)
        owner = 2 * chip + (1 - core if other_core else core)
        return survey_ref[owner * self.owned + offset]


def forward(order, survey_ref, half_ref, dense_ref, own_ref, away_ref):
    core = order.core()
    half = own_ref.shape[0]
    for i in range(2 * half):
        travel = lax.dot_general(
            half_ref[order.survey(core, survey_ref, i)],
            dense_ref[i],
            (((1,), (1,)), ((), ())),
            preferred_element_type=jnp.float32,
        )
        if i < half:
            own_ref[i] = travel
        else:
            away_ref[i - half] = travel


def setup_kernel(
    order, count_ref, ray_hbm, cell_hbm, survey_hbm, members_hbm, blocks_hbm,
    dense_ref, half_ref, own_ref, away_ref,
    ray_ref, cell_ref, survey_ref, members_ref, staged, upper, lower, small_sems, sems,
):
    slots, rays, width = blocks_hbm.shape
    chunks = slots // CHUNK
    core = order.core()
    small = [
        pltpu.make_async_copy(source, target, small_sems.at[i])
        for i, (source, target) in enumerate(
            (
                (ray_hbm, ray_ref),
                (cell_hbm, cell_ref),
                (survey_hbm, survey_ref),
                (members_hbm, members_ref),
            )
        )
    ]
    large = []
    for i in range(chunks):
        part = pl.ds(i * CHUNK, CHUNK)
        large.append(pltpu.make_async_copy(blocks_hbm.at[part], staged.at[part], sems.at[i]))
    for copy in small + large:
        copy.start()
    upper[...] = jnp.zeros_like(upper)
    lower[...] = jnp.zeros_like(lower)
    middle = rays // 2
    for copy in small:
        copy.wait()
    half_ref[...] = members_ref[...].astype(half_ref.dtype)
    count = count_ref[0]
    spare = dense_ref.shape[0]
    for i in range(chunks):
        large[i].wait()
        for k in range(i * CHUNK, (i + 1) * CHUNK):
            place = jnp.where(k < count, order.place(core, ray_ref[k]), spare)
            b = cell_ref[k]
            upper[b, place] = upper[b, place] + staged[k, :middle].astype(jnp.float32)
            lower[b, place] = lower[b, place] + staged[k, middle:].astype(jnp.float32)
    for b in range(upper.shape[0]):
        cells = slice(b * width, (b + 1) * width)
        dense_ref[:, :middle, cells] = upper[b, :spare].astype(dense_ref.dtype)
        dense_ref[:, middle:, cells] = lower[b, :spare].astype(dense_ref.dtype)
    forward(order, survey_ref, half_ref, dense_ref, own_ref, away_ref)


def misfit_kernel(travel_ref, observed_ref, noise_ref, out_ref):
    travel = travel_ref[...]
    spread = noise_ref[...][:, None, :]
    scaled = (travel - observed_ref[...]) / spread
    residual = DATA_GAIN * scaled / (spread * (1.0 + scaled * scaled))
    out_ref[...] = jnp.broadcast_to(residual.astype(out_ref.dtype)[None], out_ref.shape)


def arrival_kernel(observed_ref, halo_ref, token_ref):
    del observed_ref, halo_ref
    token_ref[...] = jnp.zeros_like(token_ref)


def add_products(order, survey_ref, low, products, upper, lower):
    core = order.core()
    middle = upper.shape[1]
    for i, product in enumerate(products):
        s = order.survey(core, survey_ref, low + i)
        upper[s] = upper[s] + product[:middle]
        lower[s] = lower[s] + product[middle:]


def gradient_kernel(
    order, survey_ref, residual_ref, dense_ref, members_ref, prior_ref, chip_ref, link_ref, token_ref,
    upper, lower,
):
    del token_ref
    products = [
        jnp.dot(residual_ref[i], dense_ref[i], preferred_element_type=jnp.float32)
        for i in range(residual_ref.shape[0])
    ]
    surveys = members_ref.shape[0]
    middle = upper.shape[1]
    for s in range(surveys):
        m = members_ref[s]
        value = ALPHA_PRIOR * (m - prior_ref[s])
        if s > 0:
            value = value + BETA_TIME * (m - members_ref[s - 1])
        if s < surveys - 1:
            value = value + BETA_TIME * (m - members_ref[s + 1])
        neighbours = chip_ref[s].astype(jnp.float32) + link_ref[s].astype(jnp.float32)
        value = value + GAMMA_DEPTH * (2.0 * m - neighbours)
        upper[s] = value[:middle]
        lower[s] = value[middle:]
    add_products(order, survey_ref, 0, products, upper, lower)


def finish_gradient(
    order, survey_ref, residual_ref, dense_ref, upper_ref, lower_ref, upper, lower
):
    half = residual_ref.shape[0]
    products = [
        jnp.dot(residual_ref[i], dense_ref[half + i], preferred_element_type=jnp.float32)
        for i in range(half)
    ]
    upper[...] = upper_ref[...]
    lower[...] = lower_ref[...]
    add_products(order, survey_ref, half, products, upper, lower)


def step_kernel(
    order, survey_ref, residual_ref, dense_ref, upper_ref, lower_ref, members_ref,
    out_ref, half_ref, own_ref, away_ref,
    upper, lower,
):
    finish_gradient(order, survey_ref, residual_ref, dense_ref, upper_ref, lower_ref, upper, lower)
    middle = upper.shape[1]
    for rows, grad in ((slice(0, middle), upper), (slice(middle, None), lower)):
        updated = members_ref[:, rows] - STEP_SIZE * grad[...]
        out_ref[:, rows] = updated
        half_ref[:, rows] = updated.astype(half_ref.dtype)
    forward(order, survey_ref, half_ref, dense_ref, own_ref, away_ref)


def last_kernel(
    order, survey_ref, residual_ref, dense_ref, upper_ref, lower_ref, members_ref,
    out_ref, gradient_ref,
    upper, lower,
):
    finish_gradient(order, survey_ref, residual_ref, dense_ref, upper_ref, lower_ref, upper, lower)
    middle = upper.shape[1]
    for rows, grad in ((slice(0, middle), upper), (slice(middle, None), lower)):
        out_ref[:, rows] = members_ref[:, rows] - STEP_SIZE * grad[...]
        gradient_ref[:, rows] = grad[...].astype(gradient_ref.dtype)


def shards(
    prior_members, blocks, block_ray, block_cell, block_count, ray_survey, observed, noise_scale
):
    surveys, ensemble, cells_dev = prior_members.shape
    slots, rays, width = blocks.shape
    ray_blocks = ray_survey.shape[0]
    count = lax.axis_size("cell")
    order = Order(count, ray_blocks)
    owned, half_blocks = order.owned, order.half_blocks
    chips = count // 2
    params = pltpu.CompilerParams(vmem_limit_bytes=VMEM_BYTES)

    def bf16(*shape):
        return jax.ShapeDtypeStruct(shape, jnp.bfloat16)

    def f32(*shape):
        return jax.ShapeDtypeStruct(shape, jnp.float32)

    members_f32 = f32(surveys, ensemble, cells_dev)
    part_f32 = f32(surveys, ensemble // 2, cells_dev)
    members_bf16 = bf16(surveys, ensemble, cells_dev)
    travels = (f32(half_blocks, ensemble, rays),) * 2

    in_hbm = [
        pltpu.with_memory_space_constraint(array, pltpu.HBM)
        for array in (block_ray, block_cell, ray_survey, prior_members, blocks)
    ]
    dense, half, own, away = pl.pallas_call(
        functools.partial(setup_kernel, order),
        out_shape=(bf16(ray_blocks, rays, cells_dev), members_bf16) + travels,
        in_specs=[SMEM] + [HBM] * 5,
        out_specs=(VMEM,) * 4,
        scratch_shapes=[
            pltpu.SMEM(block_ray.shape, jnp.int32),
            pltpu.SMEM(block_cell.shape, jnp.int32),
            pltpu.SMEM(ray_survey.shape, jnp.int32),
            pltpu.VMEM(prior_members.shape, jnp.float32),
            pltpu.VMEM(blocks.shape, blocks.dtype),
            pltpu.VMEM((cells_dev // width, ray_blocks + 1, rays // 2, width), jnp.float32),
            pltpu.VMEM((cells_dev // width, ray_blocks + 1, rays // 2, width), jnp.float32),
            pltpu.SemaphoreType.DMA((4,)),
            pltpu.SemaphoreType.DMA((slots // CHUNK,)),
        ],
        compiler_params=pltpu.CompilerParams(vmem_limit_bytes=VMEM_BYTES),
    )(block_count, *in_hbm)

    chip_pairs = [(i, i ^ 1) for i in range(count)]
    link_pairs = [pair for i in range(1, count - 1, 2) for pair in ((i, i + 1), (i + 1, i))]
    same_core = [list(range(core, count, 2)) for core in range(2)]

    def exchange(array):
        return lax.all_to_all(
            array, "cell", split_axis=0, concat_axis=0, axis_index_groups=same_core, tiled=True
        )

    members = prior_members
    for iteration in range(ITERS):
        received = lax.ppermute(away, "cell", chip_pairs)
        chip_halo = lax.ppermute(half, "cell", chip_pairs)
        received, chip_halo = lax.optimization_barrier((received, chip_halo))
        chip_travel = ((own + received) * SENT_SCALE).astype(jnp.float16)
        parts = exchange(chip_travel)
        parts, moved_half = lax.optimization_barrier((parts, half))
        link_halo = lax.ppermute(moved_half, "cell", link_pairs)
        parts = parts.reshape(chips, owned, ensemble, rays).astype(jnp.float32)
        travel = jnp.sum(parts, axis=0) / SENT_SCALE
        copies = pl.pallas_call(
            misfit_kernel,
            out_shape=bf16(chips, owned, ensemble, rays),
            in_specs=[VMEM] * 3,
            out_specs=VMEM,
            compiler_params=params,
        )(travel, observed, noise_scale)
        residual = exchange(copies.reshape(half_blocks, ensemble, rays))
        residual, after_exchange = lax.optimization_barrier((residual, observed))
        token = pl.pallas_call(
            arrival_kernel,
            out_shape=f32(8, 128),
            in_specs=[ANY] * 2,
            out_specs=VMEM,
            compiler_params=params,
        )(after_exchange, link_halo)
        residual, token = lax.optimization_barrier((residual, token))
        other_residual = lax.ppermute(residual, "cell", chip_pairs)
        partial = pl.pallas_call(
            functools.partial(gradient_kernel, order),
            out_shape=(part_f32, part_f32),
            in_specs=[SMEM] + [VMEM] * 6 + [ANY],
            out_specs=(VMEM, VMEM),
            compiler_params=params,
        )(ray_survey, residual, dense, members, prior_members, chip_halo, link_halo, token)
        last = iteration == ITERS - 1
        outputs = (members_f32, members_bf16) + (() if last else travels)
        results = pl.pallas_call(
            functools.partial(last_kernel if last else step_kernel, order),
            out_shape=outputs,
            in_specs=[SMEM] + [VMEM] * 5,
            out_specs=(VMEM,) * len(outputs),
            scratch_shapes=[pltpu.VMEM(part_f32.shape, jnp.float32)] * 2,
            compiler_params=params,
        )(ray_survey, other_residual, dense, *partial, members)
        if last:
            return results
        members, half, own, away = results


def solution(mesh):
    placed = (
        P(None, "ens", "cell"),
        P("cell", None, None),
        P("cell"),
        P("cell"),
        P("cell"),
        P(),
        P("cell", "ens", None),
        P("cell", None),
    )
    return jax.shard_map(
        shards,
        mesh=mesh,
        in_specs=placed,
        out_specs=(P(None, "ens", "cell"), P(None, "ens", "cell")),
        check_vma=False,
    )
```

```python
import functools

import jax
import jax.numpy as jnp
from jax import lax
from jax.experimental import pallas as pl
from jax.experimental.pallas import tpu as pltpu
from jax.sharding import PartitionSpec as P

ITERS = 3

ALPHA_PRIOR = 0.5
BETA_TIME = 0.25
GAMMA_DEPTH = 0.25
STEP_SIZE = 0.05
DATA_GAIN = 1.0

SENT_SCALE = 1.0 / 32.0

CHUNK = 8
VMEM_BYTES = 24 * 1024 * 1024
SETUP_VMEM_BYTES = 60 * 1024 * 1024

SMEM = pl.BlockSpec(memory_space=pltpu.SMEM)
VMEM = pl.BlockSpec(memory_space=pltpu.VMEM)
ANY = pl.BlockSpec(memory_space=pl.ANY)
HBM = pl.BlockSpec(memory_space=pltpu.HBM)


class Order:
    def __init__(self, count, ray_blocks):
        self.owned = ray_blocks // count
        self.half_blocks = ray_blocks // 2

    def core(self):
        return lax.rem(lax.axis_index("cell"), 2)

    def place(self, core, q):
        owner = lax.div(q, self.owned)
        other_core = lax.rem(owner + core, 2)
        first = other_core * self.half_blocks + lax.div(owner, 2) * self.owned
        return first + lax.rem(q, self.owned)

    def survey(self, core, survey_ref, i):
        other_core, rest = divmod(i, self.half_blocks)
        chip, offset = divmod(rest, self.owned)
        owner = 2 * chip + (1 - core if other_core else core)
        return survey_ref[owner * self.owned + offset]


def forward(order, survey_ref, half_ref, dense_ref, own_ref, away_ref):
    core = order.core()
    half = own_ref.shape[0]
    for i in range(2 * half):
        travel = lax.dot_general(
            half_ref[order.survey(core, survey_ref, i)],
            dense_ref[i],
            (((1,), (1,)), ((), ())),
            preferred_element_type=jnp.float32,
        )
        if i < half:
            own_ref[i] = travel
        else:
            away_ref[i - half] = travel


def setup_kernel(
    order, count_ref, ray_hbm, cell_hbm, survey_hbm, members_hbm, blocks_hbm,
    dense_ref, half_ref, own_ref, away_ref,
    ray_ref, cell_ref, survey_ref, members_ref, staged, upper, lower, small_sems, sems,
):
    slots, rays, width = blocks_hbm.shape
    chunks = slots // CHUNK
    core = order.core()
    small = [
        pltpu.make_async_copy(source, target, small_sems.at[i])
        for i, (source, target) in enumerate(
            (
                (ray_hbm, ray_ref),
                (cell_hbm, cell_ref),
                (survey_hbm, survey_ref),
                (members_hbm, members_ref),
            )
        )
    ]
    large = []
    for i in range(chunks):
        part = pl.ds(i * CHUNK, CHUNK)
        large.append(pltpu.make_async_copy(blocks_hbm.at[part], staged.at[part], sems.at[i]))
    for copy in small + large:
        copy.start()
    upper[...] = jnp.zeros_like(upper)
    lower[...] = jnp.zeros_like(lower)
    middle = rays // 2
    for copy in small:
        copy.wait()
    half_ref[...] = members_ref[...].astype(half_ref.dtype)
    count = count_ref[0]
    spare = dense_ref.shape[0]
    for i in range(chunks):
        large[i].wait()
        for k in range(i * CHUNK, (i + 1) * CHUNK):
            place = jnp.where(k < count, order.place(core, ray_ref[k]), spare)
            b = cell_ref[k]
            upper[b, place] = upper[b, place] + staged[k, :middle].astype(jnp.float32)
            lower[b, place] = lower[b, place] + staged[k, middle:].astype(jnp.float32)
    for b in range(upper.shape[0]):
        cells = slice(b * width, (b + 1) * width)
        dense_ref[:, :middle, cells] = upper[b, :spare].astype(dense_ref.dtype)
        dense_ref[:, middle:, cells] = lower[b, :spare].astype(dense_ref.dtype)
    forward(order, survey_ref, half_ref, dense_ref, own_ref, away_ref)


def misfit_kernel(travel_ref, observed_ref, noise_ref, token_ref, out_ref):
    del token_ref
    travel = travel_ref[...]
    spread = noise_ref[...][:, None, :]
    scaled = (travel - observed_ref[...]) / spread
    residual = DATA_GAIN * scaled / (spread * (1.0 + scaled * scaled))
    out_ref[...] = jnp.broadcast_to(residual.astype(out_ref.dtype)[None], out_ref.shape)


def arrival_kernel(observed_ref, chip_ref, link_ref, token_ref):
    del observed_ref, chip_ref, link_ref
    token_ref[...] = jnp.zeros_like(token_ref)


def add_products(order, survey_ref, low, products, upper, lower):
    core = order.core()
    middle = upper.shape[1]
    for i, product in enumerate(products):
        s = order.survey(core, survey_ref, low + i)
        upper[s] = upper[s] + product[:middle]
        lower[s] = lower[s] + product[middle:]


def gradient_kernel(
    order, survey_ref, residual_ref, dense_ref, members_ref, prior_ref, chip_ref, link_ref,
    upper, lower,
):
    products = [
        jnp.dot(residual_ref[i], dense_ref[i], preferred_element_type=jnp.float32)
        for i in range(residual_ref.shape[0])
    ]
    surveys = members_ref.shape[0]
    middle = upper.shape[1]
    for s in range(surveys):
        m = members_ref[s]
        value = ALPHA_PRIOR * (m - prior_ref[s])
        if s > 0:
            value = value + BETA_TIME * (m - members_ref[s - 1])
        if s < surveys - 1:
            value = value + BETA_TIME * (m - members_ref[s + 1])
        neighbours = chip_ref[s].astype(jnp.float32) + link_ref[s].astype(jnp.float32)
        value = value + GAMMA_DEPTH * (2.0 * m - neighbours)
        upper[s] = value[:middle]
        lower[s] = value[middle:]
    add_products(order, survey_ref, 0, products, upper, lower)


def finish_gradient(
    order, survey_ref, residual_ref, dense_ref, upper_ref, lower_ref, upper, lower
):
    half = residual_ref.shape[0]
    products = [
        jnp.dot(residual_ref[i], dense_ref[half + i], preferred_element_type=jnp.float32)
        for i in range(half)
    ]
    upper[...] = upper_ref[...]
    lower[...] = lower_ref[...]
    add_products(order, survey_ref, half, products, upper, lower)


def step_kernel(
    order, survey_ref, residual_ref, dense_ref, upper_ref, lower_ref, members_ref,
    out_ref, half_ref, own_ref, away_ref,
    upper, lower,
):
    finish_gradient(order, survey_ref, residual_ref, dense_ref, upper_ref, lower_ref, upper, lower)
    middle = upper.shape[1]
    for rows, grad in ((slice(0, middle), upper), (slice(middle, None), lower)):
        updated = members_ref[:, rows] - STEP_SIZE * grad[...]
        out_ref[:, rows] = updated
        half_ref[:, rows] = updated.astype(half_ref.dtype)
    forward(order, survey_ref, half_ref, dense_ref, own_ref, away_ref)


def last_kernel(
    order, survey_ref, residual_ref, dense_ref, upper_ref, lower_ref, members_ref,
    out_ref, gradient_ref,
    upper, lower,
):
    finish_gradient(order, survey_ref, residual_ref, dense_ref, upper_ref, lower_ref, upper, lower)
    middle = upper.shape[1]
    for rows, grad in ((slice(0, middle), upper), (slice(middle, None), lower)):
        out_ref[:, rows] = members_ref[:, rows] - STEP_SIZE * grad[...]
        gradient_ref[:, rows] = grad[...].astype(gradient_ref.dtype)


def shards(
    prior_members, blocks, block_ray, block_cell, block_count, ray_survey, observed, noise_scale
):
    surveys, ensemble, cells_dev = prior_members.shape
    slots, rays, width = blocks.shape
    ray_blocks = ray_survey.shape[0]
    count = lax.axis_size("cell")
    order = Order(count, ray_blocks)
    owned, half_blocks = order.owned, order.half_blocks
    chips = count // 2
    params = pltpu.CompilerParams(vmem_limit_bytes=VMEM_BYTES)

    def bf16(*shape):
        return jax.ShapeDtypeStruct(shape, jnp.bfloat16)

    def f32(*shape):
        return jax.ShapeDtypeStruct(shape, jnp.float32)

    members_f32 = f32(surveys, ensemble, cells_dev)
    part_f32 = f32(surveys, ensemble // 2, cells_dev)
    members_bf16 = bf16(surveys, ensemble, cells_dev)
    travels = (f32(half_blocks, ensemble, rays),) * 2

    in_hbm = [
        pltpu.with_memory_space_constraint(array, pltpu.HBM)
        for array in (block_ray, block_cell, ray_survey, prior_members, blocks)
    ]
    dense, half, own, away = pl.pallas_call(
        functools.partial(setup_kernel, order),
        out_shape=(bf16(ray_blocks, rays, cells_dev), members_bf16) + travels,
        in_specs=[SMEM] + [HBM] * 5,
        out_specs=(VMEM,) * 4,
        scratch_shapes=[
            pltpu.SMEM(block_ray.shape, jnp.int32),
            pltpu.SMEM(block_cell.shape, jnp.int32),
            pltpu.SMEM(ray_survey.shape, jnp.int32),
            pltpu.VMEM(prior_members.shape, jnp.float32),
            pltpu.VMEM(blocks.shape, blocks.dtype),
            pltpu.VMEM((cells_dev // width, ray_blocks + 1, rays // 2, width), jnp.float32),
            pltpu.VMEM((cells_dev // width, ray_blocks + 1, rays // 2, width), jnp.float32),
            pltpu.SemaphoreType.DMA((4,)),
            pltpu.SemaphoreType.DMA((slots // CHUNK,)),
        ],
        compiler_params=pltpu.CompilerParams(vmem_limit_bytes=VMEM_BYTES),
    )(block_count, *in_hbm)

    chip_pairs = [(i, i ^ 1) for i in range(count)]
    link_pairs = [pair for i in range(1, count - 1, 2) for pair in ((i, i + 1), (i + 1, i))]
    same_core = [list(range(core, count, 2)) for core in range(2)]

    def exchange(array):
        return lax.all_to_all(
            array, "cell", split_axis=0, concat_axis=0, axis_index_groups=same_core, tiled=True
        )

    members = prior_members
    for iteration in range(ITERS):
        received = lax.ppermute(away, "cell", chip_pairs)
        chip_halo = lax.ppermute(half, "cell", chip_pairs)
        chip_travel = ((own + received) * SENT_SCALE).astype(jnp.float16)
        link_halo = lax.ppermute(half, "cell", link_pairs)
        parts = exchange(chip_travel)
        parts, after_parts = lax.optimization_barrier((parts, observed))
        token = pl.pallas_call(
            arrival_kernel,
            out_shape=f32(8, 128),
            in_specs=[ANY] * 3,
            out_specs=VMEM,
            compiler_params=params,
        )(after_parts, chip_halo, link_halo)
        parts, token = lax.optimization_barrier((parts, token))
        parts = parts.reshape(chips, owned, ensemble, rays).astype(jnp.float32)
        travel = jnp.sum(parts, axis=0) / SENT_SCALE
        copies = pl.pallas_call(
            misfit_kernel,
            out_shape=bf16(chips, owned, ensemble, rays),
            in_specs=[VMEM] * 3 + [ANY],
            out_specs=VMEM,
            compiler_params=params,
        )(travel, observed, noise_scale, token)
        residual = exchange(copies.reshape(half_blocks, ensemble, rays))
        other_residual = lax.ppermute(residual, "cell", chip_pairs)
        partial = pl.pallas_call(
            functools.partial(gradient_kernel, order),
            out_shape=(part_f32, part_f32),
            in_specs=[SMEM] + [VMEM] * 6,
            out_specs=(VMEM, VMEM),
            compiler_params=params,
        )(ray_survey, residual, dense, members, prior_members, chip_halo, link_halo)
        last = iteration == ITERS - 1
        outputs = (members_f32, members_bf16) + (() if last else travels)
        results = pl.pallas_call(
            functools.partial(last_kernel if last else step_kernel, order),
            out_shape=outputs,
            in_specs=[SMEM] + [VMEM] * 5,
            out_specs=(VMEM,) * len(outputs),
            scratch_shapes=[pltpu.VMEM(part_f32.shape, jnp.float32)] * 2,
            compiler_params=params,
        )(ray_survey, other_residual, dense, *partial, members)
        if last:
            return results
        members, half, own, away = results


def solution(mesh):
    placed = (
        P(None, "ens", "cell"),
        P("cell", None, None),
        P("cell"),
        P("cell"),
        P("cell"),
        P(),
        P("cell", "ens", None),
        P("cell", None),
    )
    return jax.shard_map(
        shards,
        mesh=mesh,
        in_specs=placed,
        out_specs=(P(None, "ens", "cell"), P(None, "ens", "cell")),
        check_vma=False,
    )
```

```python
import functools

import jax
import jax.numpy as jnp
from jax import lax
from jax.experimental import pallas as pl
from jax.experimental.pallas import tpu as pltpu
from jax.sharding import PartitionSpec as P

ITERS = 3

ALPHA_PRIOR = 0.5
BETA_TIME = 0.25
GAMMA_DEPTH = 0.25
STEP_SIZE = 0.05
DATA_GAIN = 1.0

SENT_SCALE = 1.0 / 32.0

CHUNK = 8
VMEM_BYTES = 24 * 1024 * 1024
SETUP_VMEM_BYTES = 60 * 1024 * 1024

SMEM = pl.BlockSpec(memory_space=pltpu.SMEM)
VMEM = pl.BlockSpec(memory_space=pltpu.VMEM)
ANY = pl.BlockSpec(memory_space=pl.ANY)
HBM = pl.BlockSpec(memory_space=pltpu.HBM)


class Order:
    def __init__(self, count, ray_blocks):
        self.owned = ray_blocks // count
        self.half_blocks = ray_blocks // 2

    def core(self):
        return lax.rem(lax.axis_index("cell"), 2)

    def place(self, core, q):
        owner = lax.div(q, self.owned)
        other_core = lax.rem(owner + core, 2)
        first = other_core * self.half_blocks + lax.div(owner, 2) * self.owned
        return first + lax.rem(q, self.owned)

    def survey(self, core, survey_ref, i):
        other_core, rest = divmod(i, self.half_blocks)
        chip, offset = divmod(rest, self.owned)
        owner = 2 * chip + (1 - core if other_core else core)
        return survey_ref[owner * self.owned + offset]


def forward(order, survey_ref, half_ref, dense_ref, own_ref, away_ref):
    core = order.core()
    half = own_ref.shape[0]
    for i in range(2 * half):
        travel = lax.dot_general(
            half_ref[order.survey(core, survey_ref, i)],
            dense_ref[i],
            (((1,), (1,)), ((), ())),
            preferred_element_type=jnp.float32,
        )
        if i < half:
            own_ref[i] = travel
        else:
            away_ref[i - half] = travel


def setup_kernel(
    order, count_ref, ray_hbm, cell_hbm, survey_hbm, members_hbm, blocks_hbm,
    dense_ref, half_ref, own_ref, away_ref,
    ray_ref, cell_ref, survey_ref, members_ref, staged, upper, lower, small_sems, sems,
):
    slots, rays, width = blocks_hbm.shape
    chunks = slots // CHUNK
    core = order.core()
    small = [
        pltpu.make_async_copy(source, target, small_sems.at[i])
        for i, (source, target) in enumerate(
            (
                (ray_hbm, ray_ref),
                (cell_hbm, cell_ref),
                (survey_hbm, survey_ref),
                (members_hbm, members_ref),
            )
        )
    ]
    large = []
    for i in range(chunks):
        part = pl.ds(i * CHUNK, CHUNK)
        large.append(pltpu.make_async_copy(blocks_hbm.at[part], staged.at[part], sems.at[i]))
    for copy in small[:-1] + large + small[-1:]:
        copy.start()
    upper[...] = jnp.zeros_like(upper)
    lower[...] = jnp.zeros_like(lower)
    middle = rays // 2
    for copy in small[:-1]:
        copy.wait()
    count = count_ref[0]
    spare = dense_ref.shape[0]
    for i in range(chunks):
        large[i].wait()
        for k in range(i * CHUNK, (i + 1) * CHUNK):
            place = jnp.where(k < count, order.place(core, ray_ref[k]), spare)
            b = cell_ref[k]
            upper[b, place] = upper[b, place] + staged[k, :middle].astype(jnp.float32)
            lower[b, place] = lower[b, place] + staged[k, middle:].astype(jnp.float32)
    for b in range(upper.shape[0]):
        cells = slice(b * width, (b + 1) * width)
        dense_ref[:, :middle, cells] = upper[b, :spare].astype(dense_ref.dtype)
        dense_ref[:, middle:, cells] = lower[b, :spare].astype(dense_ref.dtype)
    small[-1].wait()
    half_ref[...] = members_ref[...].astype(half_ref.dtype)
    forward(order, survey_ref, half_ref, dense_ref, own_ref, away_ref)


def misfit_kernel(travel_ref, observed_ref, noise_ref, token_ref, out_ref):
    del token_ref
    travel = travel_ref[...]
    spread = noise_ref[...][:, None, :]
    scaled = (travel - observed_ref[...]) / spread
    residual = DATA_GAIN * scaled / (spread * (1.0 + scaled * scaled))
    out_ref[...] = jnp.broadcast_to(residual.astype(out_ref.dtype)[None], out_ref.shape)


def arrival_kernel(observed_ref, halo_ref, token_ref):
    del observed_ref, halo_ref
    token_ref[...] = jnp.zeros_like(token_ref)


def add_products(order, survey_ref, low, products, upper, lower):
    core = order.core()
    middle = upper.shape[1]
    for i, product in enumerate(products):
        s = order.survey(core, survey_ref, low + i)
        upper[s] = upper[s] + product[:middle]
        lower[s] = lower[s] + product[middle:]


def gradient_kernel(
    order, survey_ref, residual_ref, dense_ref, members_ref, prior_ref, chip_ref, link_ref,
    upper, lower,
):
    products = [
        jnp.dot(residual_ref[i], dense_ref[i], preferred_element_type=jnp.float32)
        for i in range(residual_ref.shape[0])
    ]
    surveys = members_ref.shape[0]
    middle = upper.shape[1]
    for s in range(surveys):
        m = members_ref[s]
        value = ALPHA_PRIOR * (m - prior_ref[s])
        if s > 0:
            value = value + BETA_TIME * (m - members_ref[s - 1])
        if s < surveys - 1:
            value = value + BETA_TIME * (m - members_ref[s + 1])
        neighbours = chip_ref[s].astype(jnp.float32) + link_ref[s].astype(jnp.float32)
        value = value + GAMMA_DEPTH * (2.0 * m - neighbours)
        upper[s] = value[:middle]
        lower[s] = value[middle:]
    add_products(order, survey_ref, 0, products, upper, lower)


def finish_gradient(
    order, survey_ref, residual_ref, dense_ref, upper_ref, lower_ref, upper, lower
):
    half = residual_ref.shape[0]
    products = [
        jnp.dot(residual_ref[i], dense_ref[half + i], preferred_element_type=jnp.float32)
        for i in range(half)
    ]
    upper[...] = upper_ref[...]
    lower[...] = lower_ref[...]
    add_products(order, survey_ref, half, products, upper, lower)


def step_kernel(
    order, survey_ref, residual_ref, dense_ref, upper_ref, lower_ref, members_ref,
    out_ref, half_ref, own_ref, away_ref,
    upper, lower,
):
    finish_gradient(order, survey_ref, residual_ref, dense_ref, upper_ref, lower_ref, upper, lower)
    middle = upper.shape[1]
    for rows, grad in ((slice(0, middle), upper), (slice(middle, None), lower)):
        updated = members_ref[:, rows] - STEP_SIZE * grad[...]
        out_ref[:, rows] = updated
        half_ref[:, rows] = updated.astype(half_ref.dtype)
    forward(order, survey_ref, half_ref, dense_ref, own_ref, away_ref)


def last_kernel(
    order, survey_ref, residual_ref, dense_ref, upper_ref, lower_ref, members_ref,
    out_ref, gradient_ref,
    upper, lower,
):
    finish_gradient(order, survey_ref, residual_ref, dense_ref, upper_ref, lower_ref, upper, lower)
    middle = upper.shape[1]
    for rows, grad in ((slice(0, middle), upper), (slice(middle, None), lower)):
        out_ref[:, rows] = members_ref[:, rows] - STEP_SIZE * grad[...]
        gradient_ref[:, rows] = grad[...].astype(gradient_ref.dtype)


def shards(
    prior_members, blocks, block_ray, block_cell, block_count, ray_survey, observed, noise_scale
):
    surveys, ensemble, cells_dev = prior_members.shape
    slots, rays, width = blocks.shape
    ray_blocks = ray_survey.shape[0]
    count = lax.axis_size("cell")
    order = Order(count, ray_blocks)
    owned, half_blocks = order.owned, order.half_blocks
    chips = count // 2
    params = pltpu.CompilerParams(vmem_limit_bytes=VMEM_BYTES)

    def bf16(*shape):
        return jax.ShapeDtypeStruct(shape, jnp.bfloat16)

    def f32(*shape):
        return jax.ShapeDtypeStruct(shape, jnp.float32)

    members_f32 = f32(surveys, ensemble, cells_dev)
    part_f32 = f32(surveys, ensemble // 2, cells_dev)
    members_bf16 = bf16(surveys, ensemble, cells_dev)
    travels = (f32(half_blocks, ensemble, rays),) * 2

    in_hbm = [
        pltpu.with_memory_space_constraint(array, pltpu.HBM)
        for array in (block_ray, block_cell, ray_survey, prior_members, blocks)
    ]
    dense, half, own, away = pl.pallas_call(
        functools.partial(setup_kernel, order),
        out_shape=(bf16(ray_blocks, rays, cells_dev), members_bf16) + travels,
        in_specs=[SMEM] + [HBM] * 5,
        out_specs=(VMEM,) * 4,
        scratch_shapes=[
            pltpu.SMEM(block_ray.shape, jnp.int32),
            pltpu.SMEM(block_cell.shape, jnp.int32),
            pltpu.SMEM(ray_survey.shape, jnp.int32),
            pltpu.VMEM(prior_members.shape, jnp.float32),
            pltpu.VMEM(blocks.shape, blocks.dtype),
            pltpu.VMEM((cells_dev // width, ray_blocks + 1, rays // 2, width), jnp.float32),
            pltpu.VMEM((cells_dev // width, ray_blocks + 1, rays // 2, width), jnp.float32),
            pltpu.SemaphoreType.DMA((4,)),
            pltpu.SemaphoreType.DMA((slots // CHUNK,)),
        ],
        compiler_params=pltpu.CompilerParams(vmem_limit_bytes=VMEM_BYTES),
    )(block_count, *in_hbm)

    chip_pairs = [(i, i ^ 1) for i in range(count)]
    link_pairs = [pair for i in range(1, count - 1, 2) for pair in ((i, i + 1), (i + 1, i))]
    same_core = [list(range(core, count, 2)) for core in range(2)]

    def exchange(array):
        return lax.all_to_all(
            array, "cell", split_axis=0, concat_axis=0, axis_index_groups=same_core, tiled=True
        )

    members = prior_members
    for iteration in range(ITERS):
        received = lax.ppermute(away, "cell", chip_pairs)
        chip_halo = lax.ppermute(half, "cell", chip_pairs)
        received, chip_halo = lax.optimization_barrier((received, chip_halo))
        chip_travel = ((own + received) * SENT_SCALE).astype(jnp.float16)
        link_halo = lax.ppermute(half, "cell", link_pairs)
        parts = exchange(chip_travel)
        parts, after_parts = lax.optimization_barrier((parts, observed))
        token = pl.pallas_call(
            arrival_kernel,
            out_shape=f32(8, 128),
            in_specs=[ANY] * 2,
            out_specs=VMEM,
            compiler_params=params,
        )(after_parts, link_halo)
        parts, token = lax.optimization_barrier((parts, token))
        parts = parts.reshape(chips, owned, ensemble, rays).astype(jnp.float32)
        travel = jnp.sum(parts, axis=0) / SENT_SCALE
        copies = pl.pallas_call(
            misfit_kernel,
            out_shape=bf16(chips, owned, ensemble, rays),
            in_specs=[VMEM] * 3 + [ANY],
            out_specs=VMEM,
            compiler_params=params,
        )(travel, observed, noise_scale, token)
        residual = exchange(copies.reshape(half_blocks, ensemble, rays))
        other_residual = lax.ppermute(residual, "cell", chip_pairs)
        partial = pl.pallas_call(
            functools.partial(gradient_kernel, order),
            out_shape=(part_f32, part_f32),
            in_specs=[SMEM] + [VMEM] * 6,
            out_specs=(VMEM, VMEM),
            compiler_params=params,
        )(ray_survey, residual, dense, members, prior_members, chip_halo, link_halo)
        last = iteration == ITERS - 1
        outputs = (members_f32, members_bf16) + (() if last else travels)
        results = pl.pallas_call(
            functools.partial(last_kernel if last else step_kernel, order),
            out_shape=outputs,
            in_specs=[SMEM] + [VMEM] * 5,
            out_specs=(VMEM,) * len(outputs),
            scratch_shapes=[pltpu.VMEM(part_f32.shape, jnp.float32)] * 2,
            compiler_params=params,
        )(ray_survey, other_residual, dense, *partial, members)
        if last:
            return results
        members, half, own, away = results


def solution(mesh):
    placed = (
        P(None, "ens", "cell"),
        P("cell", None, None),
        P("cell"),
        P("cell"),
        P("cell"),
        P(),
        P("cell", "ens", None),
        P("cell", None),
    )
    return jax.shard_map(
        shards,
        mesh=mesh,
        in_specs=placed,
        out_specs=(P(None, "ens", "cell"), P(None, "ens", "cell")),
        check_vma=False,
    )
```

```python
import functools

import jax
import jax.numpy as jnp
from jax import lax
from jax.experimental import pallas as pl
from jax.experimental.pallas import tpu as pltpu
from jax.sharding import PartitionSpec as P

ITERS = 3

ALPHA_PRIOR = 0.5
BETA_TIME = 0.25
GAMMA_DEPTH = 0.25
STEP_SIZE = 0.05
DATA_GAIN = 1.0

SENT_SCALE = 1.0 / 32.0

CHUNK = 16
VMEM_BYTES = 24 * 1024 * 1024
SETUP_VMEM_BYTES = 60 * 1024 * 1024

SMEM = pl.BlockSpec(memory_space=pltpu.SMEM)
VMEM = pl.BlockSpec(memory_space=pltpu.VMEM)
ANY = pl.BlockSpec(memory_space=pl.ANY)
HBM = pl.BlockSpec(memory_space=pltpu.HBM)


class Order:
    def __init__(self, count, ray_blocks):
        self.owned = ray_blocks // count
        self.half_blocks = ray_blocks // 2

    def core(self):
        return lax.rem(lax.axis_index("cell"), 2)

    def place(self, core, q):
        owner = lax.div(q, self.owned)
        other_core = lax.rem(owner + core, 2)
        first = other_core * self.half_blocks + lax.div(owner, 2) * self.owned
        return first + lax.rem(q, self.owned)

    def survey(self, core, survey_ref, i):
        other_core, rest = divmod(i, self.half_blocks)
        chip, offset = divmod(rest, self.owned)
        owner = 2 * chip + (1 - core if other_core else core)
        return survey_ref[owner * self.owned + offset]


def forward(order, survey_ref, half_ref, dense_ref, own_ref, away_ref):
    core = order.core()
    half = own_ref.shape[0]
    for i in range(2 * half):
        travel = lax.dot_general(
            half_ref[order.survey(core, survey_ref, i)],
            dense_ref[i],
            (((1,), (1,)), ((), ())),
            preferred_element_type=jnp.float32,
        )
        if i < half:
            own_ref[i] = travel
        else:
            away_ref[i - half] = travel


def setup_kernel(
    order, count_ref, ray_hbm, cell_hbm, survey_hbm, members_hbm, blocks_hbm,
    dense_ref, half_ref, own_ref, away_ref,
    ray_ref, cell_ref, survey_ref, members_ref, staged, upper, lower, small_sems, sems,
):
    slots, rays, width = blocks_hbm.shape
    chunks = slots // CHUNK
    core = order.core()
    small = [
        pltpu.make_async_copy(source, target, small_sems.at[i])
        for i, (source, target) in enumerate(
            (
                (ray_hbm, ray_ref),
                (cell_hbm, cell_ref),
                (survey_hbm, survey_ref),
                (members_hbm, members_ref),
            )
        )
    ]
    large = []
    for i in range(chunks):
        part = pl.ds(i * CHUNK, CHUNK)
        large.append(pltpu.make_async_copy(blocks_hbm.at[part], staged.at[part], sems.at[i]))
    for copy in small[:-1] + large + small[-1:]:
        copy.start()
    upper[...] = jnp.zeros_like(upper)
    lower[...] = jnp.zeros_like(lower)
    middle = rays // 2
    for copy in small[:-1]:
        copy.wait()
    count = count_ref[0]
    spare = dense_ref.shape[0]
    for i in range(chunks):
        large[i].wait()
        for k in range(i * CHUNK, (i + 1) * CHUNK):
            place = jnp.where(k < count, order.place(core, ray_ref[k]), spare)
            b = cell_ref[k]
            upper[b, place] = upper[b, place] + staged[k, :middle].astype(jnp.float32)
            lower[b, place] = lower[b, place] + staged[k, middle:].astype(jnp.float32)
    for b in range(upper.shape[0]):
        cells = slice(b * width, (b + 1) * width)
        dense_ref[:, :middle, cells] = upper[b, :spare].astype(dense_ref.dtype)
        dense_ref[:, middle:, cells] = lower[b, :spare].astype(dense_ref.dtype)
    small[-1].wait()
    half_ref[...] = members_ref[...].astype(half_ref.dtype)
    forward(order, survey_ref, half_ref, dense_ref, own_ref, away_ref)


def misfit_kernel(travel_ref, observed_ref, noise_ref, token_ref, out_ref):
    del token_ref
    travel = travel_ref[...]
    spread = noise_ref[...][:, None, :]
    scaled = (travel - observed_ref[...]) / spread
    residual = DATA_GAIN * scaled / (spread * (1.0 + scaled * scaled))
    out_ref[...] = jnp.broadcast_to(residual.astype(out_ref.dtype)[None], out_ref.shape)


def arrival_kernel(observed_ref, halo_ref, token_ref):
    del observed_ref, halo_ref
    token_ref[...] = jnp.zeros_like(token_ref)


def add_products(order, survey_ref, low, products, upper, lower):
    core = order.core()
    middle = upper.shape[1]
    for i, product in enumerate(products):
        s = order.survey(core, survey_ref, low + i)
        upper[s] = upper[s] + product[:middle]
        lower[s] = lower[s] + product[middle:]


def gradient_kernel(
    order, survey_ref, residual_ref, dense_ref, members_ref, prior_ref, chip_ref, link_ref,
    upper, lower,
):
    products = [
        jnp.dot(residual_ref[i], dense_ref[i], preferred_element_type=jnp.float32)
        for i in range(residual_ref.shape[0])
    ]
    surveys = members_ref.shape[0]
    middle = upper.shape[1]
    for s in range(surveys):
        m = members_ref[s]
        value = ALPHA_PRIOR * (m - prior_ref[s])
        if s > 0:
            value = value + BETA_TIME * (m - members_ref[s - 1])
        if s < surveys - 1:
            value = value + BETA_TIME * (m - members_ref[s + 1])
        neighbours = chip_ref[s].astype(jnp.float32) + link_ref[s].astype(jnp.float32)
        value = value + GAMMA_DEPTH * (2.0 * m - neighbours)
        upper[s] = value[:middle]
        lower[s] = value[middle:]
    add_products(order, survey_ref, 0, products, upper, lower)


def finish_gradient(
    order, survey_ref, residual_ref, dense_ref, upper_ref, lower_ref, upper, lower
):
    half = residual_ref.shape[0]
    products = [
        jnp.dot(residual_ref[i], dense_ref[half + i], preferred_element_type=jnp.float32)
        for i in range(half)
    ]
    upper[...] = upper_ref[...]
    lower[...] = lower_ref[...]
    add_products(order, survey_ref, half, products, upper, lower)


def step_kernel(
    order, survey_ref, residual_ref, dense_ref, upper_ref, lower_ref, members_ref,
    out_ref, half_ref, own_ref, away_ref,
    upper, lower,
):
    finish_gradient(order, survey_ref, residual_ref, dense_ref, upper_ref, lower_ref, upper, lower)
    middle = upper.shape[1]
    for rows, grad in ((slice(0, middle), upper), (slice(middle, None), lower)):
        updated = members_ref[:, rows] - STEP_SIZE * grad[...]
        out_ref[:, rows] = updated
        half_ref[:, rows] = updated.astype(half_ref.dtype)
    forward(order, survey_ref, half_ref, dense_ref, own_ref, away_ref)


def last_kernel(
    order, survey_ref, residual_ref, dense_ref, upper_ref, lower_ref, members_ref,
    out_ref, gradient_ref,
    upper, lower,
):
    finish_gradient(order, survey_ref, residual_ref, dense_ref, upper_ref, lower_ref, upper, lower)
    middle = upper.shape[1]
    for rows, grad in ((slice(0, middle), upper), (slice(middle, None), lower)):
        out_ref[:, rows] = members_ref[:, rows] - STEP_SIZE * grad[...]
        gradient_ref[:, rows] = grad[...].astype(gradient_ref.dtype)


def shards(
    prior_members, blocks, block_ray, block_cell, block_count, ray_survey, observed, noise_scale
):
    surveys, ensemble, cells_dev = prior_members.shape
    slots, rays, width = blocks.shape
    ray_blocks = ray_survey.shape[0]
    count = lax.axis_size("cell")
    order = Order(count, ray_blocks)
    owned, half_blocks = order.owned, order.half_blocks
    chips = count // 2
    params = pltpu.CompilerParams(vmem_limit_bytes=VMEM_BYTES)

    def bf16(*shape):
        return jax.ShapeDtypeStruct(shape, jnp.bfloat16)

    def f32(*shape):
        return jax.ShapeDtypeStruct(shape, jnp.float32)

    members_f32 = f32(surveys, ensemble, cells_dev)
    part_f32 = f32(surveys, ensemble // 2, cells_dev)
    members_bf16 = bf16(surveys, ensemble, cells_dev)
    travels = (f32(half_blocks, ensemble, rays),) * 2

    in_hbm = [
        pltpu.with_memory_space_constraint(array, pltpu.HBM)
        for array in (block_ray, block_cell, ray_survey, prior_members, blocks)
    ]
    dense, half, own, away = pl.pallas_call(
        functools.partial(setup_kernel, order),
        out_shape=(bf16(ray_blocks, rays, cells_dev), members_bf16) + travels,
        in_specs=[SMEM] + [HBM] * 5,
        out_specs=(VMEM,) * 4,
        scratch_shapes=[
            pltpu.SMEM(block_ray.shape, jnp.int32),
            pltpu.SMEM(block_cell.shape, jnp.int32),
            pltpu.SMEM(ray_survey.shape, jnp.int32),
            pltpu.VMEM(prior_members.shape, jnp.float32),
            pltpu.VMEM(blocks.shape, blocks.dtype),
            pltpu.VMEM((cells_dev // width, ray_blocks + 1, rays // 2, width), jnp.float32),
            pltpu.VMEM((cells_dev // width, ray_blocks + 1, rays // 2, width), jnp.float32),
            pltpu.SemaphoreType.DMA((4,)),
            pltpu.SemaphoreType.DMA((slots // CHUNK,)),
        ],
        compiler_params=pltpu.CompilerParams(vmem_limit_bytes=VMEM_BYTES),
    )(block_count, *in_hbm)

    chip_pairs = [(i, i ^ 1) for i in range(count)]
    link_pairs = [pair for i in range(1, count - 1, 2) for pair in ((i, i + 1), (i + 1, i))]
    same_core = [list(range(core, count, 2)) for core in range(2)]

    def exchange(array):
        return lax.all_to_all(
            array, "cell", split_axis=0, concat_axis=0, axis_index_groups=same_core, tiled=True
        )

    members = prior_members
    for iteration in range(ITERS):
        received = lax.ppermute(away, "cell", chip_pairs)
        chip_halo = lax.ppermute(half, "cell", chip_pairs)
        received, chip_halo = lax.optimization_barrier((received, chip_halo))
        chip_travel = ((own + received) * SENT_SCALE).astype(jnp.float16)
        link_halo = lax.ppermute(half, "cell", link_pairs)
        parts = exchange(chip_travel)
        parts, after_parts = lax.optimization_barrier((parts, observed))
        token = pl.pallas_call(
            arrival_kernel,
            out_shape=f32(8, 128),
            in_specs=[ANY] * 2,
            out_specs=VMEM,
            compiler_params=params,
        )(after_parts, link_halo)
        parts, token = lax.optimization_barrier((parts, token))
        parts = parts.reshape(chips, owned, ensemble, rays).astype(jnp.float32)
        travel = jnp.sum(parts, axis=0) / SENT_SCALE
        copies = pl.pallas_call(
            misfit_kernel,
            out_shape=bf16(chips, owned, ensemble, rays),
            in_specs=[VMEM] * 3 + [ANY],
            out_specs=VMEM,
            compiler_params=params,
        )(travel, observed, noise_scale, token)
        residual = exchange(copies.reshape(half_blocks, ensemble, rays))
        other_residual = lax.ppermute(residual, "cell", chip_pairs)
        partial = pl.pallas_call(
            functools.partial(gradient_kernel, order),
            out_shape=(part_f32, part_f32),
            in_specs=[SMEM] + [VMEM] * 6,
            out_specs=(VMEM, VMEM),
            compiler_params=params,
        )(ray_survey, residual, dense, members, prior_members, chip_halo, link_halo)
        last = iteration == ITERS - 1
        outputs = (members_f32, members_bf16) + (() if last else travels)
        results = pl.pallas_call(
            functools.partial(last_kernel if last else step_kernel, order),
            out_shape=outputs,
            in_specs=[SMEM] + [VMEM] * 5,
            out_specs=(VMEM,) * len(outputs),
            scratch_shapes=[pltpu.VMEM(part_f32.shape, jnp.float32)] * 2,
            compiler_params=params,
        )(ray_survey, other_residual, dense, *partial, members)
        if last:
            return results
        members, half, own, away = results


def solution(mesh):
    placed = (
        P(None, "ens", "cell"),
        P("cell", None, None),
        P("cell"),
        P("cell"),
        P("cell"),
        P(),
        P("cell", "ens", None),
        P("cell", None),
    )
    return jax.shard_map(
        shards,
        mesh=mesh,
        in_specs=placed,
        out_specs=(P(None, "ens", "cell"), P(None, "ens", "cell")),
        check_vma=False,
    )
```
